32 devices in a mesh: groups: 2 (over x), lon: 16 (over z, y, core).
Axes of the slice: x: 2, y: 2, z: 4, core: 2. Of those that a mesh axis runs over, the one named last changes fastest.
Arguments:
- latlon_fields: bfloat16 [32, 32, 2048], P('groups', 'lon'), parts along dimension 0, may hold values from -6 to 6
- remap_table: int32 [2, 32, 2048], P(None, None, 'lon'), may hold values from 0 to 2047, as said below
- kernel_first: bfloat16 [3, 3, 64, 16], replicated, may hold values from -0.5 to 0.5
- kernel_second: bfloat16 [3, 3, 64, 64], replicated, may hold values from -0.25 to 0.25
- kernel_down: bfloat16 [3, 3, 128, 64], replicated, may hold values from -0.25 to 0.25
- kernel_coarse: bfloat16 [3, 3, 128, 128], replicated, may hold values from -0.1875 to 0.1875
- kernel_up: bfloat16 [3, 3, 64, 128], replicated, may hold values from -0.375 to 0.375
- kernel_merge: bfloat16 [3, 3, 64, 128], replicated, may hold values from -0.1875 to 0.1875
- projection: bfloat16 [8, 64], replicated, may hold values from -0.75 to 0.75
Outputs:
- forecast: float32 [16, 32, 2048], P('groups', None, 'lon'), parts along dimension 0
The draws below stay inside these ranges and needn't reach their ends.
There are 2 independent parts, one for each index of `groups`. The reference program is written for one: setup_inputs(seed, part) draws one part's arguments, and reference() takes and returns one part's arrays. A program takes and returns all parts, laid end to end along the dimension named above; an argument that names none is the same for every part. Nothing has to cross between parts.
Inputs may be any that keep to these rules, and one draw needn't show every extreme that they name: remap_table[0] is a lat-lon row below 32; remap_table[1] is a lat-lon column, and for a grid cell in column w it lies in the same block of 128 columns as w, that is between (w // 128) * 128 and (w // 128) * 128 + 127.
All inputs are finite; a program needn't handle non-finite values.
Results may differ from the reference program's by a relative error of at most 0.00084.
Values may be sent and summed in bfloat16 or wider, within the bound.
No kernel may reach another device: no remote copies, remote signals or barrier semaphores. Data moves between devices by JAX's collectives and lax.ppermute only.
A program may use at most 128 MiB of HBM per device.

```python
import jax
import jax.numpy as jnp
from jax import lax

C = 64
C2 = 128
CIN = 16
COUT = 8
H = 32
WD = 128
W = 2048
NLAT = 32


def draw_remap_table(key, part):
    key_rows, key_cols = jax.random.split(jax.random.fold_in(key, 7))
    row_index = jnp.broadcast_to(jnp.arange(H, dtype=jnp.int32)[:, None], (H, W))
    col_index = jnp.broadcast_to(jnp.arange(W, dtype=jnp.int32)[None, :], (H, W))
    jitter_rows = jax.random.randint(key_rows, (H, W), -2, 3, dtype=jnp.int32)
    latitude = jnp.clip(row_index * NLAT // H + jitter_rows, 0, NLAT - 1)
    owners = col_index // WD
    offset = col_index % WD
    jitter_cols = jax.random.randint(key_cols, (H, W), -1, 2, dtype=jnp.int32)
    longitude = owners * WD + jnp.clip(offset + jitter_cols, 0, WD - 1)
    latitude = latitude.at[0, 0].set(0)
    longitude = longitude.at[0, 0].set(0)
    longitude = longitude.at[H - 1, W - 1].set(W - 1)
    return jnp.stack([latitude, longitude]).astype(jnp.int32)


def steps_of(own_key, dims, cuts, least, largest):
    def one(axis_at, blocks):
        steps = jax.random.uniform(jax.random.fold_in(jax.random.fold_in(own_key, 6), axis_at), (blocks,), jnp.float32, least / len(cuts), largest / len(cuts))
        return jnp.repeat(jnp.exp(steps), dims[axis_at] // blocks).reshape((-1,) + (1,) * (len(dims) - axis_at - 1))

    level = one(*cuts[0])
    for cut in cuts[1:]:
        level = level * one(*cut)
    return level


def noise(stream_key, dims, width, most, shards=(), kind=jnp.bfloat16):
    entries = jax.random.normal(stream_key, dims, jnp.float32) * width
    if len(shards) > 0:
        entries = steps_of(stream_key, dims, shards, -0.22, 0.18) * entries
    return jnp.clip(entries, min=-most, max=most).astype(kind)


def setup_inputs(seed: int = 0, part: int = 0) -> dict:
    splits = jax.random.split(jax.random.key(seed), 10)
    part_keys = jax.random.split(jax.random.fold_in(splits[9], part), 10)
    return {
        "latlon_fields": noise(part_keys[0], (CIN, NLAT, W), 1.0, 6.0, ((1, 16),)),
        "remap_table": draw_remap_table(jax.random.fold_in(splits[9], 71), part),
        "kernel_first": noise(splits[2], (3, 3, C, CIN), (9 * CIN) ** -0.5, 0.5),
        "kernel_second": noise(splits[3], (3, 3, C, C), (9 * C) ** -0.5, 0.25),
        "kernel_down": noise(splits[4], (3, 3, C2, C), (9 * C) ** -0.5, 0.25),
        "kernel_coarse": noise(splits[5], (3, 3, C2, C2), (9 * C2) ** -0.5, 0.1875),
        "kernel_up": noise(splits[6], (3, 3, C, C2), (9 * C2 // 4) ** -0.5, 0.375),
        "kernel_merge": noise(splits[7], (3, 3, C, 2 * C), (18 * C) ** -0.5, 0.1875),
        "projection": noise(splits[8], (COUT, C), C ** -0.5, 0.75),
    }


def extend_full(field_in):
    half = field_in.shape[2] // 2
    top_row = jnp.roll(field_in[:, :1], half, axis=2)
    bottom_row = jnp.zeros_like(field_in[:, :1])
    tall = jnp.concatenate([top_row, field_in, bottom_row], axis=1)
    return jnp.concatenate([tall[:, :, -1:], tall, tall[:, :, :1]], axis=2)


def convolve(extended, kernel, stride):
    channels = extended.shape[0]
    out_rows = (extended.shape[1] - 2) // stride
    out_cols = (extended.shape[2] - 2) // stride
    source = extended.astype(jnp.float32)
    weights = kernel.astype(jnp.float32)
    total = jnp.zeros((kernel.shape[2], out_rows, out_cols), jnp.float32)
    for row_tap in range(3):
        for col_tap in range(3):
            piece = lax.slice(source, (0, row_tap, col_tap),
                              (channels, row_tap + (out_rows - 1) * stride + 1, col_tap + (out_cols - 1) * stride + 1),
                              (1, stride, stride))
            total = total + jnp.einsum("oc,chw->ohw", weights[row_tap, col_tap], piece,
                                       precision=lax.Precision.HIGHEST)
    return total


def activate(values):
    return jax.nn.silu(values).astype(jnp.bfloat16)


def reference(latlon_fields, remap_table, kernel_first, kernel_second, kernel_down, kernel_coarse, kernel_up, kernel_merge, projection):
    remapped = latlon_fields[:, remap_table[0], remap_table[1]]
    first = activate(convolve(extend_full(remapped), kernel_first, 1))
    second = activate(convolve(extend_full(first), kernel_second, 1))
    coarse_in = activate(convolve(extend_full(second), kernel_down, 2))
    coarse_out = activate(convolve(extend_full(coarse_in), kernel_coarse, 1))
    grid_rows = second.shape[1]
    grid_cols = second.shape[2]
    stuffed = jnp.zeros((coarse_out.shape[0], grid_rows, grid_cols), jnp.float32)
    stuffed = stuffed.at[:, ::2, ::2].set(coarse_out.astype(jnp.float32))
    padded = jnp.pad(stuffed, ((0, 0), (1, 1), (0, 0)))
    padded = jnp.concatenate([padded[:, :, -1:], padded, padded[:, :, :1]], axis=2)
    lifted = convolve(padded, kernel_up, 1)
    upsampled = activate(lifted)
    joined = jnp.concatenate([second, upsampled], axis=0)
    merged = activate(convolve(extend_full(joined), kernel_merge, 1))
    count_out = projection.shape[0]
    update = jnp.einsum("oc,chw->ohw", projection.astype(jnp.float32), merged.astype(jnp.float32),
                        precision=lax.Precision.HIGHEST)
    return remapped[:count_out].astype(jnp.float32) + update
```

```python
import functools

import jax
import jax.numpy as jnp
from jax import lax
from jax.experimental import pallas as pl
from jax.experimental.pallas import tpu as pltpu
from jax.sharding import PartitionSpec as P

F32 = jnp.float32
BF16 = jnp.bfloat16
HALO = 8
FINE_COLUMN = (1, 2, 3, 0)


def from_behind(block, axis, distance):
    devices = range(lax.axis_size(axis))
    route = [((i - distance) % len(devices), i) for i in devices]
    return lax.ppermute(block, axis, route)


def tap(kernel_ref, row, col):
    if 0 <= row < 3 and 0 <= col < 3:
        return kernel_ref[row, col].astype(F32)
    return jnp.zeros(kernel_ref.shape[2:], F32)


def arrange_kernel(first, second, down, coarse, up, merge, projection, w1, w2, wd, wc, wu, wm, wp):
    channels = second.shape[3]
    inputs = first.shape[2]
    for half in range(2):
        for side in range(2):
            for p in range(2):
                for q in range(2):
                    t = 1 + p if half == 0 else (3, 0)[p]
                    u = 1 + q if side == 0 else (3, 0)[q]
                    at = (((half * 2 + side) * 2 + p) * 2 + q) * inputs
                    pieces = [tap(first, t - a, u - b) for a in range(2) for b in range(2)]
                    w1[at : at + inputs, :] = jnp.concatenate(pieces, axis=1).astype(BF16)
    for t in range(4):
        for code, u in enumerate(FINE_COLUMN):
            at = t * 4 * channels + code * channels
            for p in range(2):
                pair = jnp.concatenate([tap(second, t - p, u), tap(second, t - p, u - 1)], axis=0)
                w2[at : at + channels, p * 128 : (p + 1) * 128] = pair.T.astype(BF16)
            for q in range(2):
                pair = jnp.concatenate([tap(merge, t, u - q), tap(merge, t - 1, u - q)], axis=0).T.astype(BF16)
                wm[at : at + channels, q * 128 : (q + 1) * 128] = pair[:channels]
                wm[16 * channels + at : 16 * channels + at + channels, q * 128 : (q + 1) * 128] = pair[channels:]
            if t < 3:
                wd[at : at + channels, :] = tap(down, t, u).T.astype(BF16)
    wide = coarse.shape[3]
    for a in range(3):
        for b in range(3):
            at = (a * 3 + b) * wide
            wc[at : at + wide, :] = tap(coarse, a, b).T.astype(BF16)
    lifts = ((1, 3), (0, 2))
    for di in range(2):
        for dj in range(2):
            at = (di * 2 + dj) * wide
            for p in range(2):
                pair = jnp.concatenate([tap(up, lifts[p][di], lifts[q][dj]) for q in range(2)], axis=0)
                wu[at : at + wide, p * 128 : (p + 1) * 128] = pair.T.astype(BF16)
    rows = projection[...].astype(F32)
    nothing = jnp.zeros_like(rows)
    upper = jnp.concatenate([rows, nothing], axis=1)
    lower = jnp.concatenate([nothing, rows], axis=1)
    wp[...] = jnp.concatenate([upper, lower], axis=0).astype(BF16)


def arrange(first, second, down, coarse, up, merge, projection):
    channels, wide = second.shape[3], coarse.shape[3]
    shapes = (
        (16 * first.shape[3], 4 * channels),
        (16 * channels, 4 * channels),
        (12 * channels, wide),
        (9 * wide, wide),
        (4 * wide, 4 * channels),
        (32 * channels, 4 * channels),
        (2 * projection.shape[0], 2 * channels),
    )
    return pl.pallas_call(
        arrange_kernel,
        out_shape=[jax.ShapeDtypeStruct(s, BF16) for s in shapes],
        compiler_params=pltpu.CompilerParams(vmem_limit_bytes=32 * 2**20),
        name="arrange_weights",
    )(jnp.swapaxes(first, 2, 3), second, down, coarse, up, merge, projection)


def remap_kernel(block, table, cells, to_left, to_right, skip, source, picked):
    devices, depth, columns = block.shape
    channels = depth // 2
    grid_rows = table.shape[1]
    half = columns // 2
    lane = lax.broadcasted_iota(jnp.int32, (8, columns), 1)
    spread = (lane % half) * 2 + lane // half

    def load(s, carry):
        source[pl.ds(pl.multiple_of(s * depth, depth), depth), :] = block[s].astype(F32)
        return carry

    lax.fori_loop(0, devices, load, 0)

    def one_row(h, carry):
        rows = jnp.broadcast_to(table[0, pl.ds(h, 1), :], (8, columns))
        cols = jnp.broadcast_to(table[1, pl.ds(h, 1), :], (8, columns))
        rows = jnp.take_along_axis(rows, spread, axis=1)
        cols = jnp.take_along_axis(cols, spread, axis=1) % columns
        parts = [jnp.zeros((8, columns), F32) for _ in range(channels // 8)]
        for r in range(2 * devices):
            here = rows == r
            for n in range(channels // 8):
                at = r * channels + n * 8
                value = jnp.take_along_axis(source[at : at + 8, :], cols, axis=1)
                parts[n] = jnp.where(here, value, parts[n])
        for n in range(channels // 8):
            picked[pl.ds(pl.multiple_of(h * channels + n * 8, 8), 8), :] = parts[n]
        skip[pl.ds(pl.multiple_of(h * 8, 8), 8), :] = parts[0]
        return carry

    lax.fori_loop(0, grid_rows, one_row, 0)
    for i in range(grid_rows // 2):
        turned = picked[i * 2 * channels : (i + 1) * 2 * channels, :].T
        pieces = []
        for p in range(2):
            for q in range(2):
                pieces.append(turned[q * half : (q + 1) * half, p * channels : (p + 1) * channels])
        paired = jnp.concatenate(pieces + pieces, axis=1)
        cells[i * half : (i + 1) * half, :] = paired.astype(BF16)
        to_left[i * HALO : (i + 1) * HALO, :] = paired[:HALO]
        to_right[i * HALO : (i + 1) * HALO, :] = paired[half - HALO :]


def remap(block, table):
    devices, depth, columns = block.shape
    grid_rows = table.shape[1]
    channels = depth // 2
    half = columns // 2
    lanes = 8 * channels
    return pl.pallas_call(
        remap_kernel,
        out_shape=[
            jax.ShapeDtypeStruct((grid_rows // 2 * half, lanes), BF16),
            jax.ShapeDtypeStruct((grid_rows // 2 * HALO, lanes), F32),
            jax.ShapeDtypeStruct((grid_rows // 2 * HALO, lanes), F32),
            jax.ShapeDtypeStruct((grid_rows * 8, columns), F32),
        ],
        scratch_shapes=[
            pltpu.VMEM((devices * depth, columns), F32),
            pltpu.VMEM((grid_rows * channels, columns), F32),
        ],
        compiler_params=pltpu.CompilerParams(vmem_limit_bytes=16 * 2**20),
        name="remap",
    )(block, table)


def silu(values):
    h = 0.5 * values
    return (h + h * jnp.tanh(h)).astype(BF16).astype(F32)


def neighbours(values):
    count = values.shape[0]
    return pltpu.roll(values, 1, 0), pltpu.roll(values, count - 1, 0)


def network_kernel(cells, left, right, across, skip, w1, w2, wd, wc, wu, wm, wp, out, x0, y0, y1, y2, yc, yo, yu):
    half = cells.shape[0] // (left.shape[0] // HALO)
    blocks = left.shape[0] // HALO
    step = half + 2 * HALO
    polar = across.shape[0] // step
    top = 0
    bottom = blocks + 1
    pole = blocks + 2
    end = pole + polar + 1
    group = 4

    def at(row, count=1):
        return slice(row * step, (row + count) * step)

    def chunks(polar_rows):
        found = [(1 + i, group) for i in range(0, blocks, group)]
        if polar_rows:
            found.append((pole + 1, polar_rows))
        return found

    def lane_mask(rows, width):
        return lax.broadcasted_iota(jnp.int32, (rows, 128), 1) // width % 2 == 0

    x0[...] = jnp.zeros_like(x0)
    for i in range(blocks):
        base = (1 + i) * step
        x0[base : base + HALO, :] = left[i * HALO : (i + 1) * HALO, :]
        x0[base + HALO : base + HALO + half, :] = cells[i * half : (i + 1) * half, :].astype(F32)
        x0[base + HALO + half : base + step, :] = right[i * HALO : (i + 1) * HALO, :]
    x0[at(pole + 1, polar), :] = across[...]
    x0[at(top), :] = pltpu.roll(x0[at(pole + 1), :], 32, 1)
    x0[at(pole), :] = pltpu.roll(x0[at(1), :], 32, 1)
    for row in range(0, end + 1):
        x = x0[at(row), :]
        before, after = neighbours(x)
        side = jnp.where(lane_mask(step, 16), after, before)
        y0[at(row), :] = jnp.where(lane_mask(step, 64), x, side)

    def store_fine(y, row, count, values):
        before, after = neighbours(values)
        mask = lane_mask(count * step, 64)
        for p in range(2):
            lanes = slice(p * 128, (p + 1) * 128)
            y[at(row, count), p * 256 : p * 256 + 128] = values[:, lanes].astype(BF16)
            y[at(row, count), p * 256 + 128 : p * 256 + 256] = jnp.where(
                mask, after[:, lanes], before[:, lanes]
            ).astype(BF16)

    def edges_fine(y, polar_rows):
        y[at(top), 256:512] = y[at(pole + 1), 0:256]
        y[at(pole), 256:512] = y[at(1), 0:256]
        y[at(bottom), 0:256] = jnp.zeros((step, 256), BF16)
        y[at(pole + 1 + polar_rows), 0:256] = jnp.zeros((step, 256), BF16)

    def patch(y, row, count):
        return [
            y[at(row - 1, count), 256:512],
            y[at(row, count), :],
            y[at(row + 1, count), 0:256],
        ]

    def product(pieces, weights):
        return jnp.dot(jnp.concatenate(pieces, axis=1), weights[...], preferred_element_type=F32)

    for row, count in chunks(polar):
        mask = lane_mask(count * step, 32)
        vertical = jnp.where(mask, y0[at(row + 1, count), :], y0[at(row - 1, count), :])
        pieces = [y0[at(row, count), :].astype(BF16), vertical.astype(BF16)]
        store_fine(y1, row, count, silu(product(pieces, w1)))
    edges_fine(y1, polar)

    for row, count in chunks(polar - 1):
        store_fine(y2, row, count, silu(product(patch(y1, row, count), w2)))
    edges_fine(y2, polar - 1)

    for row, count in chunks(polar - 1):
        pieces = [y2[at(row - 1, count), 256:512], y2[at(row, count), :]]
        values = silu(product(pieces, wd))
        before, after = neighbours(values)
        yc[at(row, count), 0:128] = before.astype(BF16)
        yc[at(row, count), 128:256] = values.astype(BF16)
        yc[at(row, count), 256:384] = after.astype(BF16)
    yc[at(top), :] = yc[at(pole + 1), :]
    yc[at(pole), :] = yc[at(1), :]
    yc[at(bottom), :] = jnp.zeros((step, 384), BF16)

    for row, count in chunks(polar - 2):
        pieces = [yc[at(row + a, count), :] for a in (-1, 0, 1)]
        values = silu(product(pieces, wc))
        yo[at(row, count), 0:128] = values.astype(BF16)
        yo[at(row, count), 128:256] = neighbours(values)[1].astype(BF16)
    yo[at(bottom), :] = jnp.zeros((step, 256), BF16)
    yo[at(pole + 2), :] = jnp.zeros((step, 256), BF16)

    for row, count in chunks(polar - 2):
        pieces = [yo[at(row, count), :], yo[at(row + 1, count), :]]
        store_fine(yu, row, count, silu(product(pieces, wu)))
    edges_fine(yu, polar - 2)

    lane = lax.broadcasted_iota(jnp.int32, (2 * 8, 2 * half), 1)
    weave = (lane % 2) * half + lane // 2
    for row, count in chunks(0):
        merged = silu(product(patch(y2, row, count) + patch(yu, row, count), wm))
        columns = []
        for i in range(count):
            own = merged[i * step + HALO : i * step + HALO + half, :]
            columns += [own[:, 0:128], own[:, 128:256]]
        columns = jnp.concatenate(columns, axis=0).astype(BF16)
        update = lax.dot_general(wp[...], columns, (((1,), (1,)), ((), ())), preferred_element_type=F32)
        for i in range(count):
            r = row - 1 + i
            total = update[:, i * 2 * half : (i + 1) * 2 * half] + skip[r * 16 : (r + 1) * 16, :]
            total = jnp.take_along_axis(total, weave, axis=1)
            for p in range(2):
                out[:, 2 * r + p, :] = total[p * 8 : (p + 1) * 8, :]


def network(cells, left, right, across, skip, weights):
    blocks = left.shape[0] // HALO
    half = cells.shape[0] // blocks
    step = half + 2 * HALO
    rows = (blocks + 2 + across.shape[0] // step + 2) * step
    vmem = pltpu.VMEM
    return pl.pallas_call(
        network_kernel,
        out_shape=jax.ShapeDtypeStruct((weights[-1].shape[0] // 2, 2 * blocks, 2 * half), F32),
        scratch_shapes=[
            vmem((rows, 128), F32),
            vmem((rows, 128), F32),
            vmem((rows, 512), BF16),
            vmem((rows, 512), BF16),
            vmem((rows, 384), BF16),
            vmem((rows, 256), BF16),
            vmem((rows, 512), BF16),
        ],
        compiler_params=pltpu.CompilerParams(vmem_limit_bytes=40 * 2**20),
        name="network",
    )(cells, left, right, across, skip, *weights)


def shards(
    latlon_fields,
    remap_table,
    kernel_first,
    kernel_second,
    kernel_down,
    kernel_coarse,
    kernel_up,
    kernel_merge,
    projection,
):
    columns = remap_table.shape[2]
    count = lax.axis_size("lon")
    channels, rows, _ = latlon_fields.shape
    parcels = latlon_fields.reshape(channels, rows, count, columns).transpose(2, 1, 0, 3)
    parcels = parcels.reshape(count, rows * channels, columns)
    block = lax.all_to_all(parcels, "lon", split_axis=0, concat_axis=0, tiled=True)
    weights = arrange(
        kernel_first, kernel_second, kernel_down, kernel_coarse, kernel_up, kernel_merge, projection
    )
    cells, to_left, to_right, skip = remap(block, remap_table)
    left = from_behind(to_right, "lon", 1)
    right = from_behind(to_left, "lon", -1)
    polar = 3
    half = columns // 2
    own = cells[: polar * half].reshape(polar, half, -1).astype(F32)
    edge = jnp.concatenate(
        [left[: polar * HALO].reshape(polar, HALO, -1), own, right[: polar * HALO].reshape(polar, HALO, -1)], axis=1
    )
    across = from_behind(edge.reshape(-1, edge.shape[2]), "lon", count // 2)
    return network(cells, left, right, across, skip, weights)


def solution(mesh):
    return jax.shard_map(
        shards,
        mesh=mesh,
        in_specs=(
            P("groups", "lon", None),
            P(None, None, "lon"),
            P(),
            P(),
            P(),
            P(),
            P(),
            P(),
            P(),
        ),
        out_specs=P("groups", None, "lon"),
        check_vma=False,
    )
```

```python
import jax
import jax.numpy as jnp
from jax import lax
from jax.experimental import pallas as pl
from jax.experimental.pallas import tpu as pltpu
from jax.sharding import PartitionSpec as P

F32 = jnp.float32
BF16 = jnp.bfloat16
HALO = 4
GAP = 8
POLAR = 3
TOP = 2


def from_behind(block, axis, distance):
    devices = range(lax.axis_size(axis))
    route = [((i - distance) % len(devices), i) for i in devices]
    return lax.ppermute(block, axis, route)


def tap(kernel_ref, row, col):
    if 0 <= row < 3 and 0 <= col < 3:
        return kernel_ref[row, col].astype(F32)
    return jnp.zeros(kernel_ref.shape[2:], F32)


def arrange_kernel(first, second, down, coarse, up, merge, projection, w1, w2, wd, wc, wu, wm, wp):
    channels = second.shape[3]
    inputs = first.shape[2]
    for half in range(2):
        for side in range(2):
            for p in range(2):
                for q in range(2):
                    t = 1 + p if half == 0 else (3, 0)[p]
                    u = 1 + q if side == 0 else (3, 0)[q]
                    at = (((half * 2 + side) * 2 + p) * 2 + q) * inputs
                    pieces = [tap(first, t - a, u - b) for a in range(2) for b in range(2)]
                    w1[at : at + inputs, :] = jnp.concatenate(pieces, axis=1).astype(BF16)
    for t in range(4):
        for code in range(4):
            at = (t * 4 + code) * channels
            source = (0, 1, -2, -1)[code]
            for p in range(2):
                pair = [tap(second, t - p, source - target + 1) for target in (-1, 0)]
                w2[at : at + channels, p * 128 : (p + 1) * 128] = jnp.concatenate(pair, axis=0).T.astype(BF16)
            source = code - 1
            for p in range(2):
                pair = [tap(merge, t - p, source - target + 1) for target in (0, 1)]
                pair = jnp.concatenate(pair, axis=0).T.astype(BF16)
                wm[at : at + channels, p * 128 : (p + 1) * 128] = pair[:channels]
                wm[16 * channels + at : 16 * channels + at + channels, p * 128 : (p + 1) * 128] = pair[channels:]
            if t < 3:
                wd[at : at + channels, :] = tap(down, t, code).astype(BF16)
    wide = coarse.shape[3]
    for a in range(3):
        for b in range(3):
            at = (a * 3 + b) * wide
            wc[at : at + wide, :] = tap(coarse, a, b).T.astype(BF16)
    row_taps = ((1, 3), (0, 2))
    col_taps = ((0, 2), (3, 1))
    for di in range(2):
        for dj in range(2):
            at = (di * 2 + dj) * wide
            for p in range(2):
                pair = jnp.concatenate([tap(up, row_taps[p][di], col_taps[q][dj]) for q in range(2)], axis=0)
                wu[at : at + wide, p * 128 : (p + 1) * 128] = pair.T.astype(BF16)
    rows = projection[...].astype(F32)
    blank = jnp.zeros_like(rows)
    lines = [jnp.concatenate([rows if m == n else blank for m in range(4)], axis=1) for n in range(4)]
    wp[...] = jnp.concatenate(lines, axis=0).astype(BF16)


def arrange(first, second, down, coarse, up, merge, projection):
    channels, wide = second.shape[3], coarse.shape[3]
    shapes = (
        (16 * first.shape[3], 4 * channels),
        (16 * channels, 4 * channels),
        (12 * channels, wide),
        (9 * wide, wide),
        (4 * wide, 4 * channels),
        (32 * channels, 4 * channels),
        (4 * projection.shape[0], 4 * channels),
    )
    return pl.pallas_call(
        arrange_kernel,
        out_shape=[jax.ShapeDtypeStruct(s, BF16) for s in shapes],
        compiler_params=pltpu.CompilerParams(vmem_limit_bytes=16 * 2**20),
        name="arrange_weights",
    )(jnp.swapaxes(first, 2, 3), second, jnp.swapaxes(down, 2, 3), coarse, up, merge, projection)


def locate_kernel(table, onehot, source):
    _, grid_rows, columns = table.shape
    half = columns // 2
    code = table[0] * columns + lax.rem(table[1], columns)
    lane = lax.broadcasted_iota(jnp.int32, (grid_rows, columns), 1)
    odd = [jnp.take_along_axis(code, lax.rem(lane, half) * 2 + q, axis=1) for q in range(2)]
    left = lax.broadcasted_iota(jnp.int32, (1, columns), 1) < half
    place = lax.broadcasted_iota(jnp.int32, (2 * columns, columns), 0)
    for pair in range(grid_rows // 4):
        for p in range(2):
            for q in range(2):
                n = p * 2 + q
                above, below = 4 * pair + p, 4 * pair + 2 + p
                line = jnp.where(left, odd[q][above : above + 1, :], odd[q][below : below + 1, :])
                source[4 * pair + n : 4 * pair + n + 1, :] = lax.div(line, 2 * columns)
                here = place == lax.rem(line, 2 * columns)
                onehot[pair * 2 * columns : (pair + 1) * 2 * columns, n * columns : (n + 1) * columns] = jnp.where(
                    here, 1.0, 0.0
                ).astype(BF16)


def locate(table):
    _, grid_rows, columns = table.shape
    return pl.pallas_call(
        locate_kernel,
        out_shape=[
            jax.ShapeDtypeStruct((grid_rows // 4 * 2 * columns, 4 * columns), BF16),
            jax.ShapeDtypeStruct((grid_rows, columns), jnp.int32),
        ],
        compiler_params=pltpu.CompilerParams(vmem_limit_bytes=16 * 2**20),
        name="locate",
    )(table)


def remap(block, onehot, source, pairs):
    devices, depth, columns = block.shape
    channels = depth // 2
    half = columns // 2
    count = len(pairs)

    def kernel(block, onehot, source, cells, to_left, to_right, skip):
        upper = block[:, 0:channels, :].reshape(devices * channels, columns)
        lower = block[:, channels:depth, :].reshape(devices * channels, columns)
        fields = jnp.concatenate([upper, lower], axis=1)
        for at, pair in enumerate(pairs):
            chosen = onehot[pair * 2 * columns : (pair + 1) * 2 * columns, :]
            found = jnp.dot(fields, chosen, preferred_element_type=F32)
            lines = []
            for n in range(4):
                own = jnp.broadcast_to(source[4 * pair + n : 4 * pair + n + 1, :], (channels, columns))
                total = jnp.zeros((channels, columns), F32)
                for s in range(devices):
                    value = found[s * channels : (s + 1) * channels, n * columns : (n + 1) * columns]
                    total = jnp.where(own == s, value, total)
                lines.append(total)
                skip[(at * 4 + n) * 8 : (at * 4 + n + 1) * 8, :] = total[:8]
            turned = jnp.concatenate(lines + lines, axis=0).T
            cells[at * columns : (at + 1) * columns, :] = turned.astype(BF16)
            for i in range(2):
                row = (at * 2 + i) * HALO
                to_left[row : row + HALO, :] = turned[i * half : i * half + HALO]
                to_right[row : row + HALO, :] = turned[(i + 1) * half - HALO : (i + 1) * half]

    return pl.pallas_call(
        kernel,
        out_shape=[
            jax.ShapeDtypeStruct((count * columns, columns), BF16),
            jax.ShapeDtypeStruct((count * 2 * HALO, columns), F32),
            jax.ShapeDtypeStruct((count * 2 * HALO, columns), F32),
            jax.ShapeDtypeStruct((count * 32, columns), F32),
        ],
        compiler_params=pltpu.CompilerParams(vmem_limit_bytes=16 * 2**20),
        name="remap",
    )(block, onehot, source)


def silu(values):
    h = 0.5 * values
    return (h + h * jnp.tanh(h)).astype(BF16).astype(F32)


def ring(values, step, shift):
    rows = [pltpu.roll(values[at : at + step], shift % step, 0) for at in range(0, values.shape[0], step)]
    return rows[0] if len(rows) == 1 else jnp.concatenate(rows, axis=0)


def network_kernel(
    cells_top, cells_rest, left, right, across, skip_top, skip_rest,
    w1, w2, wd, wc, wu, wm, wp, out, x0, y0, y1, y2, yc, yo, yu,
):
    half = out.shape[2] // 2
    blocks = out.shape[1] // 2
    step = half + 2 * HALO + GAP
    polar = POLAR
    top = 0
    bottom = blocks + 1
    pole = blocks + 2
    end = pole + polar + 1
    group = 4

    def at(row, count=1):
        return slice(row * step, (row + count) * step)

    def chunks(polar_rows):
        return [(1 + i, group) for i in range(0, blocks, group)] + [(pole + 1, polar_rows)]

    def lane_mask(rows, width):
        return lax.rem(lax.div(lax.broadcasted_iota(jnp.int32, (rows, 128), 1), width), 2) == 0

    x0[...] = jnp.zeros_like(x0)
    rows_of_top = cells_top.shape[0] // half
    for i in range(blocks + polar):
        base = (1 + i if i < blocks else pole + 1 + i - blocks) * step
        if i >= blocks:
            own = across[(i - blocks) * half : (i - blocks + 1) * half, :]
        elif i < rows_of_top:
            own = cells_top[i * half : (i + 1) * half, :]
        else:
            own = cells_rest[(i - rows_of_top) * half : (i - rows_of_top + 1) * half, :]
        x0[base : base + half, :] = own.astype(F32)
        x0[base + half : base + half + HALO, :] = right[i * HALO : (i + 1) * HALO, :]
        x0[base + step - HALO : base + step, :] = left[i * HALO : (i + 1) * HALO, :]
    x0[at(top), :] = pltpu.roll(x0[at(pole + 1), :], 32, 1)
    x0[at(pole), :] = pltpu.roll(x0[at(1), :], 32, 1)
    for row in range(0, end + 1):
        x = x0[at(row), :]
        side = jnp.where(lane_mask(step, 16), ring(x, step, -1), ring(x, step, 1))
        y0[at(row), :] = jnp.where(lane_mask(step, 64), x, side)

    def store_fine(y, row, count, values, shift):
        moved = ring(values, step, shift).astype(BF16)
        values = values.astype(BF16)
        for p in range(2):
            lanes = slice(p * 128, (p + 1) * 128)
            y[at(row, count), p * 256 : p * 256 + 128] = values[:, lanes]
            y[at(row, count), p * 256 + 128 : p * 256 + 256] = moved[:, lanes]

    def edges_fine(y, polar_rows):
        y[at(top), 256:512] = y[at(pole + 1), 0:256]
        y[at(pole), 256:512] = y[at(1), 0:256]
        y[at(bottom), 0:256] = jnp.zeros((step, 256), BF16)
        y[at(pole + 1 + polar_rows), 0:256] = jnp.zeros((step, 256), BF16)

    def product(pieces, weights):
        return jnp.dot(jnp.concatenate(pieces, axis=1), weights[...], preferred_element_type=F32)

    for row, count in chunks(polar):
        mask = lane_mask(count * step, 32)
        vertical = jnp.where(mask, y0[at(row + 1, count), :], y0[at(row - 1, count), :])
        pieces = [y0[at(row, count), :].astype(BF16), vertical.astype(BF16)]
        store_fine(y1, row, count, silu(product(pieces, w1)), 1)
    edges_fine(y1, polar)

    for row, count in chunks(polar - 1):
        pieces = [y1[at(row - 1, count), 256:512], y1[at(row, count), :], y1[at(row + 1, count), 0:256]]
        store_fine(y2, row, count, silu(product(pieces, w2)), -1)
    edges_fine(y2, polar - 1)

    for row, count in chunks(polar - 1):
        pieces = [y2[at(row - 1, count), 256:512], y2[at(row, count), :]]
        values = silu(product(pieces, wd))
        yc[at(row, count), 0:128] = ring(values, step, 1).astype(BF16)
        yc[at(row, count), 128:256] = values.astype(BF16)
        yc[at(row, count), 256:384] = ring(values, step, -1).astype(BF16)
    yc[at(top), :] = yc[at(pole + 1), :]
    yc[at(pole), :] = yc[at(1), :]
    yc[at(bottom), :] = jnp.zeros((step, 384), BF16)

    for row, count in chunks(polar - 2):
        pieces = [yc[at(row + a, count), :] for a in (-1, 0, 1)]
        values = silu(product(pieces, wc))
        yo[at(row, count), 0:128] = ring(values, step, 1).astype(BF16)
        yo[at(row, count), 128:256] = values.astype(BF16)
    yo[at(bottom), :] = jnp.zeros((step, 256), BF16)
    yo[at(pole + 2), :] = jnp.zeros((step, 256), BF16)

    for row, count in chunks(polar - 2):
        pieces = [yo[at(row, count), :], yo[at(row + 1, count), :]]
        store_fine(yu, row, count, silu(product(pieces, wu)), -1)
    edges_fine(yu, polar - 2)

    lane = lax.broadcasted_iota(jnp.int32, (8, 2 * half), 1)
    even = lax.rem(lane, 2) == 0
    for row in range(1, 1 + blocks, group):

        def own(y, offset, lanes):
            rows = [y[(row + offset + i) * step : (row + offset + i) * step + half, lanes] for i in range(group)]
            return jnp.concatenate(rows, axis=0)

        pieces = []
        for y in (y2, yu):
            pieces += [own(y, -1, slice(256, 512)), own(y, 0, slice(0, 512)), own(y, 1, slice(0, 256))]
        merged = silu(product(pieces, wm)).astype(BF16)
        update = lax.dot_general(wp[...], merged, (((1,), (1,)), ((), ())), preferred_element_type=F32)
        for n in range(group // 2):
            pair = (row - 1) // 2 + n
            skip, place = (skip_top, pair) if pair < TOP else (skip_rest, pair - TOP)
            total = update[:, n * 2 * half : (n + 1) * 2 * half] + skip[place * 32 : (place + 1) * 32, :]
            for i in range(2):
                spread = lax.div(lane, 2) + i * half
                for p in range(2):
                    evens = jnp.take_along_axis(total[p * 16 : p * 16 + 8], spread, axis=1)
                    odds = jnp.take_along_axis(total[p * 16 + 8 : p * 16 + 16], spread, axis=1)
                    out[:, 4 * pair + 2 * i + p, :] = jnp.where(even, evens, odds)


def network(out_shape, cells_top, cells_rest, left, right, across, skip_top, skip_rest, weights):
    step = out_shape[2] // 2 + 2 * HALO + GAP
    rows = (out_shape[1] // 2 + 2 + POLAR + 2) * step
    vmem = pltpu.VMEM
    return pl.pallas_call(
        network_kernel,
        out_shape=jax.ShapeDtypeStruct(out_shape, F32),
        scratch_shapes=[
            vmem((rows, 128), F32),
            vmem((rows, 128), F32),
            vmem((rows, 512), BF16),
            vmem((rows, 512), BF16),
            vmem((rows, 384), BF16),
            vmem((rows, 256), BF16),
            vmem((rows, 512), BF16),
        ],
        compiler_params=pltpu.CompilerParams(vmem_limit_bytes=40 * 2**20),
        name="network",
    )(cells_top, cells_rest, left, right, across, skip_top, skip_rest, *weights)


def shards(
    latlon_fields,
    remap_table,
    kernel_first,
    kernel_second,
    kernel_down,
    kernel_coarse,
    kernel_up,
    kernel_merge,
    projection,
):
    _, grid_rows, columns = remap_table.shape
    count = lax.axis_size("lon")
    channels, rows, _ = latlon_fields.shape
    half = columns // 2
    parcels = latlon_fields.reshape(channels, rows, count, columns).transpose(2, 1, 0, 3)
    parcels = parcels.reshape(count, rows * channels, columns)
    block = lax.all_to_all(parcels, "lon", split_axis=0, concat_axis=0, tiled=True)
    weights = arrange(
        kernel_first, kernel_second, kernel_down, kernel_coarse, kernel_up, kernel_merge, projection
    )
    onehot, source = locate(remap_table)
    cells_top, left_top, right_top, skip_top = remap(block, onehot, source, range(TOP))
    across = from_behind(cells_top[: POLAR * half], "lon", count // 2)
    cells_rest, left_rest, right_rest, skip_rest = remap(block, onehot, source, range(TOP, grid_rows // 4))
    polar = across.reshape(POLAR, half, -1).astype(F32)
    to_left = jnp.concatenate([left_top, left_rest, polar[:, :HALO].reshape(POLAR * HALO, -1)], axis=0)
    to_right = jnp.concatenate([right_top, right_rest, polar[:, half - HALO :].reshape(POLAR * HALO, -1)], axis=0)
    left = from_behind(to_right, "lon", 1)
    right = from_behind(to_left, "lon", -1)
    out_shape = (projection.shape[0], grid_rows, columns)
    return network(out_shape, cells_top, cells_rest, left, right, across, skip_top, skip_rest, weights)


def solution(mesh):
    return jax.shard_map(
        shards,
        mesh=mesh,
        in_specs=(
            P("groups", "lon", None),
            P(None, None, "lon"),
            P(),
            P(),
            P(),
            P(),
            P(),
            P(),
            P(),
        ),
        out_specs=P("groups", None, "lon"),
        check_vma=False,
    )
```

```python
import jax
import jax.numpy as jnp
from jax import lax
from jax.experimental import pallas as pl
from jax.experimental.pallas import tpu as pltpu
from jax.sharding import PartitionSpec as P

F32 = jnp.float32
BF16 = jnp.bfloat16
HALO = 4
GAP = 8
POLAR = 3
PLACES = 16


def from_behind(block, axis, distance):
    devices = range(lax.axis_size(axis))
    route = [((i - distance) % len(devices), i) for i in devices]
    return lax.ppermute(block, axis, route)


def pack_kernel(fields_hbm, table_hbm, parcels, fields, table, sems):
    channels, rows, _ = fields.shape
    devices, depth, columns = parcels.shape
    depth = rows * channels
    copies = [
        pltpu.make_async_copy(fields_hbm, fields, sems.at[0]),
        pltpu.make_async_copy(table_hbm, table, sems.at[1]),
    ]
    for copy in copies:
        copy.start()
    copies[1].wait()
    lines = [table[0, : 2 * POLAR, :], lax.rem(table[1, : 2 * POLAR, :], columns)]
    lines.append(jnp.zeros((PLACES - 4 * POLAR, columns), jnp.int32))
    lines = jnp.concatenate(lines, axis=0).astype(F32).astype(BF16)
    for target in range(devices):
        parcels[target, 2 * depth :, :] = lines
    copies[0].wait()
    values = fields[...].astype(F32)
    for row in range(rows):
        line = values[:, row, :].astype(BF16)
        for target in range(devices):
            piece = line[:, target * columns : (target + 1) * columns]
            opposite = (target + devices // 2) % devices
            parcels[target, row * channels : (row + 1) * channels, :] = piece
            parcels[opposite, depth + row * channels : depth + (row + 1) * channels, :] = piece


def pack(fields, table, devices):
    channels, rows, _ = fields.shape
    args = (fields, table)
    return pl.pallas_call(
        pack_kernel,
        in_specs=[pl.BlockSpec(memory_space=pltpu.HBM)] * 2,
        out_shape=jax.ShapeDtypeStruct((devices, 2 * rows * channels + PLACES, table.shape[2]), BF16),
        scratch_shapes=[pltpu.VMEM(a.shape, a.dtype) for a in args] + [pltpu.SemaphoreType.DMA((2,))],
        compiler_params=pltpu.CompilerParams(vmem_limit_bytes=16 * 2**20),
        name="pack",
    )(*[pltpu.with_memory_space_constraint(a, pltpu.HBM) for a in args])


def tap(kernel_ref, row, col):
    if 0 <= row < 3 and 0 <= col < 3:
        return kernel_ref[row, col].astype(F32)
    return jnp.zeros(kernel_ref.shape[2:], F32)


def arrange(first, second, down, coarse, up, merge, projection, w1, w2, wd, wc, wu, wm, wp):
    channels = second.shape[3]
    inputs = first.shape[2]
    for half in range(2):
        for side in range(2):
            for p in range(2):
                for q in range(2):
                    t = 1 + p if half == 0 else (3, 0)[p]
                    u = 1 + q if side == 0 else (3, 0)[q]
                    at = (((half * 2 + side) * 2 + p) * 2 + q) * inputs
                    pieces = [tap(first, t - a, u - b) for a in range(2) for b in range(2)]
                    w1[at : at + inputs, :] = jnp.concatenate(pieces, axis=1).astype(BF16)
    for t in range(4):
        for code in range(4):
            at = (t * 4 + code) * channels
            source = (0, 1, -2, -1)[code]
            for p in range(2):
                pair = [tap(second, t - p, source - target + 1) for target in (-1, 0)]
                w2[at : at + channels, p * 128 : (p + 1) * 128] = jnp.concatenate(pair, axis=0).T.astype(BF16)
            source = code - 1
            for p in range(2):
                pair = [tap(merge, t - p, source - target + 1) for target in (0, 1)]
                pair = jnp.concatenate(pair, axis=0).T.astype(BF16)
                wm[at : at + channels, p * 128 : (p + 1) * 128] = pair[:channels]
                wm[16 * channels + at : 16 * channels + at + channels, p * 128 : (p + 1) * 128] = pair[channels:]
            if t < 3:
                wd[at : at + channels, :] = tap(down, t, code).astype(BF16)
    wide = coarse.shape[3]
    for a in range(3):
        for b in range(3):
            at = (a * 3 + b) * wide
            wc[at : at + wide, :] = tap(coarse, a, b).T.astype(BF16)
    row_taps = ((1, 3), (0, 2))
    col_taps = ((0, 2), (3, 1))
    for di in range(2):
        for dj in range(2):
            at = (di * 2 + dj) * wide
            for p in range(2):
                pair = jnp.concatenate([tap(up, row_taps[p][di], col_taps[q][dj]) for q in range(2)], axis=0)
                wu[at : at + wide, p * 128 : (p + 1) * 128] = pair.T.astype(BF16)
    rows = projection[...].astype(F32)
    blank = jnp.zeros_like(rows)
    lines = [jnp.concatenate([rows if m == n else blank for m in range(4)], axis=1) for n in range(4)]
    wp[...] = jnp.concatenate(lines, axis=0).astype(BF16)


def locate(rows, cols, onehot, source):
    grid_rows, columns = rows.shape
    half = columns // 2
    code = rows * columns + cols
    lane = lax.broadcasted_iota(jnp.int32, (grid_rows, columns), 1)
    odd = [jnp.take_along_axis(code, lax.rem(lane, half) * 2 + q, axis=1) for q in range(2)]
    left = lax.broadcasted_iota(jnp.int32, (1, columns), 1) < half
    place = lax.broadcasted_iota(jnp.int32, (2 * columns, columns), 0)
    for pair in range(grid_rows // 4):
        for p in range(2):
            for q in range(2):
                n = p * 2 + q
                above, below = 4 * pair + p, 4 * pair + 2 + p
                line = jnp.where(left, odd[q][above : above + 1, :], odd[q][below : below + 1, :])
                source[4 * pair + n : 4 * pair + n + 1, :] = lax.div(line, 2 * columns)
                here = place == lax.rem(line, 2 * columns)
                onehot[pair * 2 * columns : (pair + 1) * 2 * columns, n * columns : (n + 1) * columns] = jnp.where(
                    here, 1.0, 0.0
                ).astype(BF16)


def prepare_kernel(*refs):
    args, outs, scratch, sems = refs[:8], refs[8:17], refs[17:25], refs[25]
    copies = [
        pltpu.make_async_copy(source, target, sems.at[n]) for n, (source, target) in enumerate(zip(args, scratch))
    ]
    for copy in copies:
        copy.start()
    copies[0].wait()
    table = scratch[0]
    locate(table[0], lax.rem(table[1], table.shape[2]), *outs[:2])
    for copy in copies[1:]:
        copy.wait()
    arrange(*scratch[1:], *outs[2:])


def prepare(table, first, second, down, coarse, up, merge, projection):
    channels, wide = second.shape[3], coarse.shape[3]
    columns = table.shape[2]
    pairs = table.shape[1] // 4
    shapes = (
        (16 * first.shape[3], 4 * channels),
        (16 * channels, 4 * channels),
        (12 * channels, wide),
        (9 * wide, wide),
        (4 * wide, 4 * channels),
        (32 * channels, 4 * channels),
        (4 * projection.shape[0], 4 * channels),
    )
    args = (table, jnp.swapaxes(first, 2, 3), second, jnp.swapaxes(down, 2, 3), coarse, up, merge, projection)
    return pl.pallas_call(
        prepare_kernel,
        in_specs=[pl.BlockSpec(memory_space=pltpu.HBM)] * 8,
        out_shape=[
            jax.ShapeDtypeStruct((pairs * 2 * columns, 4 * columns), BF16),
            jax.ShapeDtypeStruct((pairs * 4, columns), jnp.int32),
        ]
        + [jax.ShapeDtypeStruct(s, BF16) for s in shapes],
        scratch_shapes=[pltpu.VMEM(a.shape, a.dtype) for a in args] + [pltpu.SemaphoreType.DMA((8,))],
        compiler_params=pltpu.CompilerParams(vmem_limit_bytes=16 * 2**20),
        name="prepare",
    )(*[pltpu.with_memory_space_constraint(a, pltpu.HBM) for a in args])


def remap_kernel(block, onehot, source, cells, to_left, to_right, skip, polar_onehot, polar_source):
    devices, depth, columns = block.shape
    depth = (depth - PLACES) // 2
    channels = depth // 2
    opposite = lax.rem(lax.axis_index("lon") + devices // 2, devices)
    places = block[opposite, 2 * depth :, :].astype(F32).astype(jnp.int32)
    blank = jnp.zeros((polar_source.shape[0] - 2 * POLAR, columns), jnp.int32)
    rows = jnp.concatenate([places[: 2 * POLAR], blank], axis=0)
    cols = jnp.concatenate([places[2 * POLAR : 4 * POLAR], blank], axis=0)
    locate(rows, cols, polar_onehot, polar_source)
    half = columns // 2
    fields = []
    for side in range(2):
        at = side * depth
        upper = block[:, at : at + channels, :].reshape(devices * channels, columns)
        lower = block[:, at + channels : at + depth, :].reshape(devices * channels, columns)
        fields.append(jnp.concatenate([upper, lower], axis=1))
    pairs = cells.shape[0] // columns
    own_pairs = skip.shape[0] // 32
    for pair in range(pairs):
        own = pair < own_pairs
        at = pair if own else pair - own_pairs
        chosen = (onehot if own else polar_onehot)[at * 2 * columns : (at + 1) * 2 * columns, :]
        found = jnp.dot(fields[0 if own else 1], chosen, preferred_element_type=F32)
        lines = []
        for n in range(4):
            line = (source if own else polar_source)[4 * at + n : 4 * at + n + 1, :]
            line = jnp.broadcast_to(line, (channels, columns))
            total = jnp.zeros((channels, columns), F32)
            for s in range(devices):
                value = found[s * channels : (s + 1) * channels, n * columns : (n + 1) * columns]
                total = jnp.where(line == s, value, total)
            lines.append(total)
            if own:
                skip[(pair * 4 + n) * 8 : (pair * 4 + n + 1) * 8, :] = total[:8]
        turned = jnp.concatenate(lines + lines, axis=0).T
        cells[pair * columns : (pair + 1) * columns, :] = turned.astype(BF16)
        for i in range(2):
            row = (pair * 2 + i) * HALO
            to_left[row : row + HALO, :] = turned[i * half : i * half + HALO]
            to_right[row : row + HALO, :] = turned[(i + 1) * half - HALO : (i + 1) * half]


def remap(block, onehot, source):
    columns = block.shape[2]
    own_rows = source.shape[0]
    polar_rows = 4 * ((POLAR + 1) // 2)
    count = (own_rows + polar_rows) // 4
    return pl.pallas_call(
        remap_kernel,
        out_shape=[
            jax.ShapeDtypeStruct((count * columns, columns), BF16),
            jax.ShapeDtypeStruct((count * 2 * HALO, columns), F32),
            jax.ShapeDtypeStruct((count * 2 * HALO, columns), F32),
            jax.ShapeDtypeStruct((own_rows * 8, columns), F32),
        ],
        scratch_shapes=[
            pltpu.VMEM((polar_rows // 4 * 2 * columns, 4 * columns), BF16),
            pltpu.VMEM((polar_rows, columns), jnp.int32),
        ],
        compiler_params=pltpu.CompilerParams(vmem_limit_bytes=16 * 2**20),
        name="remap",
    )(block, onehot, source)


def silu(values):
    h = 0.5 * values
    return (h + h * jnp.tanh(h)).astype(BF16).astype(F32)


def ring(values, step, shift):
    rows = [pltpu.roll(values[at : at + step], shift % step, 0) for at in range(0, values.shape[0], step)]
    return rows[0] if len(rows) == 1 else jnp.concatenate(rows, axis=0)


def network_kernel(
    cells, left, right, skip, w1, w2, wd, wc, wu, wm, wp, out, x0, y0, y1, y2, yc, yo, yu
):
    half = out.shape[2] // 2
    blocks = out.shape[1] // 2
    step = half + 2 * HALO + GAP
    polar = POLAR
    top = 0
    bottom = blocks + 1
    pole = blocks + 2
    end = pole + polar + 1
    group = 4

    def at(row, count=1):
        return slice(row * step, (row + count) * step)

    def chunks(polar_rows):
        return [(1 + i, group) for i in range(0, blocks, group)] + [(pole + 1, polar_rows)]

    def lane_mask(rows, width):
        return lax.rem(lax.div(lax.broadcasted_iota(jnp.int32, (rows, 128), 1), width), 2) == 0

    x0[...] = jnp.zeros_like(x0)
    for i in range(blocks + polar):
        base = (1 + i if i < blocks else pole + 1 + i - blocks) * step
        x0[base : base + half, :] = cells[i * half : (i + 1) * half, :].astype(F32)
        x0[base + half : base + half + HALO, :] = right[i * HALO : (i + 1) * HALO, :]
        x0[base + step - HALO : base + step, :] = left[i * HALO : (i + 1) * HALO, :]
    x0[at(top), :] = pltpu.roll(x0[at(pole + 1), :], 32, 1)
    x0[at(pole), :] = pltpu.roll(x0[at(1), :], 32, 1)
    for row in range(0, end + 1):
        x = x0[at(row), :]
        side = jnp.where(lane_mask(step, 16), ring(x, step, -1), ring(x, step, 1))
        y0[at(row), :] = jnp.where(lane_mask(step, 64), x, side)

    def store_fine(y, row, count, values, shift):
        moved = ring(values, step, shift).astype(BF16)
        values = values.astype(BF16)
        for p in range(2):
            lanes = slice(p * 128, (p + 1) * 128)
            y[at(row, count), p * 256 : p * 256 + 128] = values[:, lanes]
            y[at(row, count), p * 256 + 128 : p * 256 + 256] = moved[:, lanes]

    def edges_fine(y, polar_rows):
        y[at(top), 256:512] = y[at(pole + 1), 0:256]
        y[at(pole), 256:512] = y[at(1), 0:256]
        y[at(bottom), 0:256] = jnp.zeros((step, 256), BF16)
        y[at(pole + 1 + polar_rows), 0:256] = jnp.zeros((step, 256), BF16)

    def product(pieces, weights):
        return jnp.dot(jnp.concatenate(pieces, axis=1), weights[...], preferred_element_type=F32)

    for row, count in chunks(polar):
        mask = lane_mask(count * step, 32)
        vertical = jnp.where(mask, y0[at(row + 1, count), :], y0[at(row - 1, count), :])
        pieces = [y0[at(row, count), :].astype(BF16), vertical.astype(BF16)]
        store_fine(y1, row, count, silu(product(pieces, w1)), 1)
    edges_fine(y1, polar)

    for row, count in chunks(polar - 1):
        pieces = [y1[at(row - 1, count), 256:512], y1[at(row, count), :], y1[at(row + 1, count), 0:256]]
        store_fine(y2, row, count, silu(product(pieces, w2)), -1)
    edges_fine(y2, polar - 1)

    for row, count in chunks(polar - 1):
        pieces = [y2[at(row - 1, count), 256:512], y2[at(row, count), :]]
        values = silu(product(pieces, wd))
        yc[at(row, count), 0:128] = ring(values, step, 1).astype(BF16)
        yc[at(row, count), 128:256] = values.astype(BF16)
        yc[at(row, count), 256:384] = ring(values, step, -1).astype(BF16)
    yc[at(top), :] = yc[at(pole + 1), :]
    yc[at(pole), :] = yc[at(1), :]
    yc[at(bottom), :] = jnp.zeros((step, 384), BF16)

    for row, count in chunks(polar - 2):
        pieces = [yc[at(row + a, count), :] for a in (-1, 0, 1)]
        values = silu(product(pieces, wc))
        yo[at(row, count), 0:128] = ring(values, step, 1).astype(BF16)
        yo[at(row, count), 128:256] = values.astype(BF16)
    yo[at(bottom), :] = jnp.zeros((step, 256), BF16)
    yo[at(pole + 2), :] = jnp.zeros((step, 256), BF16)

    for row, count in chunks(polar - 2):
        pieces = [yo[at(row, count), :], yo[at(row + 1, count), :]]
        store_fine(yu, row, count, silu(product(pieces, wu)), -1)
    edges_fine(yu, polar - 2)

    lane = lax.broadcasted_iota(jnp.int32, (8, 2 * half), 1)
    even = lax.rem(lane, 2) == 0
    for row in range(1, 1 + blocks, group):

        def own(y, offset, lanes):
            rows = [y[(row + offset + i) * step : (row + offset + i) * step + half, lanes] for i in range(group)]
            return jnp.concatenate(rows, axis=0)

        pieces = []
        for y in (y2, yu):
            pieces += [own(y, -1, slice(256, 512)), own(y, 0, slice(0, 512)), own(y, 1, slice(0, 256))]
        merged = silu(product(pieces, wm)).astype(BF16)
        update = lax.dot_general(wp[...], merged, (((1,), (1,)), ((), ())), preferred_element_type=F32)
        for n in range(group // 2):
            pair = (row - 1) // 2 + n
            total = update[:, n * 2 * half : (n + 1) * 2 * half] + skip[pair * 32 : (pair + 1) * 32, :]
            for i in range(2):
                spread = lax.div(lane, 2) + i * half
                for p in range(2):
                    evens = jnp.take_along_axis(total[p * 16 : p * 16 + 8], spread, axis=1)
                    odds = jnp.take_along_axis(total[p * 16 + 8 : p * 16 + 16], spread, axis=1)
                    out[:, 4 * pair + 2 * i + p, :] = jnp.where(even, evens, odds)


def network(out_shape, cells, left, right, skip, weights):
    step = out_shape[2] // 2 + 2 * HALO + GAP
    rows = (out_shape[1] // 2 + 2 + POLAR + 2) * step
    vmem = pltpu.VMEM
    return pl.pallas_call(
        network_kernel,
        out_shape=jax.ShapeDtypeStruct(out_shape, F32),
        scratch_shapes=[
            vmem((rows, 128), F32),
            vmem((rows, 128), F32),
            vmem((rows, 512), BF16),
            vmem((rows, 512), BF16),
            vmem((rows, 384), BF16),
            vmem((rows, 256), BF16),
            vmem((rows, 512), BF16),
        ],
        compiler_params=pltpu.CompilerParams(vmem_limit_bytes=24 * 2**20),
        name="network",
    )(cells, left, right, skip, *weights)


def shards(
    latlon_fields,
    remap_table,
    kernel_first,
    kernel_second,
    kernel_down,
    kernel_coarse,
    kernel_up,
    kernel_merge,
    projection,
):
    _, grid_rows, columns = remap_table.shape
    count = lax.axis_size("lon")
    parcels = pack(latlon_fields, remap_table, count)
    block = lax.all_to_all(parcels, "lon", split_axis=0, concat_axis=0, tiled=True)
    onehot, source, *weights = prepare(
        remap_table, kernel_first, kernel_second, kernel_down, kernel_coarse, kernel_up, kernel_merge, projection
    )
    cells, to_left, to_right, skip = remap(block, onehot, source)
    left = from_behind(to_right, "lon", 1)
    right = from_behind(to_left, "lon", -1)
    return network((projection.shape[0], grid_rows, columns), cells, left, right, skip, weights)


def solution(mesh):
    return jax.shard_map(
        shards,
        mesh=mesh,
        in_specs=(
            P("groups", "lon", None),
            P(None, None, "lon"),
            P(),
            P(),
            P(),
            P(),
            P(),
            P(),
            P(),
        ),
        out_specs=P("groups", None, "lon"),
        check_vma=False,
    )
```

```python
import jax
import jax.numpy as jnp
from jax import lax
from jax.experimental import pallas as pl
from jax.experimental.pallas import tpu as pltpu
from jax.sharding import PartitionSpec as P

F32 = jnp.float32
BF16 = jnp.bfloat16
HALO = 4
POLAR = 3
PLACES = 16


def swap(block, axis, first):
    devices = lax.axis_size(axis)
    pairs = [((first + i) % devices, (first + i + 1) % devices) for i in range(0, devices, 2)]
    return lax.ppermute(block, axis, pairs + [(b, a) for a, b in pairs])


def pack_kernel(fields_hbm, table_hbm, parcels, fields, table, sems):
    channels, rows, _ = fields.shape
    devices, depth, columns = parcels.shape
    depth = rows * channels
    copies = [
        pltpu.make_async_copy(fields_hbm, fields, sems.at[0]),
        pltpu.make_async_copy(table_hbm, table, sems.at[1]),
    ]
    for copy in copies:
        copy.start()
    copies[1].wait()
    lines = [table[0, : 2 * POLAR, :], lax.rem(table[1, : 2 * POLAR, :], columns)]
    lines.append(jnp.zeros((PLACES - 4 * POLAR, columns), jnp.int32))
    lines = jnp.concatenate(lines, axis=0).astype(F32).astype(BF16)
    for target in range(devices):
        parcels[target, 2 * depth :, :] = lines
    copies[0].wait()
    values = fields[...].astype(F32)
    for row in range(rows):
        line = values[:, row, :].astype(BF16)
        for target in range(devices):
            piece = line[:, target * columns : (target + 1) * columns]
            opposite = (target + devices // 2) % devices
            parcels[target, row * channels : (row + 1) * channels, :] = piece
            parcels[opposite, depth + row * channels : depth + (row + 1) * channels, :] = piece


def pack(fields, table, devices):
    channels, rows, _ = fields.shape
    args = (fields, table)
    return pl.pallas_call(
        pack_kernel,
        in_specs=[pl.BlockSpec(memory_space=pltpu.HBM)] * 2,
        out_shape=jax.ShapeDtypeStruct((devices, 2 * rows * channels + PLACES, table.shape[2]), BF16),
        scratch_shapes=[pltpu.VMEM(a.shape, a.dtype) for a in args] + [pltpu.SemaphoreType.DMA((2,))],
        compiler_params=pltpu.CompilerParams(vmem_limit_bytes=16 * 2**20),
        name="pack",
    )(*[pltpu.with_memory_space_constraint(a, pltpu.HBM) for a in args])


def tap(kernel_ref, row, col):
    if 0 <= row < 3 and 0 <= col < 3:
        return kernel_ref[row, col].astype(F32)
    return jnp.zeros(kernel_ref.shape[2:], F32)


def arrange(first, second, down, coarse, up, merge, projection, w1, w2, wd, wc, wu, wm, wp):
    channels = second.shape[3]
    inputs = first.shape[2]
    for half in range(2):
        for side in range(2):
            for p in range(2):
                for q in range(2):
                    t = 1 + p if half == 0 else (3, 0)[p]
                    u = 1 + q if side == 0 else (3, 0)[q]
                    at = (((half * 2 + side) * 2 + p) * 2 + q) * inputs
                    pieces = [tap(first, t - a, u - b) for a in range(2) for b in range(2)]
                    w1[at : at + inputs, :] = jnp.concatenate(pieces, axis=1).astype(BF16)
    for t in range(4):
        for code in range(4):
            at = (t * 4 + code) * channels
            source = (0, 1, -2, -1)[code]
            for p in range(2):
                pair = [tap(second, t - p, source - target + 1) for target in (-1, 0)]
                w2[at : at + channels, p * 128 : (p + 1) * 128] = jnp.concatenate(pair, axis=0).T.astype(BF16)
            source = code - 1
            for p in range(2):
                pair = [tap(merge, t - p, source - target + 1) for target in (0, 1)]
                pair = jnp.concatenate(pair, axis=0).T.astype(BF16)
                wm[at : at + channels, p * 128 : (p + 1) * 128] = pair[:channels]
                wm[16 * channels + at : 16 * channels + at + channels, p * 128 : (p + 1) * 128] = pair[channels:]
            if t < 3:
                wd[at : at + channels, :] = tap(down, t, code).astype(BF16)
    wide = coarse.shape[3]
    for a in range(3):
        for b in range(3):
            at = (a * 3 + b) * wide
            wc[at : at + wide, :] = tap(coarse, a, b).T.astype(BF16)
    row_taps = ((1, 3), (0, 2))
    col_taps = ((0, 2), (3, 1))
    for di in range(2):
        for dj in range(2):
            at = (di * 2 + dj) * wide
            for p in range(2):
                pair = jnp.concatenate([tap(up, row_taps[p][di], col_taps[q][dj]) for q in range(2)], axis=0)
                wu[at : at + wide, p * 128 : (p + 1) * 128] = pair.T.astype(BF16)
    rows = projection[...].astype(F32)
    blank = jnp.zeros_like(rows)
    lines = [jnp.concatenate([rows if m == n else blank for m in range(4)], axis=1) for n in range(4)]
    wp[...] = jnp.concatenate(lines, axis=0).astype(BF16)


def locate(rows, cols, onehot, source):
    grid_rows, columns = rows.shape
    half = columns // 2
    code = rows * columns + cols
    lane = lax.broadcasted_iota(jnp.int32, (grid_rows, columns), 1)
    odd = [jnp.take_along_axis(code, lax.rem(lane, half) * 2 + q, axis=1) for q in range(2)]
    left = lax.broadcasted_iota(jnp.int32, (1, columns), 1) < half
    place = lax.broadcasted_iota(jnp.int32, (2 * columns, columns), 0)
    for pair in range(grid_rows // 4):
        for p in range(2):
            for q in range(2):
                n = p * 2 + q
                above, below = 4 * pair + p, 4 * pair + 2 + p
                line = jnp.where(left, odd[q][above : above + 1, :], odd[q][below : below + 1, :])
                source[4 * pair + n : 4 * pair + n + 1, :] = lax.div(line, 2 * columns)
                here = place == lax.rem(line, 2 * columns)
                onehot[pair * 2 * columns : (pair + 1) * 2 * columns, n * columns : (n + 1) * columns] = jnp.where(
                    here, 1.0, 0.0
                ).astype(BF16)


def prepare_kernel(*refs):
    args, outs, scratch, sems = refs[:8], refs[8:17], refs[17:25], refs[25]
    copies = [
        pltpu.make_async_copy(source, target, sems.at[n]) for n, (source, target) in enumerate(zip(args, scratch))
    ]
    for copy in copies:
        copy.start()
    copies[0].wait()
    table = scratch[0]
    locate(table[0], lax.rem(table[1], table.shape[2]), *outs[:2])
    for copy in copies[1:]:
        copy.wait()
    arrange(*scratch[1:], *outs[2:])


def prepare(table, first, second, down, coarse, up, merge, projection):
    channels, wide = second.shape[3], coarse.shape[3]
    columns = table.shape[2]
    pairs = table.shape[1] // 4
    shapes = (
        (16 * first.shape[3], 4 * channels),
        (16 * channels, 4 * channels),
        (12 * channels, wide),
        (9 * wide, wide),
        (4 * wide, 4 * channels),
        (32 * channels, 4 * channels),
        (4 * projection.shape[0], 4 * channels),
    )
    args = (table, jnp.swapaxes(first, 2, 3), second, jnp.swapaxes(down, 2, 3), coarse, up, merge, projection)
    return pl.pallas_call(
        prepare_kernel,
        in_specs=[pl.BlockSpec(memory_space=pltpu.HBM)] * 8,
        out_shape=[
            jax.ShapeDtypeStruct((pairs * 2 * columns, 4 * columns), BF16),
            jax.ShapeDtypeStruct((pairs * 4, columns), jnp.int32),
        ]
        + [jax.ShapeDtypeStruct(s, BF16) for s in shapes],
        scratch_shapes=[pltpu.VMEM(a.shape, a.dtype) for a in args] + [pltpu.SemaphoreType.DMA((8,))],
        compiler_params=pltpu.CompilerParams(vmem_limit_bytes=16 * 2**20),
        name="prepare",
    )(*[pltpu.with_memory_space_constraint(a, pltpu.HBM) for a in args])


def remap_kernel(block, onehot, source, cells, inner, outer, skip, polar_onehot, polar_source):
    even = lax.rem(lax.axis_index("lon"), 2) == 0
    devices, depth, columns = block.shape
    depth = (depth - PLACES) // 2
    channels = depth // 2
    opposite = lax.rem(lax.axis_index("lon") + devices // 2, devices)
    places = block[opposite, 2 * depth :, :].astype(F32).astype(jnp.int32)
    blank = jnp.zeros((polar_source.shape[0] - 2 * POLAR, columns), jnp.int32)
    rows = jnp.concatenate([places[: 2 * POLAR], blank], axis=0)
    cols = jnp.concatenate([places[2 * POLAR : 4 * POLAR], blank], axis=0)
    locate(rows, cols, polar_onehot, polar_source)
    half = columns // 2
    fields = []
    for side in range(2):
        at = side * depth
        upper = block[:, at : at + channels, :].reshape(devices * channels, columns)
        lower = block[:, at + channels : at + depth, :].reshape(devices * channels, columns)
        fields.append(jnp.concatenate([upper, lower], axis=1))
    pairs = cells.shape[0] // columns
    own_pairs = skip.shape[0] // 32
    for pair in range(pairs):
        own = pair < own_pairs
        at = pair if own else pair - own_pairs
        chosen = (onehot if own else polar_onehot)[at * 2 * columns : (at + 1) * 2 * columns, :]
        found = jnp.dot(fields[0 if own else 1], chosen, preferred_element_type=F32)
        lines = []
        for n in range(4):
            line = (source if own else polar_source)[4 * at + n : 4 * at + n + 1, :]
            line = jnp.broadcast_to(line, (channels, columns))
            total = jnp.zeros((channels, columns), F32)
            for s in range(devices):
                value = found[s * channels : (s + 1) * channels, n * columns : (n + 1) * columns]
                total = jnp.where(line == s, value, total)
            lines.append(total)
            if own:
                skip[(pair * 4 + n) * 8 : (pair * 4 + n + 1) * 8, :] = total[:8]
        turned = jnp.concatenate(lines + lines, axis=0).T
        cells[pair * columns : (pair + 1) * columns, :] = turned.astype(BF16)
        for i in range(2):
            row = (pair * 2 + i) * HALO
            begin = turned[i * half : i * half + HALO]
            finish = turned[(i + 1) * half - HALO : (i + 1) * half]
            inner[row : row + HALO, :] = jnp.where(even, finish, begin)
            outer[row : row + HALO, :] = jnp.where(even, begin, finish)


def remap(block, onehot, source):
    columns = block.shape[2]
    own_rows = source.shape[0]
    polar_rows = 4 * ((POLAR + 1) // 2)
    count = (own_rows + polar_rows) // 4
    return pl.pallas_call(
        remap_kernel,
        out_shape=[
            jax.ShapeDtypeStruct((count * columns, columns), BF16),
            jax.ShapeDtypeStruct((count * 2 * HALO, columns), F32),
            jax.ShapeDtypeStruct((count * 2 * HALO, columns), F32),
            jax.ShapeDtypeStruct((own_rows * 8, columns), F32),
        ],
        scratch_shapes=[
            pltpu.VMEM((polar_rows // 4 * 2 * columns, 4 * columns), BF16),
            pltpu.VMEM((polar_rows, columns), jnp.int32),
        ],
        compiler_params=pltpu.CompilerParams(vmem_limit_bytes=16 * 2**20),
        name="remap",
    )(block, onehot, source)


def silu(values):
    h = 0.5 * values
    return (h + h * jnp.tanh(h)).astype(BF16).astype(F32)


def ring(values, step, shift):
    rows = [pltpu.roll(values[at : at + step], shift % step, 0) for at in range(0, values.shape[0], step)]
    return rows[0] if len(rows) == 1 else jnp.concatenate(rows, axis=0)


class Rows:
    def __init__(self, step, blocks):
        self.step, self.blocks = step, blocks
        self.top, self.bottom, self.pole = 0, blocks + 1, blocks + 2
        self.count = blocks + 2 + POLAR + 2

    def __call__(self, row, count=1):
        return slice(row * self.step, (row + count) * self.step)

    def of(self, i):
        return 1 + i if i < self.blocks else self.pole + 1 + i - self.blocks

    def mask(self, count, width):
        lane = lax.broadcasted_iota(jnp.int32, (count * self.step, 128), 1)
        return lax.rem(lax.div(lane, width), 2) == 0


def product(pieces, weights):
    return jnp.dot(jnp.concatenate(pieces, axis=1), weights[...], preferred_element_type=F32)


def layers(at, chunks, moved, x0, y0, y1, y2, yc, yo, yu, w1, w2, wd, wc, wu):
    step, top, bottom, pole = at.step, at.top, at.bottom, at.pole
    x0[at(top), :] = pltpu.roll(x0[at(pole + 1), :], 32, 1)
    x0[at(pole), :] = pltpu.roll(x0[at(1), :], 32, 1)
    for row in range(at.count):
        x = x0[at(row), :]
        side = jnp.where(at.mask(1, 16), moved("x0", row, 1, x, -1), moved("x0", row, 1, x, 1))
        y0[at(row), :] = jnp.where(at.mask(1, 64), x, side)

    def store_fine(y, name, row, count, values, shift):
        shifted = moved(name, row, count, values, shift).astype(BF16)
        values = values.astype(BF16)
        for p in range(2):
            lanes = slice(p * 128, (p + 1) * 128)
            y[at(row, count), p * 256 : p * 256 + 128] = values[:, lanes]
            y[at(row, count), p * 256 + 128 : p * 256 + 256] = shifted[:, lanes]

    def edges_fine(y, polar_rows):
        y[at(top), 256:512] = y[at(pole + 1), 0:256]
        y[at(pole), 256:512] = y[at(1), 0:256]
        y[at(bottom), 0:256] = jnp.zeros((step, 256), BF16)
        y[at(pole + 1 + polar_rows), 0:256] = jnp.zeros((step, 256), BF16)

    for row, count in chunks(POLAR):
        vertical = jnp.where(at.mask(count, 32), y0[at(row + 1, count), :], y0[at(row - 1, count), :])
        pieces = [y0[at(row, count), :].astype(BF16), vertical.astype(BF16)]
        store_fine(y1, "y1", row, count, silu(product(pieces, w1)), 1)
    edges_fine(y1, POLAR)

    for row, count in chunks(POLAR - 1):
        pieces = [y1[at(row - 1, count), 256:512], y1[at(row, count), :], y1[at(row + 1, count), 0:256]]
        store_fine(y2, "y2", row, count, silu(product(pieces, w2)), -1)
    edges_fine(y2, POLAR - 1)

    for row, count in chunks(POLAR - 1):
        values = silu(product([y2[at(row - 1, count), 256:512], y2[at(row, count), :]], wd))
        yc[at(row, count), 0:128] = moved("yc", row, count, values, 1).astype(BF16)
        yc[at(row, count), 128:256] = values.astype(BF16)
        yc[at(row, count), 256:384] = moved("yc", row, count, values, -1).astype(BF16)
    yc[at(top), :] = yc[at(pole + 1), :]
    yc[at(pole), :] = yc[at(1), :]
    yc[at(bottom), :] = jnp.zeros((step, 384), BF16)

    for row, count in chunks(POLAR - 2):
        values = silu(product([yc[at(row + a, count), :] for a in (-1, 0, 1)], wc))
        yo[at(row, count), 0:128] = moved("yo", row, count, values, 1).astype(BF16)
        yo[at(row, count), 128:256] = values.astype(BF16)
    yo[at(bottom), :] = jnp.zeros((step, 256), BF16)
    yo[at(pole + 2), :] = jnp.zeros((step, 256), BF16)

    for row, count in chunks(POLAR - 2):
        values = silu(product([yo[at(row, count), :], yo[at(row + 1, count), :]], wu))
        store_fine(yu, "yu", row, count, values, -1)
    edges_fine(yu, POLAR - 2)


def merge(at, row, count, y2, yu, wm, wp):
    pieces = []
    for y in (y2, yu):
        pieces += [y[at(row - 1, count), 256:512], y[at(row, count), :], y[at(row + 1, count), 0:256]]
    merged = silu(product(pieces, wm)).astype(BF16)
    return lax.dot_general(wp[...], merged, (((1,), (1,)), ((), ())), preferred_element_type=F32)


SHARED = (("y1", 256, (1,)), ("y2", 256, (-1,)), ("yc", 128, (1, -1)), ("yo", 128, (1,)), ("yu", 256, (-1,)))
SHARED_KEYS = [(name, lanes, shift) for name, lanes, shifts in SHARED for shift in shifts]


def inside_kernel(cells, skip, w1, w2, wd, wc, wu, wm, wp, update, rest, *refs):
    shared, scratch = refs[: len(SHARED_KEYS)], refs[len(SHARED_KEYS) :]
    half = update.shape[1] // 2
    blocks = update.shape[0] // 16
    at = Rows(half, blocks)
    group = 4

    def chunks(polar_rows):
        return [(1 + i, group) for i in range(0, blocks, group)] + [(at.pole + 1, polar_rows)]

    def moved(name, row, count, values, shift):
        for (key, _, way), ref in zip(SHARED_KEYS, shared):
            if key == name and way == shift:
                column = half - HALO - 1 if shift == 1 else HALO
                for i in range(count):
                    ref[row + i : row + i + 1, :] = values[i * half + column : i * half + column + 1, :]
        return ring(values, half, shift)

    x0 = scratch[0]
    for row in (at.top, at.bottom, at.pole, at.count - 1):
        x0[at(row), :] = jnp.zeros((half, 128), F32)
    for i in range(blocks + POLAR):
        x0[at(at.of(i)), :] = cells[i * half : (i + 1) * half, :].astype(F32)
    layers(at, chunks, moved, *scratch, w1, w2, wd, wc, wu)

    y2, yu = scratch[3], scratch[6]
    lane = lax.broadcasted_iota(jnp.int32, (8, 2 * half), 1)
    even = lax.rem(lane, 2) == 0

    def weave(values, i, p):
        spread = lax.div(lane, 2) + i * half
        evens = jnp.take_along_axis(values[p * 16 : p * 16 + 8], spread, axis=1)
        odds = jnp.take_along_axis(values[p * 16 + 8 : p * 16 + 16], spread, axis=1)
        return jnp.where(even, evens, odds)

    for row in range(1, 1 + blocks, group):
        found = merge(at, row, group, y2, yu, wm, wp)
        for n in range(group // 2):
            pair = (row - 1) // 2 + n
            own = found[:, n * 2 * half : (n + 1) * 2 * half]
            base = skip[pair * 32 : (pair + 1) * 32, :]
            for i in range(2):
                for p in range(2):
                    line = (4 * pair + 2 * i + p) * 8
                    update[line : line + 8, :] = weave(own, i, p)
                    rest[line : line + 8, :] = weave(base, i, p)


def edges_kernel(cells, inner, outer, w1, w2, wd, wc, wu, wm, wp, update, rest, *refs):
    shared, out, scratch = refs[: len(SHARED_KEYS)], refs[len(SHARED_KEYS)], refs[len(SHARED_KEYS) + 1 :]
    even = lax.rem(lax.axis_index("lon"), 2) == 0
    half = out.shape[2] // 2
    blocks = out.shape[1] // 2
    step = 4 * HALO
    at = Rows(step, blocks)
    place = lax.broadcasted_iota(jnp.int32, (step, 128), 0)
    x0 = scratch[0]
    beside = {}
    for row in (at.top, at.bottom, at.pole, at.count - 1):
        x0[at(row), :] = jnp.zeros((step, 128), F32)
    for i in range(blocks + POLAR):
        row = at.of(i)
        begin = cells[i * half : i * half + 16, :].astype(F32)
        finish = cells[(i + 1) * half - 16 : (i + 1) * half, :].astype(F32)
        near = inner[i * HALO : (i + 1) * HALO, :]
        far = outer[i * HALO : (i + 1) * HALO, :]
        base = row * step
        x0[base : base + HALO, :] = jnp.where(even, far, near)
        x0[base + HALO : base + 2 * HALO, :] = begin[:HALO]
        x0[base + 2 * HALO : base + 3 * HALO, :] = finish[16 - HALO :]
        x0[base + 3 * HALO : base + 4 * HALO, :] = jnp.where(even, near, far)
        beside[row] = {-1: begin[HALO : HALO + 1], 1: finish[15 - HALO : 16 - HALO]}
    beside[at.top] = {way: pltpu.roll(line, 32, 1) for way, line in beside[at.pole + 1].items()}
    beside[at.pole] = {way: pltpu.roll(line, 32, 1) for way, line in beside[1].items()}

    def moved(name, row, count, values, shift):
        lines = []
        target = 2 * HALO if shift == 1 else 2 * HALO - 1
        for i in range(count):
            line = pltpu.roll(values[i * step : (i + 1) * step], shift % step, 0)
            if name == "x0":
                own = beside[row + i][shift] if row + i in beside else None
            else:
                ref = next(r for (key, _, way), r in zip(SHARED_KEYS, shared) if (key, way) == (name, shift))
                own = ref[row + i : row + i + 1, :]
            if own is not None:
                parts = []
                for lanes in range(0, values.shape[1], 128):
                    fix = jnp.broadcast_to(own[:, lanes : lanes + 128], (step, 128))
                    parts.append(jnp.where(place == target, fix, line[:, lanes : lanes + 128]))
                line = parts[0] if len(parts) == 1 else jnp.concatenate(parts, axis=1)
            lines.append(line)
        return lines[0] if count == 1 else jnp.concatenate(lines, axis=0)

    def chunks(polar_rows):
        return [(1, at.pole + polar_rows)]

    layers(at, chunks, moved, *scratch, w1, w2, wd, wc, wu)
    found = merge(at, 1, blocks, scratch[3], scratch[6], wm, wp)

    columns = 2 * half
    lane = lax.broadcasted_iota(jnp.int32, (8, columns), 1)
    first = lane < 2 * HALO
    edge = first | (lane >= columns - 2 * HALO)
    column = jnp.where(first, HALO + lax.div(lane, 2), 3 * HALO - lax.div(columns + 1 - lane, 2))
    column = jnp.where(edge, column, 0)
    odd = lax.rem(lane, 2) == 1
    per = columns // step
    for i in range(blocks):
        spread = column + (i % per) * step
        lanes = slice(i // per * columns, (i // per + 1) * columns)
        for p in range(2):
            evens = jnp.take_along_axis(found[p * 16 : p * 16 + 8, lanes], spread, axis=1)
            odds = jnp.take_along_axis(found[p * 16 + 8 : p * 16 + 16, lanes], spread, axis=1)
            h = 2 * i + p
            line = slice(h * 8, (h + 1) * 8)
            value = jnp.where(edge, jnp.where(odd, odds, evens), update[line, :])
            out[:, h, :] = value + rest[line, :]


def buffers(step, blocks):
    rows = Rows(step, blocks).count * step
    shapes = ((128, F32), (128, F32), (512, BF16), (512, BF16), (384, BF16), (256, BF16), (512, BF16))
    return [pltpu.VMEM((rows, lanes), dtype) for lanes, dtype in shapes]


def inside(cells, skip, weights):
    columns = skip.shape[1]
    blocks = skip.shape[0] // 16
    rows = Rows(columns // 2, blocks).count
    return pl.pallas_call(
        inside_kernel,
        out_shape=[jax.ShapeDtypeStruct((blocks * 16, columns), F32)] * 2
        + [jax.ShapeDtypeStruct((rows, lanes), F32) for _, lanes, _ in SHARED_KEYS],
        scratch_shapes=buffers(columns // 2, blocks),
        compiler_params=pltpu.CompilerParams(vmem_limit_bytes=20 * 2**20),
        cost_estimate=pl.CostEstimate(flops=4 * 10**9, bytes_accessed=4 * 10**6, transcendentals=0),
        name="inside",
    )(cells, skip, *weights)


def edges(out_shape, cells, inner, outer, weights, found):
    return pl.pallas_call(
        edges_kernel,
        out_shape=jax.ShapeDtypeStruct(out_shape, F32),
        scratch_shapes=buffers(4 * HALO, out_shape[1] // 2),
        compiler_params=pltpu.CompilerParams(vmem_limit_bytes=20 * 2**20),
        name="edges",
    )(cells, inner, outer, *weights, *found)


def shards(
    latlon_fields,
    remap_table,
    kernel_first,
    kernel_second,
    kernel_down,
    kernel_coarse,
    kernel_up,
    kernel_merge,
    projection,
):
    _, grid_rows, columns = remap_table.shape
    count = lax.axis_size("lon")
    parcels = pack(latlon_fields, remap_table, count)
    block = lax.all_to_all(parcels, "lon", split_axis=0, concat_axis=0, tiled=True)
    onehot, source, *weights = prepare(
        remap_table, kernel_first, kernel_second, kernel_down, kernel_coarse, kernel_up, kernel_merge, projection
    )
    cells, inner, outer, skip = remap(block, onehot, source)
    outer = swap(outer, "lon", 1)
    inner = swap(inner, "lon", 0)
    found = inside(cells, skip, weights)
    return edges((projection.shape[0], grid_rows, columns), cells, inner, outer, weights, found)


def solution(mesh):
    return jax.shard_map(
        shards,
        mesh=mesh,
        in_specs=(
            P("groups", "lon", None),
            P(None, None, "lon"),
            P(),
            P(),
            P(),
            P(),
            P(),
            P(),
            P(),
        ),
        out_specs=P("groups", None, "lon"),
        check_vma=False,
    )
```

```python
import jax
import jax.numpy as jnp
from jax import lax
from jax.experimental import pallas as pl
from jax.experimental.pallas import tpu as pltpu
from jax.sharding import PartitionSpec as P

F32 = jnp.float32
BF16 = jnp.bfloat16
HALO = 4
EDGE_GROUPS = [(1, 8), (9, 13)]
AHEAD = 2
POLAR = 3
PLACES = 16


def swap(block, axis, first):
    devices = lax.axis_size(axis)
    pairs = [((first + i) % devices, (first + i + 1) % devices) for i in range(0, devices, 2)]
    return lax.ppermute(block, axis, pairs + [(b, a) for a, b in pairs])


def pack_kernel(fields_hbm, table_hbm, parcels, fields, table, sems):
    channels, rows, _ = fields.shape
    devices, depth, columns = parcels.shape
    depth = rows * channels
    copies = [
        pltpu.make_async_copy(fields_hbm, fields, sems.at[0]),
        pltpu.make_async_copy(table_hbm, table, sems.at[1]),
    ]
    for copy in copies:
        copy.start()
    copies[1].wait()
    lines = [table[0, : 2 * POLAR, :], lax.rem(table[1, : 2 * POLAR, :], columns)]
    lines.append(jnp.zeros((PLACES - 4 * POLAR, columns), jnp.int32))
    lines = jnp.concatenate(lines, axis=0).astype(F32).astype(BF16)
    for target in range(devices):
        parcels[target, 2 * depth :, :] = lines
    copies[0].wait()
    values = fields[...].astype(F32)
    for row in range(rows):
        line = values[:, row, :].astype(BF16)
        for target in range(devices):
            piece = line[:, target * columns : (target + 1) * columns]
            opposite = (target + devices // 2) % devices
            parcels[target, row * channels : (row + 1) * channels, :] = piece
            parcels[opposite, depth + row * channels : depth + (row + 1) * channels, :] = piece


def pack(fields, table, devices):
    channels, rows, _ = fields.shape
    args = (fields, table)
    return pl.pallas_call(
        pack_kernel,
        in_specs=[pl.BlockSpec(memory_space=pltpu.HBM)] * 2,
        out_shape=jax.ShapeDtypeStruct((devices, 2 * rows * channels + PLACES, table.shape[2]), BF16),
        scratch_shapes=[pltpu.VMEM(a.shape, a.dtype) for a in args] + [pltpu.SemaphoreType.DMA((2,))],
        compiler_params=pltpu.CompilerParams(vmem_limit_bytes=16 * 2**20),
        name="pack",
    )(*[pltpu.with_memory_space_constraint(a, pltpu.HBM) for a in args])


def tap(kernel_ref, row, col):
    if 0 <= row < 3 and 0 <= col < 3:
        return kernel_ref[row, col].astype(F32)
    return jnp.zeros(kernel_ref.shape[2:], F32)


def arrange(first, second, down, coarse, up, merge, projection, w1, w2, wd, wc, wu, wm, wp):
    channels = second.shape[3]
    inputs = first.shape[2]
    for half in range(2):
        for side in range(2):
            for p in range(2):
                for q in range(2):
                    t = 1 + p if half == 0 else (3, 0)[p]
                    u = 1 + q if side == 0 else (3, 0)[q]
                    at = (((half * 2 + side) * 2 + p) * 2 + q) * inputs
                    pieces = [tap(first, t - a, u - b) for a in range(2) for b in range(2)]
                    w1[at : at + inputs, :] = jnp.concatenate(pieces, axis=1).astype(BF16)
    for t in range(4):
        for code in range(4):
            at = (t * 4 + code) * channels
            source = (0, 1, -2, -1)[code]
            for p in range(2):
                pair = [tap(second, t - p, source - target + 1) for target in (-1, 0)]
                w2[at : at + channels, p * 128 : (p + 1) * 128] = jnp.concatenate(pair, axis=0).T.astype(BF16)
            source = code - 1
            for p in range(2):
                pair = [tap(merge, t - p, source - target + 1) for target in (0, 1)]
                pair = jnp.concatenate(pair, axis=0).T.astype(BF16)
                wm[at : at + channels, p * 128 : (p + 1) * 128] = pair[:channels]
                wm[16 * channels + at : 16 * channels + at + channels, p * 128 : (p + 1) * 128] = pair[channels:]
            if t < 3:
                wd[at : at + channels, :] = tap(down, t, code).astype(BF16)
    wide = coarse.shape[3]
    for a in range(3):
        for b in range(3):
            at = (a * 3 + b) * wide
            wc[at : at + wide, :] = tap(coarse, a, b).T.astype(BF16)
    row_taps = ((1, 3), (0, 2))
    col_taps = ((0, 2), (3, 1))
    for di in range(2):
        for dj in range(2):
            at = (di * 2 + dj) * wide
            for p in range(2):
                pair = jnp.concatenate([tap(up, row_taps[p][di], col_taps[q][dj]) for q in range(2)], axis=0)
                wu[at : at + wide, p * 128 : (p + 1) * 128] = pair.T.astype(BF16)
    rows = projection[...].astype(F32)
    blank = jnp.zeros_like(rows)
    lines = [jnp.concatenate([rows if m == n else blank for m in range(4)], axis=1) for n in range(4)]
    wp[...] = jnp.concatenate(lines, axis=0).astype(BF16)


def locate(rows, cols, onehot, source):
    grid_rows, columns = rows.shape
    half = columns // 2
    code = rows * columns + cols
    lane = lax.broadcasted_iota(jnp.int32, (grid_rows, columns), 1)
    odd = [jnp.take_along_axis(code, lax.rem(lane, half) * 2 + q, axis=1) for q in range(2)]
    left = lax.broadcasted_iota(jnp.int32, (1, columns), 1) < half
    place = lax.broadcasted_iota(jnp.int32, (2 * columns, columns), 0)
    for pair in range(grid_rows // 4):
        for p in range(2):
            for q in range(2):
                n = p * 2 + q
                above, below = 4 * pair + p, 4 * pair + 2 + p
                line = jnp.where(left, odd[q][above : above + 1, :], odd[q][below : below + 1, :])
                source[4 * pair + n : 4 * pair + n + 1, :] = lax.div(line, 2 * columns)
                here = place == lax.rem(line, 2 * columns)
                onehot[pair * 2 * columns : (pair + 1) * 2 * columns, n * columns : (n + 1) * columns] = jnp.where(
                    here, 1.0, 0.0
                ).astype(BF16)


def prepare_kernel(*refs):
    args, outs, scratch, sems = refs[:8], refs[8:17], refs[17:25], refs[25]
    copies = [
        pltpu.make_async_copy(source, target, sems.at[n]) for n, (source, target) in enumerate(zip(args, scratch))
    ]
    for copy in copies:
        copy.start()
    copies[0].wait()
    table = scratch[0]
    locate(table[0], lax.rem(table[1], table.shape[2]), *outs[:2])
    for copy in copies[1:]:
        copy.wait()
    arrange(*scratch[1:], *outs[2:])


def prepare(table, first, second, down, coarse, up, merge, projection):
    channels, wide = second.shape[3], coarse.shape[3]
    columns = table.shape[2]
    pairs = table.shape[1] // 4
    shapes = (
        (16 * first.shape[3], 4 * channels),
        (16 * channels, 4 * channels),
        (12 * channels, wide),
        (9 * wide, wide),
        (4 * wide, 4 * channels),
        (32 * channels, 4 * channels),
        (4 * projection.shape[0], 4 * channels),
    )
    args = (table, jnp.swapaxes(first, 2, 3), second, jnp.swapaxes(down, 2, 3), coarse, up, merge, projection)
    return pl.pallas_call(
        prepare_kernel,
        in_specs=[pl.BlockSpec(memory_space=pltpu.HBM)] * 8,
        out_shape=[
            jax.ShapeDtypeStruct((pairs * 2 * columns, 4 * columns), BF16),
            jax.ShapeDtypeStruct((pairs * 4, columns), jnp.int32),
        ]
        + [jax.ShapeDtypeStruct(s, BF16) for s in shapes],
        scratch_shapes=[pltpu.VMEM(a.shape, a.dtype) for a in args] + [pltpu.SemaphoreType.DMA((8,))],
        compiler_params=pltpu.CompilerParams(vmem_limit_bytes=16 * 2**20),
        name="prepare",
    )(*[pltpu.with_memory_space_constraint(a, pltpu.HBM) for a in args])


def remap_kernel(block, onehot, source, cells, inner, outer, skip, polar_onehot, polar_source):
    even = lax.rem(lax.axis_index("lon"), 2) == 0
    devices, depth, columns = block.shape
    depth = (depth - PLACES) // 2
    channels = depth // 2
    opposite = lax.rem(lax.axis_index("lon") + devices // 2, devices)
    places = block[opposite, 2 * depth :, :].astype(F32).astype(jnp.int32)
    blank = jnp.zeros((polar_source.shape[0] - 2 * POLAR, columns), jnp.int32)
    rows = jnp.concatenate([places[: 2 * POLAR], blank], axis=0)
    cols = jnp.concatenate([places[2 * POLAR : 4 * POLAR], blank], axis=0)
    locate(rows, cols, polar_onehot, polar_source)
    half = columns // 2
    fields = []
    for side in range(2):
        at = side * depth
        upper = block[:, at : at + channels, :].reshape(devices * channels, columns)
        lower = block[:, at + channels : at + depth, :].reshape(devices * channels, columns)
        fields.append(jnp.concatenate([upper, lower], axis=1))
    pairs = cells.shape[0] // columns
    own_pairs = skip.shape[0] // 32
    for pair in range(pairs):
        own = pair < own_pairs
        at = pair if own else pair - own_pairs
        chosen = (onehot if own else polar_onehot)[at * 2 * columns : (at + 1) * 2 * columns, :]
        found = jnp.dot(fields[0 if own else 1], chosen, preferred_element_type=F32)
        lines = []
        for n in range(4):
            line = (source if own else polar_source)[4 * at + n : 4 * at + n + 1, :]
            line = jnp.broadcast_to(line, (channels, columns))
            total = jnp.zeros((channels, columns), F32)
            for s in range(devices):
                value = found[s * channels : (s + 1) * channels, n * columns : (n + 1) * columns]
                total = jnp.where(line == s, value, total)
            lines.append(total)
            if own:
                skip[(pair * 4 + n) * 8 : (pair * 4 + n + 1) * 8, :] = total[:8]
        turned = jnp.concatenate(lines + lines, axis=0).T
        cells[pair * columns : (pair + 1) * columns, :] = turned.astype(BF16)
        for i in range(2):
            row = (pair * 2 + i) * HALO
            begin = turned[i * half : i * half + HALO]
            finish = turned[(i + 1) * half - HALO : (i + 1) * half]
            inner[row : row + HALO, :] = jnp.where(even, finish, begin)
            outer[row : row + HALO, :] = jnp.where(even, begin, finish)


def remap(block, onehot, source):
    columns = block.shape[2]
    own_rows = source.shape[0]
    polar_rows = 4 * ((POLAR + 1) // 2)
    count = (own_rows + polar_rows) // 4
    return pl.pallas_call(
        remap_kernel,
        out_shape=[
            jax.ShapeDtypeStruct((count * columns, columns), BF16),
            jax.ShapeDtypeStruct((count * 2 * HALO, columns), F32),
            jax.ShapeDtypeStruct((count * 2 * HALO, columns), F32),
            jax.ShapeDtypeStruct((own_rows * 8, columns), F32),
        ],
        scratch_shapes=[
            pltpu.VMEM((polar_rows // 4 * 2 * columns, 4 * columns), BF16),
            pltpu.VMEM((polar_rows, columns), jnp.int32),
        ],
        compiler_params=pltpu.CompilerParams(vmem_limit_bytes=16 * 2**20),
        name="remap",
    )(block, onehot, source)


def silu(values):
    h = 0.5 * values
    return (h + h * jnp.tanh(h)).astype(BF16).astype(F32)


def ring(values, step, shift):
    rows = [pltpu.roll(values[at : at + step], shift % step, 0) for at in range(0, values.shape[0], step)]
    return rows[0] if len(rows) == 1 else jnp.concatenate(rows, axis=0)


class Rows:
    def __init__(self, step, blocks):
        self.step, self.blocks = step, blocks
        self.top, self.bottom, self.pole = 0, blocks + 1, blocks + 2
        self.count = blocks + 2 + POLAR + 2

    def __call__(self, row, count=1):
        return slice(row * self.step, (row + count) * self.step)

    def of(self, i):
        return 1 + i if i < self.blocks else self.pole + 1 + i - self.blocks

    def mask(self, count, width):
        lane = lax.broadcasted_iota(jnp.int32, (count * self.step, 128), 1)
        return lax.rem(lax.div(lane, width), 2) == 0


def product(pieces, weights):
    return jnp.dot(jnp.concatenate(pieces, axis=1), weights[...], preferred_element_type=F32)


def layers(at, groups, moved, x0, y0, y1, y2, yc, yo, yu, w1, w2, wd, wc, wu):
    step, top, bottom, pole = at.step, at.top, at.bottom, at.pole
    x0[at(top), :] = pltpu.roll(x0[at(pole + 1), :], 32, 1)
    x0[at(pole), :] = pltpu.roll(x0[at(1), :], 32, 1)
    for row in range(at.count):
        x = x0[at(row), :]
        side = jnp.where(at.mask(1, 16), moved("x0", row, 1, x, -1), moved("x0", row, 1, x, 1))
        y0[at(row), :] = jnp.where(at.mask(1, 64), x, side)
    for y, polar_rows in ((y1, POLAR), (y2, POLAR - 1), (yc, POLAR - 1), (yo, POLAR - 2), (yu, POLAR - 2)):
        for row in (bottom, pole + 1 + polar_rows):
            y[at(row), :] = jnp.zeros((step, y.shape[1]), BF16)

    def layer(name, polar_rows, inputs, weights, store, edge, clear):
        def task(row, count):
            def finish(found):
                store(name, row, count, silu(found))
                if row < bottom < row + count:
                    clear()
                if row <= pole + 1 < row + count:
                    edge(top, pole + 1)
                if row == 1 or row < pole < row + count:
                    edge(pole, 1)

            return lambda: product(inputs(row, count), weights), finish

        return [task(row, polar_rows if row == pole + 1 else count) for row, count in groups]

    def fine(y, shift):
        def store(name, row, count, values):
            shifted = moved(name, row, count, values, shift).astype(BF16)
            values = values.astype(BF16)
            for p in range(2):
                lanes = slice(p * 128, (p + 1) * 128)
                y[at(row, count), p * 256 : p * 256 + 128] = values[:, lanes]
                y[at(row, count), p * 256 + 128 : p * 256 + 256] = shifted[:, lanes]

        def edge(target, source):
            y[at(target), 256:512] = y[at(source), 0:256]

        def clear():
            y[at(bottom), 0:256] = jnp.zeros((step, 256), BF16)

        return store, edge, clear

    def first_inputs(row, count):
        vertical = jnp.where(at.mask(count, 32), y0[at(row + 1, count), :], y0[at(row - 1, count), :])
        return [y0[at(row, count), :].astype(BF16), vertical.astype(BF16)]

    def second_inputs(row, count):
        return [y1[at(row - 1, count), 256:512], y1[at(row, count), :], y1[at(row + 1, count), 0:256]]

    def down_inputs(row, count):
        return [y2[at(row - 1, count), 256:512], y2[at(row, count), :]]

    def coarse_inputs(row, count):
        return [yc[at(row + a, count), :] for a in (-1, 0, 1)]

    def up_inputs(row, count):
        return [yo[at(row, count), :], yo[at(row + 1, count), :]]

    def store_coarse_in(name, row, count, values):
        yc[at(row, count), 0:128] = moved(name, row, count, values, 1).astype(BF16)
        yc[at(row, count), 128:256] = values.astype(BF16)
        yc[at(row, count), 256:384] = moved(name, row, count, values, -1).astype(BF16)

    def edge_coarse_in(target, source):
        yc[at(target), :] = yc[at(source), :]

    def clear_coarse_in():
        yc[at(bottom), :] = jnp.zeros((step, 384), BF16)

    def clear_coarse_out():
        yo[at(bottom), :] = jnp.zeros((step, 256), BF16)

    def store_coarse_out(name, row, count, values):
        yo[at(row, count), 0:128] = moved(name, row, count, values, 1).astype(BF16)
        yo[at(row, count), 128:256] = values.astype(BF16)

    return [
        layer("y1", POLAR, first_inputs, w1, *fine(y1, 1)),
        layer("y2", POLAR - 1, second_inputs, w2, *fine(y2, -1)),
        layer("yc", POLAR - 1, down_inputs, wd, store_coarse_in, edge_coarse_in, clear_coarse_in),
        layer("yo", POLAR - 2, coarse_inputs, wc, store_coarse_out, lambda target, source: None, clear_coarse_out),
        layer("yu", POLAR - 2, up_inputs, wu, *fine(yu, -1)),
    ]


def run(tasks, ahead):
    found = {}
    for n in range(len(tasks) + ahead):
        if n < len(tasks):
            found[n] = tasks[n][0]()
        if n >= ahead:
            tasks[n - ahead][1](found.pop(n - ahead))


def merge(at, row, count, y2, yu, wm):
    pieces = []
    for y in (y2, yu):
        pieces += [y[at(row - 1, count), 256:512], y[at(row, count), :], y[at(row + 1, count), 0:256]]
    return product(pieces, wm)


def project(found, wp):
    merged = silu(found).astype(BF16)
    return lax.dot_general(wp[...], merged, (((1,), (1,)), ((), ())), preferred_element_type=F32)


SHARED = (("y1", 256, (1,)), ("y2", 256, (-1,)), ("yc", 128, (1, -1)), ("yo", 128, (1,)), ("yu", 256, (-1,)))
SHARED_KEYS = [(name, lanes, shift) for name, lanes, shifts in SHARED for shift in shifts]


def inside_kernel(cells, skip, w1, w2, wd, wc, wu, wm, wp, update, rest, *refs):
    shared, scratch = refs[: len(SHARED_KEYS)], refs[len(SHARED_KEYS) :]
    half = update.shape[1] // 2
    blocks = update.shape[0] // 16
    at = Rows(half, blocks)
    group = 4

    groups = [(1 + i, group) for i in range(0, blocks, group)]
    polar = [(at.pole + 1, POLAR)]

    def moved(name, row, count, values, shift):
        for (key, _, way), ref in zip(SHARED_KEYS, shared):
            if key == name and way == shift:
                column = half - HALO - 1 if shift == 1 else HALO
                for i in range(count):
                    ref[row + i : row + i + 1, :] = values[i * half + column : i * half + column + 1, :]
        return ring(values, half, shift)

    x0 = scratch[0]
    for row in (at.top, at.bottom, at.pole, at.count - 1):
        x0[at(row), :] = jnp.zeros((half, 128), F32)
    for i in range(blocks + POLAR):
        x0[at(at.of(i)), :] = cells[i * half : (i + 1) * half, :].astype(F32)
    tasks = sum(layers(at, polar + groups, moved, *scratch, w1, w2, wd, wc, wu), [])

    y2, yu = scratch[3], scratch[6]
    lane = lax.broadcasted_iota(jnp.int32, (8, 2 * half), 1)
    even = lax.rem(lane, 2) == 0

    def weave(values, i, p):
        spread = lax.div(lane, 2) + i * half
        evens = jnp.take_along_axis(values[p * 16 : p * 16 + 8], spread, axis=1)
        odds = jnp.take_along_axis(values[p * 16 + 8 : p * 16 + 16], spread, axis=1)
        return jnp.where(even, evens, odds)

    def last(row, count):
        def finish(found):
            found = project(found, wp)
            for n in range(count // 2):
                pair = (row - 1) // 2 + n
                own = found[:, n * 2 * half : (n + 1) * 2 * half]
                base = skip[pair * 32 : (pair + 1) * 32, :]
                for i in range(2):
                    for p in range(2):
                        line = (4 * pair + 2 * i + p) * 8
                        update[line : line + 8, :] = weave(own, i, p)
                        rest[line : line + 8, :] = weave(base, i, p)

        return lambda: merge(at, row, count, y2, yu, wm), finish

    run(tasks + [last(row, count) for row, count in groups], AHEAD)


def edges_kernel(cells, inner, outer, w1, w2, wd, wc, wu, wm, wp, update, rest, *refs):
    shared, out, scratch = refs[: len(SHARED_KEYS)], refs[len(SHARED_KEYS)], refs[len(SHARED_KEYS) + 1 :]
    even = lax.rem(lax.axis_index("lon"), 2) == 0
    half = out.shape[2] // 2
    blocks = out.shape[1] // 2
    step = 4 * HALO
    at = Rows(step, blocks)
    place = lax.broadcasted_iota(jnp.int32, (step, 128), 0)
    x0 = scratch[0]
    beside = {}
    for row in (at.top, at.bottom, at.pole, at.count - 1):
        x0[at(row), :] = jnp.zeros((step, 128), F32)
    for i in range(blocks + POLAR):
        row = at.of(i)
        begin = cells[i * half : i * half + 16, :].astype(F32)
        finish = cells[(i + 1) * half - 16 : (i + 1) * half, :].astype(F32)
        near = inner[i * HALO : (i + 1) * HALO, :]
        far = outer[i * HALO : (i + 1) * HALO, :]
        base = row * step
        x0[base : base + HALO, :] = jnp.where(even, far, near)
        x0[base + HALO : base + 2 * HALO, :] = begin[:HALO]
        x0[base + 2 * HALO : base + 3 * HALO, :] = finish[16 - HALO :]
        x0[base + 3 * HALO : base + 4 * HALO, :] = jnp.where(even, near, far)
        beside[row] = {-1: begin[HALO : HALO + 1], 1: finish[15 - HALO : 16 - HALO]}
    beside[at.top] = {way: pltpu.roll(line, 32, 1) for way, line in beside[at.pole + 1].items()}
    beside[at.pole] = {way: pltpu.roll(line, 32, 1) for way, line in beside[1].items()}

    def moved(name, row, count, values, shift):
        lines = []
        target = 2 * HALO if shift == 1 else 2 * HALO - 1
        for i in range(count):
            line = pltpu.roll(values[i * step : (i + 1) * step], shift % step, 0)
            if name == "x0":
                own = beside[row + i][shift] if row + i in beside else None
            else:
                ref = next(r for (key, _, way), r in zip(SHARED_KEYS, shared) if (key, way) == (name, shift))
                own = ref[row + i : row + i + 1, :]
            if own is not None:
                parts = []
                for lanes in range(0, values.shape[1], 128):
                    fix = jnp.broadcast_to(own[:, lanes : lanes + 128], (step, 128))
                    parts.append(jnp.where(place == target, fix, line[:, lanes : lanes + 128]))
                line = parts[0] if len(parts) == 1 else jnp.concatenate(parts, axis=1)
            lines.append(line)
        return lines[0] if count == 1 else jnp.concatenate(lines, axis=0)

    for tasks in layers(at, EDGE_GROUPS, moved, *scratch, w1, w2, wd, wc, wu):
        run(tasks, 1)
    parts = []
    run([(lambda row=row: merge(at, row, 8, scratch[3], scratch[6], wm), lambda v: parts.append(project(v, wp))) for row in (1, 9)], 1)
    found = jnp.concatenate(parts, axis=1)

    columns = 2 * half
    lane = lax.broadcasted_iota(jnp.int32, (8, columns), 1)
    first = lane < 2 * HALO
    edge = first | (lane >= columns - 2 * HALO)
    column = jnp.where(first, HALO + lax.div(lane, 2), 3 * HALO - lax.div(columns + 1 - lane, 2))
    column = jnp.where(edge, column, 0)
    odd = lax.rem(lane, 2) == 1
    per = columns // step
    for i in range(blocks):
        spread = column + (i % per) * step
        lanes = slice(i // per * columns, (i // per + 1) * columns)
        for p in range(2):
            evens = jnp.take_along_axis(found[p * 16 : p * 16 + 8, lanes], spread, axis=1)
            odds = jnp.take_along_axis(found[p * 16 + 8 : p * 16 + 16, lanes], spread, axis=1)
            h = 2 * i + p
            line = slice(h * 8, (h + 1) * 8)
            value = jnp.where(edge, jnp.where(odd, odds, evens), update[line, :])
            out[:, h, :] = value + rest[line, :]


def buffers(step, blocks):
    rows = Rows(step, blocks).count * step
    shapes = ((128, F32), (128, F32), (512, BF16), (512, BF16), (384, BF16), (256, BF16), (512, BF16))
    return [pltpu.VMEM((rows, lanes), dtype) for lanes, dtype in shapes]


def inside(cells, skip, weights):
    columns = skip.shape[1]
    blocks = skip.shape[0] // 16
    rows = Rows(columns // 2, blocks).count
    return pl.pallas_call(
        inside_kernel,
        out_shape=[jax.ShapeDtypeStruct((blocks * 16, columns), F32)] * 2
        + [jax.ShapeDtypeStruct((rows, lanes), F32) for _, lanes, _ in SHARED_KEYS],
        scratch_shapes=buffers(columns // 2, blocks),
        compiler_params=pltpu.CompilerParams(vmem_limit_bytes=20 * 2**20),
        cost_estimate=pl.CostEstimate(flops=4 * 10**9, bytes_accessed=4 * 10**6, transcendentals=0),
        name="inside",
    )(cells, skip, *weights)


def edges(out_shape, cells, inner, outer, weights, found):
    return pl.pallas_call(
        edges_kernel,
        out_shape=jax.ShapeDtypeStruct(out_shape, F32),
        scratch_shapes=buffers(4 * HALO, out_shape[1] // 2),
        compiler_params=pltpu.CompilerParams(vmem_limit_bytes=20 * 2**20),
        name="edges",
    )(cells, inner, outer, *weights, *found)


def shards(
    latlon_fields,
    remap_table,
    kernel_first,
    kernel_second,
    kernel_down,
    kernel_coarse,
    kernel_up,
    kernel_merge,
    projection,
):
    _, grid_rows, columns = remap_table.shape
    count = lax.axis_size("lon")
    parcels = pack(latlon_fields, remap_table, count)
    block = lax.all_to_all(parcels, "lon", split_axis=0, concat_axis=0, tiled=True)
    onehot, source, *weights = prepare(
        remap_table, kernel_first, kernel_second, kernel_down, kernel_coarse, kernel_up, kernel_merge, projection
    )
    cells, inner, outer, skip = remap(block, onehot, source)
    outer = swap(outer, "lon", 1)
    inner = swap(inner, "lon", 0)
    found = inside(cells, skip, weights)
    return edges((projection.shape[0], grid_rows, columns), cells, inner, outer, weights, found)


def solution(mesh):
    return jax.shard_map(
        shards,
        mesh=mesh,
        in_specs=(
            P("groups", "lon", None),
            P(None, None, "lon"),
            P(),
            P(),
            P(),
            P(),
            P(),
            P(),
            P(),
        ),
        out_specs=P("groups", None, "lon"),
        check_vma=False,
    )
```

```python
import jax
import jax.numpy as jnp
from jax import lax
from jax.experimental import pallas as pl
from jax.experimental.pallas import tpu as pltpu
from jax.sharding import PartitionSpec as P

F32 = jnp.float32
BF16 = jnp.bfloat16
HALO = 4
EDGE_ROWS = 9
AHEAD = 2
POLAR = 3
PARTS = 4


def swap(block, axis, first):
    devices = lax.axis_size(axis)
    pairs = [((first + i) % devices, (first + i + 1) % devices) for i in range(0, devices, 2)]
    return lax.ppermute(block, axis, pairs + [(b, a) for a, b in pairs])


def opposite(block, axis):
    devices = lax.axis_size(axis)
    return lax.ppermute(block, axis, [(i, (i + devices // 2) % devices) for i in range(devices)])


def pack_kernel(fields_hbm, parcels_hbm, fields, parcels, in_sems, out_sems):
    channels, rows, _ = fields.shape
    devices, depth, columns = parcels.shape
    depth = rows * channels
    parts = in_sems.shape[0]
    span = devices // parts

    def lanes(n):
        return slice(n * span * columns, (n + 1) * span * columns)

    loads = [
        pltpu.make_async_copy(fields_hbm.at[:, :, lanes(n)], fields.at[:, :, lanes(n)], in_sems.at[n])
        for n in range(parts)
    ]
    for load in loads:
        load.start()
    stores = []

    def send(targets, part):
        at = parcels.at[targets, part, :], parcels_hbm.at[targets, part, :]
        stores.append(pltpu.make_async_copy(*at, out_sems.at[len(stores)]))
        stores[-1].start()

    for n in range(parts):
        loads[n].wait()
        values = fields[:, :, lanes(n)].astype(F32)
        first, other = n * span, (n * span + devices // 2) % devices
        for row in range(rows):
            line = values[:, row, :].astype(BF16)
            for m in range(span):
                piece = line[:, m * columns : (m + 1) * columns]
                parcels[first + m, row * channels : (row + 1) * channels, :] = piece
                parcels[other + m, depth + row * channels : depth + (row + 1) * channels, :] = piece
        send(slice(first, first + span), slice(0, depth))
        send(slice(other, other + span), slice(depth, 2 * depth))
    for store in stores:
        store.wait()


def pack(fields, devices, columns):
    channels, rows, _ = fields.shape
    shape = (devices, 2 * rows * channels, columns)
    return pl.pallas_call(
        pack_kernel,
        in_specs=[pl.BlockSpec(memory_space=pltpu.HBM)],
        out_specs=pl.BlockSpec(memory_space=pltpu.HBM),
        out_shape=pltpu.HBM(shape, BF16),
        scratch_shapes=[
            pltpu.VMEM(fields.shape, BF16),
            pltpu.VMEM(shape, BF16),
            pltpu.SemaphoreType.DMA((PARTS,)),
            pltpu.SemaphoreType.DMA((2 * PARTS,)),
        ],
        compiler_params=pltpu.CompilerParams(vmem_limit_bytes=16 * 2**20),
        name="pack",
    )(pltpu.with_memory_space_constraint(fields, pltpu.HBM))


def tap(kernel_ref, row, col):
    if 0 <= row < 3 and 0 <= col < 3:
        return kernel_ref[row, col].astype(F32)
    return jnp.zeros(kernel_ref.shape[2:], F32)


def arrange(first, second, down, coarse, up, merge, projection, w1, w2, wd, wc, wu, wm, wp):
    channels = second.shape[3]
    inputs = first.shape[2]
    for half in range(2):
        for side in range(2):
            for p in range(2):
                for q in range(2):
                    t = 1 + p if half == 0 else (3, 0)[p]
                    u = 1 + q if side == 0 else (3, 0)[q]
                    at = (((half * 2 + side) * 2 + p) * 2 + q) * inputs
                    pieces = [tap(first, t - a, u - b) for a in range(2) for b in range(2)]
                    w1[at : at + inputs, :] = jnp.concatenate(pieces, axis=1).astype(BF16)
    for t in range(4):
        for code in range(4):
            at = (t * 4 + code) * channels
            source = (0, 1, -2, -1)[code]
            for p in range(2):
                pair = [tap(second, t - p, source - target + 1) for target in (-1, 0)]
                w2[at : at + channels, p * 128 : (p + 1) * 128] = jnp.concatenate(pair, axis=0).T.astype(BF16)
            source = code - 1
            for p in range(2):
                pair = [tap(merge, t - p, source - target + 1) for target in (0, 1)]
                pair = jnp.concatenate(pair, axis=0).T.astype(BF16)
                wm[at : at + channels, p * 128 : (p + 1) * 128] = pair[:channels]
                wm[16 * channels + at : 16 * channels + at + channels, p * 128 : (p + 1) * 128] = pair[channels:]
            if t < 3:
                wd[at : at + channels, :] = tap(down, t, code).astype(BF16)
    wide = coarse.shape[3]
    for a in range(3):
        for b in range(3):
            at = (a * 3 + b) * wide
            wc[at : at + wide, :] = tap(coarse, a, b).T.astype(BF16)
    row_taps = ((1, 3), (0, 2))
    col_taps = ((0, 2), (3, 1))
    for di in range(2):
        for dj in range(2):
            at = (di * 2 + dj) * wide
            for p in range(2):
                pair = jnp.concatenate([tap(up, row_taps[p][di], col_taps[q][dj]) for q in range(2)], axis=0)
                wu[at : at + wide, p * 128 : (p + 1) * 128] = pair.T.astype(BF16)
    rows = projection[...].astype(F32)
    blank = jnp.zeros_like(rows)
    lines = [jnp.concatenate([rows if m == n else blank for m in range(4)], axis=1) for n in range(4)]
    wp[...] = jnp.concatenate(lines, axis=0).astype(BF16)


def locate(rows, cols):
    grid_rows, columns = rows.shape
    half = columns // 2
    code = rows * columns + cols
    lane = lax.broadcasted_iota(jnp.int32, (grid_rows, columns), 1)
    odd = [jnp.take_along_axis(code, lax.rem(lane, half) * 2 + q, axis=1) for q in range(2)]
    left = lax.broadcasted_iota(jnp.int32, (1, columns), 1) < half
    lines = []
    for pair in range(grid_rows // 4):
        for p in range(2):
            for q in range(2):
                above, below = 4 * pair + p, 4 * pair + 2 + p
                lines.append(jnp.where(left, odd[q][above : above + 1, :], odd[q][below : below + 1, :]))
    return jnp.concatenate(lines, axis=0)


def prepare_kernel(*refs):
    args, (places, *weights), scratch, sems = refs[:8], refs[8:16], refs[16:24], refs[24]
    copies = [
        pltpu.make_async_copy(source, target, sems.at[n]) for n, (source, target) in enumerate(zip(args, scratch))
    ]
    for copy in copies:
        copy.start()
    copies[0].wait()
    table = scratch[0]
    places[...] = locate(table[0], lax.rem(table[1], table.shape[2]))
    for copy in copies[1:]:
        copy.wait()
    arrange(*scratch[1:], *weights)


def prepare(table, first, second, down, coarse, up, merge, projection):
    channels, wide = second.shape[3], coarse.shape[3]
    columns = table.shape[2]
    shapes = (
        (16 * first.shape[3], 4 * channels),
        (16 * channels, 4 * channels),
        (12 * channels, wide),
        (9 * wide, wide),
        (4 * wide, 4 * channels),
        (32 * channels, 4 * channels),
        (4 * projection.shape[0], 4 * channels),
    )
    args = (table, jnp.swapaxes(first, 2, 3), second, jnp.swapaxes(down, 2, 3), coarse, up, merge, projection)
    return pl.pallas_call(
        prepare_kernel,
        in_specs=[pl.BlockSpec(memory_space=pltpu.HBM)] * 8,
        out_shape=[jax.ShapeDtypeStruct(table.shape[1:], jnp.int32)] + [jax.ShapeDtypeStruct(s, BF16) for s in shapes],
        scratch_shapes=[pltpu.VMEM(a.shape, a.dtype) for a in args] + [pltpu.SemaphoreType.DMA((8,))],
        compiler_params=pltpu.CompilerParams(vmem_limit_bytes=16 * 2**20),
        name="prepare",
    )(*[pltpu.with_memory_space_constraint(a, pltpu.HBM) for a in args])


def remap_kernel(block, places, polar, cells, inner, outer, skip):
    even = lax.rem(lax.axis_index("lon"), 2) == 0
    devices, depth, columns = block.shape
    depth = depth // 2
    channels = depth // 2
    lines = [places[...], locate(polar[0], lax.rem(polar[1], columns))]
    lines = jnp.concatenate(lines, axis=0)
    sources = lax.div(lines, 2 * columns)
    offsets = lax.rem(lines, 2 * columns).astype(F32)
    line_at = lax.broadcasted_iota(jnp.int32, (2 * columns, columns), 0).astype(F32)
    half = columns // 2
    fields = []
    for side in range(2):
        at = side * depth
        upper = block[:, at : at + channels, :].reshape(devices * channels, columns)
        lower = block[:, at + channels : at + depth, :].reshape(devices * channels, columns)
        fields.append(jnp.concatenate([upper, lower], axis=1))
    pairs = cells.shape[0] // columns
    begins, finishes = [], []
    own_pairs = skip.shape[0] // 32
    for pair in range(pairs):
        own = pair < own_pairs
        chosen = []
        for n in range(4):
            here = line_at == jnp.broadcast_to(offsets[4 * pair + n : 4 * pair + n + 1, :], line_at.shape)
            chosen.append(jnp.where(here, 1.0, 0.0).astype(BF16))
        found = jnp.dot(fields[0 if own else 1], jnp.concatenate(chosen, axis=1), preferred_element_type=F32)
        lines = []
        for n in range(4):
            line = sources[4 * pair + n : 4 * pair + n + 1, :]
            line = jnp.broadcast_to(line, (channels, columns))
            total = jnp.zeros((channels, columns), F32)
            for s in range(devices):
                value = found[s * channels : (s + 1) * channels, n * columns : (n + 1) * columns]
                total = jnp.where(line == s, value, total)
            lines.append(total)
            if own:
                skip[(pair * 4 + n) * 8 : (pair * 4 + n + 1) * 8, :] = total[:8]
        turned = jnp.concatenate(lines + lines, axis=0).T
        cells[pair * columns : (pair + 1) * columns, :] = turned.astype(BF16)
        for i in range(2):
            begins.append(turned[i * half : i * half + HALO])
            finishes.append(turned[(i + 1) * half - HALO : (i + 1) * half])
    begins, finishes = jnp.concatenate(begins, axis=0), jnp.concatenate(finishes, axis=0)
    inner[...] = jnp.where(even, finishes, begins).astype(BF16)
    outer[...] = jnp.where(even, begins, finishes).astype(BF16)


def remap(block, places, polar):
    columns = block.shape[2]
    grid_rows = places.shape[0]
    count = (grid_rows + polar.shape[1]) // 4
    return pl.pallas_call(
        remap_kernel,
        out_shape=[
            jax.ShapeDtypeStruct((count * columns, columns), BF16),
            jax.ShapeDtypeStruct((count * 2 * HALO, columns), BF16),
            jax.ShapeDtypeStruct((count * 2 * HALO, columns), BF16),
            jax.ShapeDtypeStruct((grid_rows * 8, columns), F32),
        ],
        compiler_params=pltpu.CompilerParams(vmem_limit_bytes=16 * 2**20),
        name="remap",
    )(block, places, polar)


def silu(values):
    h = 0.5 * values
    return (h + h * jnp.tanh(h)).astype(BF16).astype(F32)


def ring(values, step, shift):
    rows = [pltpu.roll(values[at : at + step], shift % step, 0) for at in range(0, values.shape[0], step)]
    return rows[0] if len(rows) == 1 else jnp.concatenate(rows, axis=0)


class Rows:
    def __init__(self, step, blocks):
        self.step, self.blocks = step, blocks
        self.top, self.bottom, self.pole = 0, blocks + 1, blocks + 2
        self.count = blocks + 2 + POLAR + 2

    def __call__(self, row, count=1):
        return slice(row * self.step, (row + count) * self.step)

    def of(self, i):
        return 1 + i if i < self.blocks else self.pole + 1 + i - self.blocks

    def mask(self, count, width):
        lane = lax.broadcasted_iota(jnp.int32, (count * self.step, 128), 1)
        return lax.rem(lax.div(lane, width), 2) == 0


def product(pieces, weights):
    values = pieces[0] if len(pieces) == 1 else jnp.concatenate(pieces, axis=0)
    return jnp.dot(values, weights[...], preferred_element_type=F32)


def layers(at, groups, pairs, moved, x0, y0, y1, y2, yc, yo, yu, w1, w2, wd, wc, wu):
    step, top, bottom, pole = at.step, at.top, at.bottom, at.pole
    x0[at(top), :] = pltpu.roll(x0[at(pole + 1), :], 32, 1)
    x0[at(pole), :] = pltpu.roll(x0[at(1), :], 32, 1)
    ready = set()

    def widen(row):
        if row not in ready:
            ready.add(row)
            x = x0[at(row), :]
            side = jnp.where(at.mask(1, 16), moved("x0", row, 1, x, -1), moved("x0", row, 1, x, 1))
            y0[at(row), :] = jnp.where(at.mask(1, 64), x, side)

    for y, polar_rows in ((y1, POLAR), (y2, POLAR - 1), (yc, POLAR - 1), (yo, POLAR - 2), (yu, POLAR - 2)):
        for row in (bottom, pole + 1 + polar_rows):
            y[at(row), :] = jnp.zeros((step, y.shape[1]), BF16)

    def layer(name, polar_rows, inputs, weights, store, edge, paired=False):
        def task(ranges):
            ranges = [(row, polar_rows if row == pole + 1 else count) for row, count in ranges]

            def begin():
                pieces = [jnp.concatenate(inputs(row, count), axis=1) for row, count in ranges]
                return product(pieces, weights)

            def finish(found):
                found = silu(found)
                start = 0
                for row, count in ranges:
                    if paired:
                        lanes = found.shape[1] // 2
                        rows = []
                        for n in range(count):
                            line = slice(start + n // 2 * step, start + (n // 2 + 1) * step)
                            rows.append(found[line, n % 2 * lanes : (n % 2 + 1) * lanes])
                        values = rows[0] if count == 1 else jnp.concatenate(rows, axis=0)
                        start += (count + 1) // 2 * step
                    else:
                        values = found[start : start + count * step]
                        start += count * step
                    store(name, row, count, values)
                    if row == pole + 1:
                        edge(top, pole + 1)
                    if row == 1:
                        edge(pole, 1)

            return begin, finish, ranges

        return [task(ranges) for ranges in (pairs if paired else groups)]

    def fine(y, shift):
        def store(name, row, count, values):
            shifted = moved(name, row, count, values, shift).astype(BF16)
            values = values.astype(BF16)
            for p in range(2):
                lanes = slice(p * 128, (p + 1) * 128)
                y[at(row, count), p * 256 : p * 256 + 128] = values[:, lanes]
                y[at(row, count), p * 256 + 128 : p * 256 + 256] = shifted[:, lanes]

        def edge(target, source):
            y[at(target), 256:512] = y[at(source), 0:256]

        return store, edge

    def first_inputs(row, count):
        for n in range(row - 1, row + count + 1):
            widen(n)
        vertical = jnp.where(at.mask(count, 32), y0[at(row + 1, count), :], y0[at(row - 1, count), :])
        return [y0[at(row, count), :].astype(BF16), vertical.astype(BF16)]

    def second_inputs(row, count):
        return [y1[at(row - 1, count), 256:512], y1[at(row, count), :], y1[at(row + 1, count), 0:256]]

    def down_inputs(row, count):
        return [y2[at(row - 1, count), 256:512], y2[at(row, count), :]]

    def coarse_inputs(row, count):
        return [yc[at(row + a, count), :] for a in (-1, 0, 1)]

    def up_inputs(row, count):
        return [yo[at(row, count), :], yo[at(row + 1, count), :]]

    def store_coarse_in(name, row, count, values):
        yc[at(row, count), 0:128] = moved(name, row, count, values, 1).astype(BF16)
        yc[at(row, count), 128:256] = values.astype(BF16)
        yc[at(row, count), 256:384] = moved(name, row, count, values, -1).astype(BF16)

    def edge_coarse_in(target, source):
        yc[at(target), :] = yc[at(source), :]

    def store_coarse_out(name, row, count, values):
        yo[at(row, count), 0:128] = moved(name, row, count, values, 1).astype(BF16)
        yo[at(row, count), 128:256] = values.astype(BF16)

    return [
        layer("y1", POLAR, first_inputs, w1, *fine(y1, 1)),
        layer("y2", POLAR - 1, second_inputs, w2, *fine(y2, -1)),
        layer("yc", POLAR - 1, down_inputs, wd, store_coarse_in, edge_coarse_in),
        layer("yo", POLAR - 2, coarse_inputs, wc, store_coarse_out, lambda target, source: None),
        layer("yu", POLAR - 2, up_inputs, wu, *fine(yu, -1)),
    ]


def run(at, stages, ahead):
    tasks, owner = [], {}
    for stage in stages:
        rows = {}
        for begin, finish, ranges in stage:
            reads = set()
            for row, count in ranges:
                reads.update(range(row - 1, row + count + 2))
            reads.update({at.pole + 1} if at.top in reads else (), {1} if at.pole in reads else ())
            tasks.append((begin, finish, {owner[row] for row in reads if row in owner}))
            for row, count in ranges:
                rows.update({n: len(tasks) - 1 for n in range(row, row + count)})
        owner = rows
    found, issued = {}, 0
    for turn in range(len(tasks)):
        while issued < len(tasks) and issued <= turn + ahead and all(n < turn for n in tasks[issued][2]):
            found[issued] = tasks[issued][0]()
            issued += 1
        tasks[turn][1](found.pop(turn))


def merge(at, row, count, y2, yu, wm):
    pieces = []
    for y in (y2, yu):
        pieces += [y[at(row - 1, count), 256:512], y[at(row, count), :], y[at(row + 1, count), 0:256]]
    return product([jnp.concatenate(pieces, axis=1)], wm)


def project(found, wp):
    merged = silu(found).astype(BF16)
    return lax.dot_general(wp[...], merged, (((1,), (1,)), ((), ())), preferred_element_type=F32)


SHARED = (("y1", 256, (1,)), ("y2", 256, (-1,)), ("yc", 128, (1, -1)), ("yo", 128, (1,)), ("yu", 256, (-1,)))
SHARED_KEYS = [(name, lanes, shift) for name, lanes, shifts in SHARED for shift in shifts]


def inside_kernel(cells, skip, w1, w2, wd, wc, wu, wm, wp, update, *refs):
    shared, scratch = refs[: len(SHARED_KEYS)], refs[len(SHARED_KEYS) :]
    half = update.shape[1] // 2
    blocks = update.shape[0] // 16
    at = Rows(half, blocks)
    group = 4

    groups = [[(1 + i, group)] for i in range(0, blocks, group)]
    pairs = [[(1 + i, 2 * group)] for i in range(0, blocks, 2 * group)]
    for first in (groups[0], pairs[0]):
        first.insert(0, (at.pole + 1, POLAR))

    def moved(name, row, count, values, shift):
        for (key, _, way), ref in zip(SHARED_KEYS, shared):
            if key == name and way == shift:
                column = half - HALO - 1 if shift == 1 else HALO
                for i in range(count):
                    ref[row + i : row + i + 1, :] = values[i * half + column : i * half + column + 1, :]
        return ring(values, half, shift)

    x0 = scratch[0]
    for row in (at.top, at.bottom, at.pole, at.count - 1):
        x0[at(row), :] = jnp.zeros((half, 128), F32)
    for i in range(blocks + POLAR):
        x0[at(at.of(i)), :] = cells[i * half : (i + 1) * half, :].astype(F32)
    stages = layers(at, groups, pairs, moved, *scratch, w1, w2, wd, wc, wu)

    y2, yu = scratch[3], scratch[6]
    lane = lax.broadcasted_iota(jnp.int32, (8, 2 * half), 1)
    even = lax.rem(lane, 2) == 0
    edge = (lane < 2 * HALO) | (lane >= 2 * half - 2 * HALO)

    def weave(values, i, p):
        spread = lax.div(lane, 2) + i * half
        evens = jnp.take_along_axis(values[p * 16 : p * 16 + 8], spread, axis=1)
        odds = jnp.take_along_axis(values[p * 16 + 8 : p * 16 + 16], spread, axis=1)
        return jnp.where(even, evens, odds)

    def last(row, count):
        def finish(found):
            found = project(found, wp)
            for n in range(count // 2):
                pair = (row - 1) // 2 + n
                own = found[:, n * 2 * half : (n + 1) * 2 * half]
                base = skip[pair * 32 : (pair + 1) * 32, :]
                for i in range(2):
                    for p in range(2):
                        line = (4 * pair + 2 * i + p) * 8
                        inner = jnp.where(edge, 0.0, weave(own, i, p))
                        update[line : line + 8, :] = inner + weave(base, i, p)

        return lambda: merge(at, row, count, y2, yu, wm), finish, [(row, count)]

    run(at, stages + [[last(*ranges[-1]) for ranges in groups]], AHEAD)


def edges_kernel(cells, inner, outer, w1, w2, wd, wc, wu, wm, wp, update, *refs):
    shared, out, scratch = refs[: len(SHARED_KEYS)], refs[len(SHARED_KEYS)], refs[len(SHARED_KEYS) + 1 :]
    even = lax.rem(lax.axis_index("lon"), 2) == 0
    half = out.shape[2] // 2
    blocks = out.shape[1] // 2
    step = 4 * HALO
    at = Rows(step, blocks)
    place = lax.broadcasted_iota(jnp.int32, (step, 128), 0)
    x0 = scratch[0]
    near, far = inner[...].astype(F32), outer[...].astype(F32)
    left, right = jnp.where(even, far, near), jnp.where(even, near, far)
    beside = {}
    for row in (at.top, at.bottom, at.pole, at.count - 1):
        x0[at(row), :] = jnp.zeros((step, 128), F32)
    for i in range(blocks + POLAR):
        row = at.of(i)
        begin = cells[i * half : i * half + 16, :].astype(F32)
        finish = cells[(i + 1) * half - 16 : (i + 1) * half, :].astype(F32)
        base = row * step
        x0[base : base + HALO, :] = left[i * HALO : (i + 1) * HALO]
        x0[base + HALO : base + 2 * HALO, :] = begin[:HALO]
        x0[base + 2 * HALO : base + 3 * HALO, :] = finish[16 - HALO :]
        x0[base + 3 * HALO : base + 4 * HALO, :] = right[i * HALO : (i + 1) * HALO]
        beside[row] = {-1: begin[HALO : HALO + 1], 1: finish[15 - HALO : 16 - HALO]}
    beside[at.top] = {way: pltpu.roll(line, 32, 1) for way, line in beside[at.pole + 1].items()}
    beside[at.pole] = {way: pltpu.roll(line, 32, 1) for way, line in beside[1].items()}

    def moved(name, row, count, values, shift):
        lines = []
        target = 2 * HALO if shift == 1 else 2 * HALO - 1
        for i in range(count):
            line = pltpu.roll(values[i * step : (i + 1) * step], shift % step, 0)
            if name == "x0":
                own = beside[row + i][shift] if row + i in beside else None
            else:
                ref = next(r for (key, _, way), r in zip(SHARED_KEYS, shared) if (key, way) == (name, shift))
                own = ref[row + i : row + i + 1, :]
            if own is not None:
                parts = []
                for lanes in range(0, values.shape[1], 128):
                    fix = jnp.broadcast_to(own[:, lanes : lanes + 128], (step, 128))
                    parts.append(jnp.where(place == target, fix, line[:, lanes : lanes + 128]))
                line = parts[0] if len(parts) == 1 else jnp.concatenate(parts, axis=1)
            lines.append(line)
        return lines[0] if count == 1 else jnp.concatenate(lines, axis=0)

    cut = EDGE_ROWS
    groups = [[(1, cut)], [(1 + cut, blocks - cut), (at.pole + 1, POLAR)]]
    pairs = [[(1, blocks), (at.pole + 1, POLAR)]]
    parts = []

    def last(row, count):
        def finish(found):
            parts.append(project(found, wp))

        return lambda: merge(at, row, count, scratch[3], scratch[6], wm), finish, [(row, count)]

    stages = layers(at, groups, pairs, moved, *scratch, w1, w2, wd, wc, wu)
    run(at, stages + [[last(1, blocks // 2), last(1 + blocks // 2, blocks // 2)]], 1)
    found = jnp.concatenate(parts, axis=1)

    columns = 2 * half
    lane = lax.broadcasted_iota(jnp.int32, (8, columns), 1)
    first = lane < 2 * HALO
    edge = first | (lane >= columns - 2 * HALO)
    column = jnp.where(first, HALO + lax.div(lane, 2), 3 * HALO - lax.div(columns + 1 - lane, 2))
    column = jnp.where(edge, column, 0)
    odd = lax.rem(lane, 2) == 1
    per = columns // step
    for i in range(blocks):
        spread = column + (i % per) * step
        lanes = slice(i // per * columns, (i // per + 1) * columns)
        for p in range(2):
            evens = jnp.take_along_axis(found[p * 16 : p * 16 + 8, lanes], spread, axis=1)
            odds = jnp.take_along_axis(found[p * 16 + 8 : p * 16 + 16, lanes], spread, axis=1)
            h = 2 * i + p
            line = slice(h * 8, (h + 1) * 8)
            out[:, h, :] = jnp.where(edge, jnp.where(odd, odds, evens), 0.0) + update[line, :]


def buffers(step, blocks):
    rows = Rows(step, blocks).count * step
    shapes = ((128, F32), (128, F32), (512, BF16), (512, BF16), (384, BF16), (256, BF16), (512, BF16))
    return [pltpu.VMEM((rows, lanes), dtype) for lanes, dtype in shapes]


def inside(cells, skip, weights):
    columns = skip.shape[1]
    blocks = skip.shape[0] // 16
    rows = Rows(columns // 2, blocks).count
    return pl.pallas_call(
        inside_kernel,
        out_shape=[jax.ShapeDtypeStruct((blocks * 16, columns), F32)]
        + [jax.ShapeDtypeStruct((rows, lanes), F32) for _, lanes, _ in SHARED_KEYS],
        scratch_shapes=buffers(columns // 2, blocks),
        compiler_params=pltpu.CompilerParams(vmem_limit_bytes=20 * 2**20),
        cost_estimate=pl.CostEstimate(flops=4 * 10**9, bytes_accessed=4 * 10**6, transcendentals=0),
        name="inside",
    )(cells, skip, *weights)


def edges(out_shape, cells, inner, outer, weights, found):
    return pl.pallas_call(
        edges_kernel,
        out_shape=jax.ShapeDtypeStruct(out_shape, F32),
        scratch_shapes=buffers(4 * HALO, out_shape[1] // 2),
        compiler_params=pltpu.CompilerParams(vmem_limit_bytes=20 * 2**20),
        name="edges",
    )(cells, inner, outer, *weights, *found)


def shards(
    latlon_fields,
    remap_table,
    kernel_first,
    kernel_second,
    kernel_down,
    kernel_coarse,
    kernel_up,
    kernel_merge,
    projection,
):
    _, grid_rows, columns = remap_table.shape
    count = lax.axis_size("lon")
    polar = opposite(remap_table[:, : 4 * ((POLAR + 1) // 2), :], "lon")
    parcels = pack(latlon_fields, count, columns)
    block = lax.all_to_all(parcels, "lon", split_axis=0, concat_axis=0, tiled=True)
    places, *weights = prepare(
        remap_table, kernel_first, kernel_second, kernel_down, kernel_coarse, kernel_up, kernel_merge, projection
    )
    cells, inner, outer, skip = remap(block, places, polar)
    outer = swap(outer, "lon", 1)
    inner = swap(inner, "lon", 0)
    found = inside(cells, skip, weights)
    return edges((projection.shape[0], grid_rows, columns), cells, inner, outer, weights, found)


def solution(mesh):
    return jax.shard_map(
        shards,
        mesh=mesh,
        in_specs=(
            P("groups", "lon", None),
            P(None, None, "lon"),
            P(),
            P(),
            P(),
            P(),
            P(),
            P(),
            P(),
        ),
        out_specs=P("groups", None, "lon"),
        check_vma=False,
    )
```

```python
import jax
import jax.numpy as jnp
from jax import lax
from jax.experimental import pallas as pl
from jax.experimental.pallas import tpu as pltpu
from jax.sharding import PartitionSpec as P

F32 = jnp.float32
BF16 = jnp.bfloat16
HALO = 4
EDGE_ROWS = 9
AHEAD = 2
PARTS = 4
POLAR = 3


def swap(block, axis, first):
    devices = lax.axis_size(axis)
    pairs = [((first + i) % devices, (first + i + 1) % devices) for i in range(0, devices, 2)]
    return lax.ppermute(block, axis, pairs + [(b, a) for a, b in pairs])


def opposite(block, axis):
    devices = lax.axis_size(axis)
    return lax.ppermute(block, axis, [(i, (i + devices // 2) % devices) for i in range(devices)])


def pack_kernel(fields_hbm, parcels, fields, load_sems, sems):
    devices, channels, _, columns = fields.shape
    span = devices // PARTS
    loads = []
    for target in range(devices):
        lanes = slice(target * columns, (target + 1) * columns)
        loads.append(pltpu.make_async_copy(fields_hbm.at[:, :, lanes], fields.at[target], load_sems.at[target]))
        loads[-1].start()
    copies = []
    for n in range(PARTS):
        for load in loads[n * span : (n + 1) * span]:
            load.wait()
        first, other = n * span, (n * span + devices // 2) % devices
        places = parcels.at[first : first + span, :channels], parcels.at[other : other + span, channels:]
        for place in places:
            copies.append(pltpu.make_async_copy(fields.at[first : first + span], place, sems.at[len(copies)]))
            copies[-1].start()
    for copy in copies:
        copy.wait()


def pack(fields, devices, columns):
    channels, rows, _ = fields.shape
    parcels = pl.pallas_call(
        pack_kernel,
        in_specs=[pl.BlockSpec(memory_space=pltpu.HBM)],
        out_specs=pl.BlockSpec(memory_space=pltpu.HBM),
        out_shape=pltpu.HBM((devices, 2 * channels, rows, columns), BF16),
        scratch_shapes=[
            pltpu.VMEM((devices, channels, rows, columns), BF16),
            pltpu.SemaphoreType.DMA((devices,)),
            pltpu.SemaphoreType.DMA((2 * PARTS,)),
        ],
        compiler_params=pltpu.CompilerParams(vmem_limit_bytes=16 * 2**20),
        name="pack",
    )(pltpu.with_memory_space_constraint(fields, pltpu.HBM))
    return parcels.reshape(devices, 2 * channels * rows, columns)


def tap(kernel_ref, row, col):
    if 0 <= row < 3 and 0 <= col < 3:
        return kernel_ref[row, col].astype(F32)
    return jnp.zeros(kernel_ref.shape[2:], F32)


def arrange(first, second, down, coarse, up, merge, projection, w1, w2, wd, wc, wu, wm, wp):
    channels = second.shape[3]
    inputs = first.shape[2]
    for half in range(2):
        for side in range(2):
            for p in range(2):
                for q in range(2):
                    t = 1 + p if half == 0 else (3, 0)[p]
                    u = 1 + q if side == 0 else (3, 0)[q]
                    at = (((half * 2 + side) * 2 + p) * 2 + q) * inputs
                    pieces = [tap(first, t - a, u - b) for a in range(2) for b in range(2)]
                    w1[at : at + inputs, :] = jnp.concatenate(pieces, axis=1).astype(BF16)
    for t in range(4):
        for code in range(4):
            at = (t * 4 + code) * channels
            source = (0, 1, -2, -1)[code]
            for p in range(2):
                pair = [tap(second, t - p, source - target + 1) for target in (-1, 0)]
                w2[at : at + channels, p * 128 : (p + 1) * 128] = jnp.concatenate(pair, axis=0).T.astype(BF16)
            source = code - 1
            for p in range(2):
                pair = [tap(merge, t - p, source - target + 1) for target in (0, 1)]
                pair = jnp.concatenate(pair, axis=0).T.astype(BF16)
                wm[at : at + channels, p * 128 : (p + 1) * 128] = pair[:channels]
                wm[16 * channels + at : 16 * channels + at + channels, p * 128 : (p + 1) * 128] = pair[channels:]
            if t < 3:
                wd[at : at + channels, :] = tap(down, t, code).astype(BF16)
    wide = coarse.shape[3]
    for a in range(3):
        for b in range(3):
            at = (a * 3 + b) * wide
            wc[at : at + wide, :] = tap(coarse, a, b).T.astype(BF16)
    row_taps = ((1, 3), (0, 2))
    col_taps = ((0, 2), (3, 1))
    for di in range(2):
        for dj in range(2):
            at = (di * 2 + dj) * wide
            for p in range(2):
                pair = jnp.concatenate([tap(up, row_taps[p][di], col_taps[q][dj]) for q in range(2)], axis=0)
                wu[at : at + wide, p * 128 : (p + 1) * 128] = pair.T.astype(BF16)
    rows = projection[...].astype(F32)
    blank = jnp.zeros_like(rows)
    lines = [jnp.concatenate([rows if m == n else blank for m in range(4)], axis=1) for n in range(4)]
    wp[...] = jnp.concatenate(lines, axis=0).astype(BF16)


def locate(rows, cols):
    grid_rows, columns = rows.shape
    half = columns // 2
    code = rows * columns + cols
    lane = lax.broadcasted_iota(jnp.int32, (grid_rows, columns), 1)
    odd = [jnp.take_along_axis(code, lax.rem(lane, half) * 2 + q, axis=1) for q in range(2)]
    left = lax.broadcasted_iota(jnp.int32, (1, columns), 1) < half
    lines = []
    for pair in range(grid_rows // 4):
        for p in range(2):
            for q in range(2):
                above, below = 4 * pair + p, 4 * pair + 2 + p
                lines.append(jnp.where(left, odd[q][above : above + 1, :], odd[q][below : below + 1, :]))
    return jnp.concatenate(lines, axis=0)


def prepare_kernel(*refs):
    args, (places, *weights), scratch, sems = refs[:8], refs[8:16], refs[16:24], refs[24]
    copies = [
        pltpu.make_async_copy(source, target, sems.at[n]) for n, (source, target) in enumerate(zip(args, scratch))
    ]
    for copy in copies:
        copy.start()
    copies[0].wait()
    table = scratch[0]
    places[...] = locate(table[0], lax.rem(table[1], table.shape[2]))
    for copy in copies[1:]:
        copy.wait()
    arrange(*scratch[1:], *weights)


def prepare(table, first, second, down, coarse, up, merge, projection):
    channels, wide = second.shape[3], coarse.shape[3]
    columns = table.shape[2]
    shapes = (
        (16 * first.shape[3], 4 * channels),
        (16 * channels, 4 * channels),
        (12 * channels, wide),
        (9 * wide, wide),
        (4 * wide, 4 * channels),
        (32 * channels, 4 * channels),
        (4 * projection.shape[0], 4 * channels),
    )
    args = (table, jnp.swapaxes(first, 2, 3), second, jnp.swapaxes(down, 2, 3), coarse, up, merge, projection)
    return pl.pallas_call(
        prepare_kernel,
        in_specs=[pl.BlockSpec(memory_space=pltpu.HBM)] * 8,
        out_shape=[jax.ShapeDtypeStruct(table.shape[1:], jnp.int32)] + [jax.ShapeDtypeStruct(s, BF16) for s in shapes],
        scratch_shapes=[pltpu.VMEM(a.shape, a.dtype) for a in args] + [pltpu.SemaphoreType.DMA((8,))],
        compiler_params=pltpu.CompilerParams(vmem_limit_bytes=16 * 2**20),
        name="prepare",
    )(*[pltpu.with_memory_space_constraint(a, pltpu.HBM) for a in args])


def remap_kernel(block, places, polar, cells, inner, outer, skip, wide):
    even = lax.rem(lax.axis_index("lon"), 2) == 0
    devices, depth, columns = block.shape
    depth = depth // 2
    channels = depth // 2
    lines = [places[...], locate(polar[0], lax.rem(polar[1], columns))]
    lines = jnp.concatenate(lines, axis=0)
    sources = lax.div(lines, 2 * columns)
    offsets = lax.rem(lines, 2 * columns).astype(F32)
    line_at = lax.broadcasted_iota(jnp.int32, (2 * columns, columns), 0).astype(F32)
    half = columns // 2
    wide[...] = block[...].astype(F32).reshape(wide.shape)
    fields = []
    for side in range(2):
        parts = []
        for row in range(2):
            places_of = [s * 2 * depth + side * depth + row for s in range(devices)]
            lines = [wide[pl.ds(at, channels, stride=2), :] for at in places_of]
            parts.append(jnp.concatenate(lines, axis=0).astype(BF16))
        fields.append(jnp.concatenate(parts, axis=1))
    pairs = cells.shape[0] // columns
    begins, finishes = [], []
    own_pairs = skip.shape[0] // 32
    for pair in range(pairs):
        own = pair < own_pairs
        chosen = []
        for n in range(4):
            here = line_at == jnp.broadcast_to(offsets[4 * pair + n : 4 * pair + n + 1, :], line_at.shape)
            chosen.append(jnp.where(here, 1.0, 0.0).astype(BF16))
        found = jnp.dot(fields[0 if own else 1], jnp.concatenate(chosen, axis=1), preferred_element_type=F32)
        lines = []
        for n in range(4):
            line = sources[4 * pair + n : 4 * pair + n + 1, :]
            line = jnp.broadcast_to(line, (channels, columns))
            total = jnp.zeros((channels, columns), F32)
            for s in range(devices):
                value = found[s * channels : (s + 1) * channels, n * columns : (n + 1) * columns]
                total = jnp.where(line == s, value, total)
            lines.append(total)
            if own:
                skip[(pair * 4 + n) * 8 : (pair * 4 + n + 1) * 8, :] = total[:8]
        turned = jnp.concatenate(lines + lines, axis=0).T
        cells[pair * columns : (pair + 1) * columns, :] = turned.astype(BF16)
        for i in range(2):
            begins.append(turned[i * half : i * half + HALO])
            finishes.append(turned[(i + 1) * half - HALO : (i + 1) * half])
    begins, finishes = jnp.concatenate(begins, axis=0), jnp.concatenate(finishes, axis=0)
    inner[...] = jnp.where(even, finishes, begins).astype(BF16)
    outer[...] = jnp.where(even, begins, finishes).astype(BF16)


def remap(block, places, polar):
    columns = block.shape[2]
    grid_rows = places.shape[0]
    count = (grid_rows + polar.shape[1]) // 4
    return pl.pallas_call(
        remap_kernel,
        out_shape=[
            jax.ShapeDtypeStruct((count * columns, columns), BF16),
            jax.ShapeDtypeStruct((count * 2 * HALO, columns), BF16),
            jax.ShapeDtypeStruct((count * 2 * HALO, columns), BF16),
            jax.ShapeDtypeStruct((grid_rows * 8, columns), F32),
        ],
        scratch_shapes=[pltpu.VMEM((block.shape[0] * block.shape[1], columns), F32)],
        compiler_params=pltpu.CompilerParams(vmem_limit_bytes=16 * 2**20),
        name="remap",
    )(block, places, polar)


def silu(values):
    h = 0.5 * values
    return (h + h * jnp.tanh(h)).astype(BF16).astype(F32)


def ring(values, step, shift):
    rows = [pltpu.roll(values[at : at + step], shift % step, 0) for at in range(0, values.shape[0], step)]
    return rows[0] if len(rows) == 1 else jnp.concatenate(rows, axis=0)


class Rows:
    def __init__(self, step, blocks):
        self.step, self.blocks = step, blocks
        self.top, self.bottom, self.pole = 0, blocks + 1, blocks + 2
        self.count = blocks + 2 + POLAR + 2

    def __call__(self, row, count=1):
        return slice(row * self.step, (row + count) * self.step)

    def of(self, i):
        return 1 + i if i < self.blocks else self.pole + 1 + i - self.blocks

    def mask(self, count, width):
        lane = lax.broadcasted_iota(jnp.int32, (count * self.step, 128), 1)
        return lax.rem(lax.div(lane, width), 2) == 0


def product(pieces, weights):
    values = pieces[0] if len(pieces) == 1 else jnp.concatenate(pieces, axis=0)
    return jnp.dot(values, weights[...], preferred_element_type=F32)


def layers(at, groups, pairs, moved, x0, y0, y1, y2, yc, yo, yu, w1, w2, wd, wc, wu):
    step, top, bottom, pole = at.step, at.top, at.bottom, at.pole
    x0[at(top), :] = pltpu.roll(x0[at(pole + 1), :], 32, 1)
    x0[at(pole), :] = pltpu.roll(x0[at(1), :], 32, 1)
    ready = set()

    def widen(row):
        if row not in ready:
            ready.add(row)
            x = x0[at(row), :]
            side = jnp.where(at.mask(1, 16), moved("x0", row, 1, x, -1), moved("x0", row, 1, x, 1))
            y0[at(row), :] = jnp.where(at.mask(1, 64), x, side)

    for y, polar_rows in ((y1, POLAR), (y2, POLAR - 1), (yc, POLAR - 1), (yo, POLAR - 2), (yu, POLAR - 2)):
        for row in (bottom, pole + 1 + polar_rows):
            y[at(row), :] = jnp.zeros((step, y.shape[1]), BF16)

    def layer(name, polar_rows, inputs, weights, store, edge, paired=False):
        def task(ranges):
            ranges = [(row, polar_rows if row == pole + 1 else count) for row, count in ranges]

            def begin():
                pieces = [jnp.concatenate(inputs(row, count), axis=1) for row, count in ranges]
                return product(pieces, weights)

            def finish(found):
                found = silu(found)
                start = 0
                for row, count in ranges:
                    if paired:
                        lanes = found.shape[1] // 2
                        rows = []
                        for n in range(count):
                            line = slice(start + n // 2 * step, start + (n // 2 + 1) * step)
                            rows.append(found[line, n % 2 * lanes : (n % 2 + 1) * lanes])
                        values = rows[0] if count == 1 else jnp.concatenate(rows, axis=0)
                        start += (count + 1) // 2 * step
                    else:
                        values = found[start : start + count * step]
                        start += count * step
                    store(name, row, count, values)
                    if row == pole + 1:
                        edge(top, pole + 1)
                    if row == 1:
                        edge(pole, 1)

            return begin, finish, ranges

        return [task(ranges) for ranges in (pairs if paired else groups)]

    def fine(y, shift):
        def store(name, row, count, values):
            shifted = moved(name, row, count, values, shift).astype(BF16)
            values = values.astype(BF16)
            for p in range(2):
                lanes = slice(p * 128, (p + 1) * 128)
                y[at(row, count), p * 256 : p * 256 + 128] = values[:, lanes]
                y[at(row, count), p * 256 + 128 : p * 256 + 256] = shifted[:, lanes]

        def edge(target, source):
            y[at(target), 256:512] = y[at(source), 0:256]

        return store, edge

    def first_inputs(row, count):
        for n in range(row - 1, row + count + 1):
            widen(n)
        vertical = jnp.where(at.mask(count, 32), y0[at(row + 1, count), :], y0[at(row - 1, count), :])
        return [y0[at(row, count), :].astype(BF16), vertical.astype(BF16)]

    def second_inputs(row, count):
        return [y1[at(row - 1, count), 256:512], y1[at(row, count), :], y1[at(row + 1, count), 0:256]]

    def down_inputs(row, count):
        return [y2[at(row - 1, count), 256:512], y2[at(row, count), :]]

    def coarse_inputs(row, count):
        return [yc[at(row + a, count), :] for a in (-1, 0, 1)]

    def up_inputs(row, count):
        return [yo[at(row, count), :], yo[at(row + 1, count), :]]

    def store_coarse_in(name, row, count, values):
        yc[at(row, count), 0:128] = moved(name, row, count, values, 1).astype(BF16)
        yc[at(row, count), 128:256] = values.astype(BF16)
        yc[at(row, count), 256:384] = moved(name, row, count, values, -1).astype(BF16)

    def edge_coarse_in(target, source):
        yc[at(target), :] = yc[at(source), :]

    def store_coarse_out(name, row, count, values):
        yo[at(row, count), 0:128] = moved(name, row, count, values, 1).astype(BF16)
        yo[at(row, count), 128:256] = values.astype(BF16)

    return [
        layer("y1", POLAR, first_inputs, w1, *fine(y1, 1)),
        layer("y2", POLAR - 1, second_inputs, w2, *fine(y2, -1)),
        layer("yc", POLAR - 1, down_inputs, wd, store_coarse_in, edge_coarse_in),
        layer("yo", POLAR - 2, coarse_inputs, wc, store_coarse_out, lambda target, source: None),
        layer("yu", POLAR - 2, up_inputs, wu, *fine(yu, -1)),
    ]


def run(at, stages, ahead):
    tasks, owner = [], {}
    for stage in stages:
        rows = {}
        for begin, finish, ranges in stage:
            reads = set()
            for row, count in ranges:
                reads.update(range(row - 1, row + count + 2))
            reads.update({at.pole + 1} if at.top in reads else (), {1} if at.pole in reads else ())
            tasks.append((begin, finish, {owner[row] for row in reads if row in owner}))
            for row, count in ranges:
                rows.update({n: len(tasks) - 1 for n in range(row, row + count)})
        owner = rows
    found, issued = {}, 0
    for turn in range(len(tasks)):
        while issued < len(tasks) and issued <= turn + ahead and all(n < turn for n in tasks[issued][2]):
            found[issued] = tasks[issued][0]()
            issued += 1
        tasks[turn][1](found.pop(turn))


def merge(at, row, count, y2, yu, wm):
    pieces = []
    for y in (y2, yu):
        pieces += [y[at(row - 1, count), 256:512], y[at(row, count), :], y[at(row + 1, count), 0:256]]
    return product([jnp.concatenate(pieces, axis=1)], wm)


def project(found, wp):
    merged = silu(found).astype(BF16)
    return lax.dot_general(wp[...], merged, (((1,), (1,)), ((), ())), preferred_element_type=F32)


SHARED = (("y1", 256, (1,)), ("y2", 256, (-1,)), ("yc", 128, (1, -1)), ("yo", 128, (1,)), ("yu", 256, (-1,)))
SHARED_KEYS = [(name, lanes, shift) for name, lanes, shifts in SHARED for shift in shifts]


def inside_kernel(cells, skip, w1, w2, wd, wc, wu, wm, wp, update, *refs):
    shared, scratch = refs[: len(SHARED_KEYS)], refs[len(SHARED_KEYS) :]
    half = update.shape[1] // 2
    blocks = update.shape[0] // 16
    at = Rows(half, blocks)
    group = 4

    groups = [[(1 + i, group)] for i in range(0, blocks, group)]
    pairs = [[(1 + i, 2 * group)] for i in range(0, blocks, 2 * group)]
    for first in (groups[0], pairs[0]):
        first.insert(0, (at.pole + 1, POLAR))

    def moved(name, row, count, values, shift):
        for (key, _, way), ref in zip(SHARED_KEYS, shared):
            if key == name and way == shift:
                column = half - HALO - 1 if shift == 1 else HALO
                for i in range(count):
                    ref[row + i : row + i + 1, :] = values[i * half + column : i * half + column + 1, :]
        return ring(values, half, shift)

    x0 = scratch[0]
    for row in (at.top, at.bottom, at.pole, at.count - 1):
        x0[at(row), :] = jnp.zeros((half, 128), F32)
    for i in range(blocks + POLAR):
        x0[at(at.of(i)), :] = cells[i * half : (i + 1) * half, :].astype(F32)
    stages = layers(at, groups, pairs, moved, *scratch, w1, w2, wd, wc, wu)

    y2, yu = scratch[3], scratch[6]
    lane = lax.broadcasted_iota(jnp.int32, (8, 2 * half), 1)
    even = lax.rem(lane, 2) == 0
    edge = (lane < 2 * HALO) | (lane >= 2 * half - 2 * HALO)

    def weave(values, i, p):
        spread = lax.div(lane, 2) + i * half
        evens = jnp.take_along_axis(values[p * 16 : p * 16 + 8], spread, axis=1)
        odds = jnp.take_along_axis(values[p * 16 + 8 : p * 16 + 16], spread, axis=1)
        return jnp.where(even, evens, odds)

    def last(row, count):
        def finish(found):
            found = project(found, wp)
            for n in range(count // 2):
                pair = (row - 1) // 2 + n
                own = found[:, n * 2 * half : (n + 1) * 2 * half]
                base = skip[pair * 32 : (pair + 1) * 32, :]
                for i in range(2):
                    for p in range(2):
                        line = (4 * pair + 2 * i + p) * 8
                        inner = jnp.where(edge, 0.0, weave(own, i, p))
                        update[line : line + 8, :] = inner + weave(base, i, p)

        return lambda: merge(at, row, count, y2, yu, wm), finish, [(row, count)]

    run(at, stages + [[last(*ranges[-1]) for ranges in groups]], AHEAD)


def edges_kernel(cells, inner, outer, w1, w2, wd, wc, wu, wm, wp, update, *refs):
    shared, out, scratch = refs[: len(SHARED_KEYS)], refs[len(SHARED_KEYS)], refs[len(SHARED_KEYS) + 1 :]
    even = lax.rem(lax.axis_index("lon"), 2) == 0
    half = out.shape[2] // 2
    blocks = out.shape[1] // 2
    step = 4 * HALO
    at = Rows(step, blocks)
    place = lax.broadcasted_iota(jnp.int32, (step, 128), 0)
    x0 = scratch[0]
    near, far = inner[...].astype(F32), outer[...].astype(F32)
    left, right = jnp.where(even, far, near), jnp.where(even, near, far)
    beside = {}
    for row in (at.top, at.bottom, at.pole, at.count - 1):
        x0[at(row), :] = jnp.zeros((step, 128), F32)
    for i in range(blocks + POLAR):
        row = at.of(i)
        begin = cells[i * half : i * half + 16, :].astype(F32)
        finish = cells[(i + 1) * half - 16 : (i + 1) * half, :].astype(F32)
        base = row * step
        x0[base : base + HALO, :] = left[i * HALO : (i + 1) * HALO]
        x0[base + HALO : base + 2 * HALO, :] = begin[:HALO]
        x0[base + 2 * HALO : base + 3 * HALO, :] = finish[16 - HALO :]
        x0[base + 3 * HALO : base + 4 * HALO, :] = right[i * HALO : (i + 1) * HALO]
        beside[row] = {-1: begin[HALO : HALO + 1], 1: finish[15 - HALO : 16 - HALO]}
    beside[at.top] = {way: pltpu.roll(line, 32, 1) for way, line in beside[at.pole + 1].items()}
    beside[at.pole] = {way: pltpu.roll(line, 32, 1) for way, line in beside[1].items()}

    def moved(name, row, count, values, shift):
        lines = []
        target = 2 * HALO if shift == 1 else 2 * HALO - 1
        for i in range(count):
            line = pltpu.roll(values[i * step : (i + 1) * step], shift % step, 0)
            if name == "x0":
                own = beside[row + i][shift] if row + i in beside else None
            else:
                ref = next(r for (key, _, way), r in zip(SHARED_KEYS, shared) if (key, way) == (name, shift))
                own = ref[row + i : row + i + 1, :]
            if own is not None:
                parts = []
                for lanes in range(0, values.shape[1], 128):
                    fix = jnp.broadcast_to(own[:, lanes : lanes + 128], (step, 128))
                    parts.append(jnp.where(place == target, fix, line[:, lanes : lanes + 128]))
                line = parts[0] if len(parts) == 1 else jnp.concatenate(parts, axis=1)
            lines.append(line)
        return lines[0] if count == 1 else jnp.concatenate(lines, axis=0)

    cut = EDGE_ROWS
    groups = [[(1, cut)], [(1 + cut, blocks - cut), (at.pole + 1, POLAR)]]
    pairs = [[(1, blocks), (at.pole + 1, POLAR)]]
    parts = []

    def last(row, count):
        def finish(found):
            parts.append(project(found, wp))

        return lambda: merge(at, row, count, scratch[3], scratch[6], wm), finish, [(row, count)]

    stages = layers(at, groups, pairs, moved, *scratch, w1, w2, wd, wc, wu)
    run(at, stages + [[last(1, blocks // 2), last(1 + blocks // 2, blocks // 2)]], 1)
    found = jnp.concatenate(parts, axis=1)

    columns = 2 * half
    lane = lax.broadcasted_iota(jnp.int32, (8, columns), 1)
    first = lane < 2 * HALO
    edge = first | (lane >= columns - 2 * HALO)
    column = jnp.where(first, HALO + lax.div(lane, 2), 3 * HALO - lax.div(columns + 1 - lane, 2))
    column = jnp.where(edge, column, 0)
    odd = lax.rem(lane, 2) == 1
    per = columns // step
    for i in range(blocks):
        spread = column + (i % per) * step
        lanes = slice(i // per * columns, (i // per + 1) * columns)
        for p in range(2):
            evens = jnp.take_along_axis(found[p * 16 : p * 16 + 8, lanes], spread, axis=1)
            odds = jnp.take_along_axis(found[p * 16 + 8 : p * 16 + 16, lanes], spread, axis=1)
            h = 2 * i + p
            line = slice(h * 8, (h + 1) * 8)
            out[:, h, :] = jnp.where(edge, jnp.where(odd, odds, evens), 0.0) + update[line, :]


def buffers(step, blocks):
    rows = Rows(step, blocks).count * step
    shapes = ((128, F32), (128, F32), (512, BF16), (512, BF16), (384, BF16), (256, BF16), (512, BF16))
    return [pltpu.VMEM((rows, lanes), dtype) for lanes, dtype in shapes]


def inside(cells, skip, weights):
    columns = skip.shape[1]
    blocks = skip.shape[0] // 16
    rows = Rows(columns // 2, blocks).count
    return pl.pallas_call(
        inside_kernel,
        out_shape=[jax.ShapeDtypeStruct((blocks * 16, columns), F32)]
        + [jax.ShapeDtypeStruct((rows, lanes), F32) for _, lanes, _ in SHARED_KEYS],
        scratch_shapes=buffers(columns // 2, blocks),
        compiler_params=pltpu.CompilerParams(vmem_limit_bytes=20 * 2**20),
        cost_estimate=pl.CostEstimate(flops=4 * 10**9, bytes_accessed=4 * 10**6, transcendentals=0),
        name="inside",
    )(cells, skip, *weights)


def edges(out_shape, cells, inner, outer, weights, found):
    return pl.pallas_call(
        edges_kernel,
        out_shape=jax.ShapeDtypeStruct(out_shape, F32),
        scratch_shapes=buffers(4 * HALO, out_shape[1] // 2),
        compiler_params=pltpu.CompilerParams(vmem_limit_bytes=20 * 2**20),
        name="edges",
    )(cells, inner, outer, *weights, *found)


def shards(
    latlon_fields,
    remap_table,
    kernel_first,
    kernel_second,
    kernel_down,
    kernel_coarse,
    kernel_up,
    kernel_merge,
    projection,
):
    _, grid_rows, columns = remap_table.shape
    count = lax.axis_size("lon")
    polar = opposite(remap_table[:, : 4 * ((POLAR + 1) // 2), :], "lon")
    parcels = pack(latlon_fields, count, columns)
    block = lax.all_to_all(parcels, "lon", split_axis=0, concat_axis=0, tiled=True)
    places, *weights = prepare(
        remap_table, kernel_first, kernel_second, kernel_down, kernel_coarse, kernel_up, kernel_merge, projection
    )
    cells, inner, outer, skip = remap(block, places, polar)
    outer = swap(outer, "lon", 1)
    inner = swap(inner, "lon", 0)
    found = inside(cells, skip, weights)
    return edges((projection.shape[0], grid_rows, columns), cells, inner, outer, weights, found)


def solution(mesh):
    return jax.shard_map(
        shards,
        mesh=mesh,
        in_specs=(
            P("groups", "lon", None),
            P(None, None, "lon"),
            P(),
            P(),
            P(),
            P(),
            P(),
            P(),
            P(),
        ),
        out_specs=P("groups", None, "lon"),
        check_vma=False,
    )
```

```python
import jax
import jax.numpy as jnp
from jax import lax
from jax.experimental import pallas as pl
from jax.experimental.pallas import tpu as pltpu
from jax.sharding import PartitionSpec as P

F32 = jnp.float32
BF16 = jnp.bfloat16
HALO = 4
EDGE_ROWS = 9
AHEAD = 2
PARTS = 4
POLAR = 3


def swap(block, axis, first):
    devices = lax.axis_size(axis)
    pairs = [((first + i) % devices, (first + i + 1) % devices) for i in range(0, devices, 2)]
    return lax.ppermute(block, axis, pairs + [(b, a) for a, b in pairs])


def opposite(block, axis):
    devices = lax.axis_size(axis)
    return lax.ppermute(block, axis, [(i, (i + devices // 2) % devices) for i in range(devices)])


def pack_kernel(fields_hbm, parcels, fields, load_sems, sems):
    devices, channels, _, columns = fields.shape
    span = devices // PARTS
    loads = []
    for target in range(devices):
        lanes = slice(target * columns, (target + 1) * columns)
        loads.append(pltpu.make_async_copy(fields_hbm.at[:, :, lanes], fields.at[target], load_sems.at[target]))
        loads[-1].start()
    copies = []
    for n in range(PARTS):
        for load in loads[n * span : (n + 1) * span]:
            load.wait()
        first, other = n * span, (n * span + devices // 2) % devices
        places = parcels.at[first : first + span, :channels], parcels.at[other : other + span, channels:]
        for place in places:
            copies.append(pltpu.make_async_copy(fields.at[first : first + span], place, sems.at[len(copies)]))
            copies[-1].start()
    for copy in copies:
        copy.wait()


def pack(fields, devices, columns):
    channels, rows, _ = fields.shape
    parcels = pl.pallas_call(
        pack_kernel,
        in_specs=[pl.BlockSpec(memory_space=pltpu.HBM)],
        out_specs=pl.BlockSpec(memory_space=pltpu.HBM),
        out_shape=pltpu.HBM((devices, 2 * channels, rows, columns), BF16),
        scratch_shapes=[
            pltpu.VMEM((devices, channels, rows, columns), BF16),
            pltpu.SemaphoreType.DMA((devices,)),
            pltpu.SemaphoreType.DMA((2 * PARTS,)),
        ],
        compiler_params=pltpu.CompilerParams(vmem_limit_bytes=16 * 2**20),
        name="pack",
    )(pltpu.with_memory_space_constraint(fields, pltpu.HBM))
    return parcels.reshape(devices, 2 * channels * rows, columns)


def tap(kernel_ref, row, col):
    if 0 <= row < 3 and 0 <= col < 3:
        return kernel_ref[row, col].astype(F32)
    return jnp.zeros(kernel_ref.shape[2:], F32)


def arrange(first, second, down, coarse, up, merge, projection, w1, w2, wd, wc, wu, wm, wp):
    channels = second.shape[3]
    inputs = first.shape[2]
    for half in range(2):
        for side in range(2):
            for p in range(2):
                for q in range(2):
                    t = 1 + p if half == 0 else (3, 0)[p]
                    u = 1 + q if side == 0 else (3, 0)[q]
                    at = (((half * 2 + side) * 2 + p) * 2 + q) * inputs
                    pieces = [tap(first, t - a, u - b) for a in range(2) for b in range(2)]
                    w1[at : at + inputs, :] = jnp.concatenate(pieces, axis=1).astype(BF16)
    for t in range(4):
        for code in range(4):
            at = (t * 4 + code) * channels
            source = (0, 1, -2, -1)[code]
            for p in range(2):
                pair = [tap(second, t - p, source - target + 1) for target in (-1, 0)]
                w2[at : at + channels, p * 128 : (p + 1) * 128] = jnp.concatenate(pair, axis=0).T.astype(BF16)
            source = code - 1
            for p in range(2):
                pair = [tap(merge, t - p, source - target + 1) for target in (0, 1)]
                pair = jnp.concatenate(pair, axis=0).T.astype(BF16)
                wm[at : at + channels, p * 128 : (p + 1) * 128] = pair[:channels]
                wm[16 * channels + at : 16 * channels + at + channels, p * 128 : (p + 1) * 128] = pair[channels:]
            if t < 3:
                wd[at : at + channels, :] = tap(down, t, code).astype(BF16)
    wide = coarse.shape[3]
    for a in range(3):
        for b in range(3):
            at = (a * 3 + b) * wide
            wc[at : at + wide, :] = tap(coarse, a, b).T.astype(BF16)
    row_taps = ((1, 3), (0, 2))
    col_taps = ((0, 2), (3, 1))
    for di in range(2):
        for dj in range(2):
            at = (di * 2 + dj) * wide
            for p in range(2):
                pair = jnp.concatenate([tap(up, row_taps[p][di], col_taps[q][dj]) for q in range(2)], axis=0)
                wu[at : at + wide, p * 128 : (p + 1) * 128] = pair.T.astype(BF16)
    rows = projection[...].astype(F32)
    blank = jnp.zeros_like(rows)
    lines = [jnp.concatenate([rows if m == n else blank for m in range(4)], axis=1) for n in range(4)]
    wp[...] = jnp.concatenate(lines, axis=0).astype(BF16)


def locate(rows, cols):
    grid_rows, columns = rows.shape
    half = columns // 2
    code = rows * columns + cols
    lane = lax.broadcasted_iota(jnp.int32, (grid_rows, columns), 1)
    odd = [jnp.take_along_axis(code, lax.rem(lane, half) * 2 + q, axis=1) for q in range(2)]
    left = lax.broadcasted_iota(jnp.int32, (1, columns), 1) < half
    lines = []
    for pair in range(grid_rows // 4):
        for p in range(2):
            for q in range(2):
                above, below = 4 * pair + p, 4 * pair + 2 + p
                lines.append(jnp.where(left, odd[q][above : above + 1, :], odd[q][below : below + 1, :]))
    return jnp.concatenate(lines, axis=0)


def prepare_kernel(*refs):
    args, (places, *weights), scratch, sems = refs[:8], refs[8:16], refs[16:24], refs[24]
    copies = [
        pltpu.make_async_copy(source, target, sems.at[n]) for n, (source, target) in enumerate(zip(args, scratch))
    ]
    for copy in copies:
        copy.start()
    copies[0].wait()
    table = scratch[0]
    places[...] = locate(table[0], lax.rem(table[1], table.shape[2]))
    for copy in copies[1:]:
        copy.wait()
    arrange(*scratch[1:], *weights)


def prepare(table, first, second, down, coarse, up, merge, projection):
    channels, wide = second.shape[3], coarse.shape[3]
    columns = table.shape[2]
    shapes = (
        (16 * first.shape[3], 4 * channels),
        (16 * channels, 4 * channels),
        (12 * channels, wide),
        (9 * wide, wide),
        (4 * wide, 4 * channels),
        (32 * channels, 4 * channels),
        (4 * projection.shape[0], 4 * channels),
    )
    args = (table, jnp.swapaxes(first, 2, 3), second, jnp.swapaxes(down, 2, 3), coarse, up, merge, projection)
    return pl.pallas_call(
        prepare_kernel,
        in_specs=[pl.BlockSpec(memory_space=pltpu.HBM)] * 8,
        out_shape=[jax.ShapeDtypeStruct(table.shape[1:], jnp.int32)] + [jax.ShapeDtypeStruct(s, BF16) for s in shapes],
        scratch_shapes=[pltpu.VMEM(a.shape, a.dtype) for a in args] + [pltpu.SemaphoreType.DMA((8,))],
        compiler_params=pltpu.CompilerParams(vmem_limit_bytes=16 * 2**20),
        name="prepare",
    )(*[pltpu.with_memory_space_constraint(a, pltpu.HBM) for a in args])


def collect(block, side, places, wide):
    devices, depth, columns = block.shape
    depth = depth // 2
    channels = depth // 2
    wide[...] = block[:, side * depth : (side + 1) * depth, :].astype(F32).reshape(wide.shape)
    parts = []
    for row in range(2):
        lines = [wide[pl.ds(s * depth + row, channels, stride=2), :] for s in range(devices)]
        parts.append(jnp.concatenate(lines, axis=0).astype(BF16))
    fields = jnp.concatenate(parts, axis=1)
    sources = lax.div(places, 2 * columns)
    offsets = lax.rem(places, 2 * columns).astype(F32)
    line_at = lax.broadcasted_iota(jnp.int32, (2 * columns, columns), 0).astype(F32)
    for pair in range(places.shape[0] // 4):
        chosen = []
        for n in range(4):
            here = line_at == jnp.broadcast_to(offsets[4 * pair + n : 4 * pair + n + 1, :], line_at.shape)
            chosen.append(jnp.where(here, 1.0, 0.0).astype(BF16))
        found = jnp.dot(fields, jnp.concatenate(chosen, axis=1), preferred_element_type=F32)
        lines = []
        for n in range(4):
            line = jnp.broadcast_to(sources[4 * pair + n : 4 * pair + n + 1, :], (channels, columns))
            total = jnp.zeros((channels, columns), F32)
            for s in range(devices):
                value = found[s * channels : (s + 1) * channels, n * columns : (n + 1) * columns]
                total = jnp.where(line == s, value, total)
            lines.append(total)
        yield pair, lines


def cells_of(lines, pair, cells):
    turned = jnp.concatenate(lines + lines, axis=0).T
    columns = turned.shape[0]
    half = columns // 2
    cells[pair * columns : (pair + 1) * columns, :] = turned.astype(BF16)
    begin = [turned[i * half : i * half + HALO] for i in range(2)]
    finish = [turned[(i + 1) * half - HALO : (i + 1) * half] for i in range(2)]
    return jnp.concatenate(begin, axis=0), jnp.concatenate(finish, axis=0)


def own_kernel(block, places, cells, begin, finish, skip, wide):
    for pair, lines in collect(block, 0, places[...], wide):
        for n in range(4):
            skip[(pair * 4 + n) * 8 : (pair * 4 + n + 1) * 8, :] = lines[n][:8]
        rows = slice(pair * 2 * HALO, (pair + 1) * 2 * HALO)
        begin[rows, :], finish[rows, :] = cells_of(lines, pair, cells)


def remap_own(block, places):
    devices, depth, columns = block.shape
    grid_rows = places.shape[0]
    count = grid_rows // 4
    return pl.pallas_call(
        own_kernel,
        out_shape=[
            jax.ShapeDtypeStruct((count * columns, columns), BF16),
            jax.ShapeDtypeStruct((count * 2 * HALO, columns), F32),
            jax.ShapeDtypeStruct((count * 2 * HALO, columns), F32),
            jax.ShapeDtypeStruct((grid_rows * 8, columns), F32),
        ],
        scratch_shapes=[pltpu.VMEM((devices * depth // 2, columns), F32)],
        compiler_params=pltpu.CompilerParams(vmem_limit_bytes=16 * 2**20),
        name="remap_own",
    )(block, places)


def polar_kernel(block, polar, begin, finish, cells, inner, outer, wide):
    columns = block.shape[2]
    places = locate(polar[0], lax.rem(polar[1], columns))
    begins, finishes = [begin[...]], [finish[...]]
    for pair, lines in collect(block, 1, places, wide):
        first, last = cells_of(lines, pair, cells)
        begins.append(first)
        finishes.append(last)
    even = lax.rem(lax.axis_index("lon"), 2) == 0
    begins, finishes = jnp.concatenate(begins, axis=0), jnp.concatenate(finishes, axis=0)
    inner[...] = jnp.where(even, finishes, begins).astype(BF16)
    outer[...] = jnp.where(even, begins, finishes).astype(BF16)


def remap_polar(block, polar, begin, finish):
    devices, depth, columns = block.shape
    count = polar.shape[1] // 4
    rows = begin.shape[0] + count * 2 * HALO
    return pl.pallas_call(
        polar_kernel,
        out_shape=[
            jax.ShapeDtypeStruct((count * columns, columns), BF16),
            jax.ShapeDtypeStruct((rows, columns), BF16),
            jax.ShapeDtypeStruct((rows, columns), BF16),
        ],
        scratch_shapes=[pltpu.VMEM((devices * depth // 2, columns), F32)],
        compiler_params=pltpu.CompilerParams(vmem_limit_bytes=16 * 2**20),
        name="remap_polar",
    )(block, polar, begin, finish)


def silu(values):
    h = 0.5 * values
    return (h + h * jnp.tanh(h)).astype(BF16).astype(F32)


def ring(values, step, shift):
    rows = [pltpu.roll(values[at : at + step], shift % step, 0) for at in range(0, values.shape[0], step)]
    return rows[0] if len(rows) == 1 else jnp.concatenate(rows, axis=0)


class Rows:
    def __init__(self, step, blocks):
        self.step, self.blocks = step, blocks
        self.top, self.bottom, self.pole = 0, blocks + 1, blocks + 2
        self.count = blocks + 2 + POLAR + 2

    def __call__(self, row, count=1):
        return slice(row * self.step, (row + count) * self.step)

    def of(self, i):
        return 1 + i if i < self.blocks else self.pole + 1 + i - self.blocks

    def mask(self, count, width):
        lane = lax.broadcasted_iota(jnp.int32, (count * self.step, 128), 1)
        return lax.rem(lax.div(lane, width), 2) == 0


def product(pieces, weights):
    values = pieces[0] if len(pieces) == 1 else jnp.concatenate(pieces, axis=0)
    return jnp.dot(values, weights[...], preferred_element_type=F32)


def layers(at, groups, pairs, moved, x0, y0, y1, y2, yc, yo, yu, w1, w2, wd, wc, wu):
    step, top, bottom, pole = at.step, at.top, at.bottom, at.pole
    x0[at(top), :] = pltpu.roll(x0[at(pole + 1), :], 32, 1)
    x0[at(pole), :] = pltpu.roll(x0[at(1), :], 32, 1)
    ready = set()

    def widen(row):
        if row not in ready:
            ready.add(row)
            x = x0[at(row), :]
            side = jnp.where(at.mask(1, 16), moved("x0", row, 1, x, -1), moved("x0", row, 1, x, 1))
            y0[at(row), :] = jnp.where(at.mask(1, 64), x, side)

    for y, polar_rows in ((y1, POLAR), (y2, POLAR - 1), (yc, POLAR - 1), (yo, POLAR - 2), (yu, POLAR - 2)):
        for row in (bottom, pole + 1 + polar_rows):
            y[at(row), :] = jnp.zeros((step, y.shape[1]), BF16)

    def layer(name, polar_rows, inputs, weights, store, edge, paired=False):
        def task(ranges):
            ranges = [(row, polar_rows if row == pole + 1 else count) for row, count in ranges]

            def begin():
                pieces = [jnp.concatenate(inputs(row, count), axis=1) for row, count in ranges]
                return product(pieces, weights)

            def finish(found):
                found = silu(found)
                start = 0
                for row, count in ranges:
                    if paired:
                        lanes = found.shape[1] // 2
                        rows = []
                        for n in range(count):
                            line = slice(start + n // 2 * step, start + (n // 2 + 1) * step)
                            rows.append(found[line, n % 2 * lanes : (n % 2 + 1) * lanes])
                        values = rows[0] if count == 1 else jnp.concatenate(rows, axis=0)
                        start += (count + 1) // 2 * step
                    else:
                        values = found[start : start + count * step]
                        start += count * step
                    store(name, row, count, values)
                    if row == pole + 1:
                        edge(top, pole + 1)
                    if row == 1:
                        edge(pole, 1)

            return begin, finish, ranges

        return [task(ranges) for ranges in (pairs if paired else groups)]

    def fine(y, shift):
        def store(name, row, count, values):
            shifted = moved(name, row, count, values, shift).astype(BF16)
            values = values.astype(BF16)
            for p in range(2):
                lanes = slice(p * 128, (p + 1) * 128)
                y[at(row, count), p * 256 : p * 256 + 128] = values[:, lanes]
                y[at(row, count), p * 256 + 128 : p * 256 + 256] = shifted[:, lanes]

        def edge(target, source):
            y[at(target), 256:512] = y[at(source), 0:256]

        return store, edge

    def first_inputs(row, count):
        for n in range(row - 1, row + count + 1):
            widen(n)
        vertical = jnp.where(at.mask(count, 32), y0[at(row + 1, count), :], y0[at(row - 1, count), :])
        return [y0[at(row, count), :].astype(BF16), vertical.astype(BF16)]

    def second_inputs(row, count):
        return [y1[at(row - 1, count), 256:512], y1[at(row, count), :], y1[at(row + 1, count), 0:256]]

    def down_inputs(row, count):
        return [y2[at(row - 1, count), 256:512], y2[at(row, count), :]]

    def coarse_inputs(row, count):
        return [yc[at(row + a, count), :] for a in (-1, 0, 1)]

    def up_inputs(row, count):
        return [yo[at(row, count), :], yo[at(row + 1, count), :]]

    def store_coarse_in(name, row, count, values):
        yc[at(row, count), 0:128] = moved(name, row, count, values, 1).astype(BF16)
        yc[at(row, count), 128:256] = values.astype(BF16)
        yc[at(row, count), 256:384] = moved(name, row, count, values, -1).astype(BF16)

    def edge_coarse_in(target, source):
        yc[at(target), :] = yc[at(source), :]

    def store_coarse_out(name, row, count, values):
        yo[at(row, count), 0:128] = moved(name, row, count, values, 1).astype(BF16)
        yo[at(row, count), 128:256] = values.astype(BF16)

    return [
        layer("y1", POLAR, first_inputs, w1, *fine(y1, 1)),
        layer("y2", POLAR - 1, second_inputs, w2, *fine(y2, -1)),
        layer("yc", POLAR - 1, down_inputs, wd, store_coarse_in, edge_coarse_in),
        layer("yo", POLAR - 2, coarse_inputs, wc, store_coarse_out, lambda target, source: None),
        layer("yu", POLAR - 2, up_inputs, wu, *fine(yu, -1)),
    ]


def run(at, stages, ahead):
    tasks, owner = [], {}
    for stage in stages:
        rows = {}
        for begin, finish, ranges in stage:
            reads = set()
            for row, count in ranges:
                reads.update(range(row - 1, row + count + 2))
            reads.update({at.pole + 1} if at.top in reads else (), {1} if at.pole in reads else ())
            tasks.append((begin, finish, {owner[row] for row in reads if row in owner}))
            for row, count in ranges:
                rows.update({n: len(tasks) - 1 for n in range(row, row + count)})
        owner = rows
    found, issued = {}, 0
    for turn in range(len(tasks)):
        while issued < len(tasks) and issued <= turn + ahead and all(n < turn for n in tasks[issued][2]):
            found[issued] = tasks[issued][0]()
            issued += 1
        tasks[turn][1](found.pop(turn))


def merge(at, row, count, y2, yu, wm):
    pieces = []
    for y in (y2, yu):
        pieces += [y[at(row - 1, count), 256:512], y[at(row, count), :], y[at(row + 1, count), 0:256]]
    return product([jnp.concatenate(pieces, axis=1)], wm)


def project(found, wp):
    merged = silu(found).astype(BF16)
    return lax.dot_general(wp[...], merged, (((1,), (1,)), ((), ())), preferred_element_type=F32)


SHARED = (("y1", 256, (1,)), ("y2", 256, (-1,)), ("yc", 128, (1, -1)), ("yo", 128, (1,)), ("yu", 256, (-1,)))
SHARED_KEYS = [(name, lanes, shift) for name, lanes, shifts in SHARED for shift in shifts]


def inside_kernel(cells, polar_cells, skip, w1, w2, wd, wc, wu, wm, wp, update, *refs):
    shared, scratch = refs[: len(SHARED_KEYS)], refs[len(SHARED_KEYS) :]
    half = update.shape[1] // 2
    blocks = update.shape[0] // 16
    at = Rows(half, blocks)
    group = 4

    groups = [[(1 + i, group)] for i in range(0, blocks, group)]
    pairs = [[(1 + i, 2 * group)] for i in range(0, blocks, 2 * group)]
    for first in (groups[0], pairs[0]):
        first.insert(0, (at.pole + 1, POLAR))

    def moved(name, row, count, values, shift):
        for (key, _, way), ref in zip(SHARED_KEYS, shared):
            if key == name and way == shift:
                column = half - HALO - 1 if shift == 1 else HALO
                for i in range(count):
                    ref[row + i : row + i + 1, :] = values[i * half + column : i * half + column + 1, :]
        return ring(values, half, shift)

    x0 = scratch[0]
    for row in (at.top, at.bottom, at.pole, at.count - 1):
        x0[at(row), :] = jnp.zeros((half, 128), F32)
    for i in range(blocks + POLAR):
        own, n = (cells, i) if i < blocks else (polar_cells, i - blocks)
        x0[at(at.of(i)), :] = own[n * half : (n + 1) * half, :].astype(F32)
    stages = layers(at, groups, pairs, moved, *scratch, w1, w2, wd, wc, wu)

    y2, yu = scratch[3], scratch[6]
    lane = lax.broadcasted_iota(jnp.int32, (8, 2 * half), 1)
    even = lax.rem(lane, 2) == 0
    edge = (lane < 2 * HALO) | (lane >= 2 * half - 2 * HALO)

    def weave(values, i, p):
        spread = lax.div(lane, 2) + i * half
        evens = jnp.take_along_axis(values[p * 16 : p * 16 + 8], spread, axis=1)
        odds = jnp.take_along_axis(values[p * 16 + 8 : p * 16 + 16], spread, axis=1)
        return jnp.where(even, evens, odds)

    def last(row, count):
        def finish(found):
            found = project(found, wp)
            for n in range(count // 2):
                pair = (row - 1) // 2 + n
                own = found[:, n * 2 * half : (n + 1) * 2 * half]
                base = skip[pair * 32 : (pair + 1) * 32, :]
                for i in range(2):
                    for p in range(2):
                        line = (4 * pair + 2 * i + p) * 8
                        inner = jnp.where(edge, 0.0, weave(own, i, p))
                        update[line : line + 8, :] = inner + weave(base, i, p)

        return lambda: merge(at, row, count, y2, yu, wm), finish, [(row, count)]

    run(at, stages + [[last(*ranges[-1]) for ranges in groups]], AHEAD)


def edges_kernel(cells, polar_cells, inner, outer, w1, w2, wd, wc, wu, wm, wp, update, *refs):
    shared, out, scratch = refs[: len(SHARED_KEYS)], refs[len(SHARED_KEYS)], refs[len(SHARED_KEYS) + 1 :]
    even = lax.rem(lax.axis_index("lon"), 2) == 0
    half = out.shape[2] // 2
    blocks = out.shape[1] // 2
    step = 4 * HALO
    at = Rows(step, blocks)
    place = lax.broadcasted_iota(jnp.int32, (step, 128), 0)
    x0 = scratch[0]
    near, far = inner[...].astype(F32), outer[...].astype(F32)
    left, right = jnp.where(even, far, near), jnp.where(even, near, far)
    beside = {}
    for row in (at.top, at.bottom, at.pole, at.count - 1):
        x0[at(row), :] = jnp.zeros((step, 128), F32)
    for i in range(blocks + POLAR):
        row = at.of(i)
        own, n = (cells, i) if i < blocks else (polar_cells, i - blocks)
        begin = own[n * half : n * half + 16, :].astype(F32)
        finish = own[(n + 1) * half - 16 : (n + 1) * half, :].astype(F32)
        base = row * step
        x0[base : base + HALO, :] = left[i * HALO : (i + 1) * HALO]
        x0[base + HALO : base + 2 * HALO, :] = begin[:HALO]
        x0[base + 2 * HALO : base + 3 * HALO, :] = finish[16 - HALO :]
        x0[base + 3 * HALO : base + 4 * HALO, :] = right[i * HALO : (i + 1) * HALO]
        beside[row] = {-1: begin[HALO : HALO + 1], 1: finish[15 - HALO : 16 - HALO]}
    beside[at.top] = {way: pltpu.roll(line, 32, 1) for way, line in beside[at.pole + 1].items()}
    beside[at.pole] = {way: pltpu.roll(line, 32, 1) for way, line in beside[1].items()}

    def moved(name, row, count, values, shift):
        lines = []
        target = 2 * HALO if shift == 1 else 2 * HALO - 1
        for i in range(count):
            line = pltpu.roll(values[i * step : (i + 1) * step], shift % step, 0)
            if name == "x0":
                own = beside[row + i][shift] if row + i in beside else None
            else:
                ref = next(r for (key, _, way), r in zip(SHARED_KEYS, shared) if (key, way) == (name, shift))
                own = ref[row + i : row + i + 1, :]
            if own is not None:
                parts = []
                for lanes in range(0, values.shape[1], 128):
                    fix = jnp.broadcast_to(own[:, lanes : lanes + 128], (step, 128))
                    parts.append(jnp.where(place == target, fix, line[:, lanes : lanes + 128]))
                line = parts[0] if len(parts) == 1 else jnp.concatenate(parts, axis=1)
            lines.append(line)
        return lines[0] if count == 1 else jnp.concatenate(lines, axis=0)

    cut = EDGE_ROWS
    groups = [[(1, cut)], [(1 + cut, blocks - cut), (at.pole + 1, POLAR)]]
    pairs = [[(1, blocks), (at.pole + 1, POLAR)]]
    parts = []

    def last(row, count):
        def finish(found):
            parts.append(project(found, wp))

        return lambda: merge(at, row, count, scratch[3], scratch[6], wm), finish, [(row, count)]

    stages = layers(at, groups, pairs, moved, *scratch, w1, w2, wd, wc, wu)
    run(at, stages + [[last(1, blocks // 2), last(1 + blocks // 2, blocks // 2)]], 1)
    found = jnp.concatenate(parts, axis=1)

    columns = 2 * half
    lane = lax.broadcasted_iota(jnp.int32, (8, columns), 1)
    first = lane < 2 * HALO
    edge = first | (lane >= columns - 2 * HALO)
    column = jnp.where(first, HALO + lax.div(lane, 2), 3 * HALO - lax.div(columns + 1 - lane, 2))
    column = jnp.where(edge, column, 0)
    odd = lax.rem(lane, 2) == 1
    per = columns // step
    for i in range(blocks):
        spread = column + (i % per) * step
        lanes = slice(i // per * columns, (i // per + 1) * columns)
        for p in range(2):
            evens = jnp.take_along_axis(found[p * 16 : p * 16 + 8, lanes], spread, axis=1)
            odds = jnp.take_along_axis(found[p * 16 + 8 : p * 16 + 16, lanes], spread, axis=1)
            h = 2 * i + p
            line = slice(h * 8, (h + 1) * 8)
            out[:, h, :] = jnp.where(edge, jnp.where(odd, odds, evens), 0.0) + update[line, :]


def buffers(step, blocks):
    rows = Rows(step, blocks).count * step
    shapes = ((128, F32), (128, F32), (512, BF16), (512, BF16), (384, BF16), (256, BF16), (512, BF16))
    return [pltpu.VMEM((rows, lanes), dtype) for lanes, dtype in shapes]


def inside(cells, polar_cells, skip, weights):
    columns = skip.shape[1]
    blocks = skip.shape[0] // 16
    rows = Rows(columns // 2, blocks).count
    return pl.pallas_call(
        inside_kernel,
        out_shape=[jax.ShapeDtypeStruct((blocks * 16, columns), F32)]
        + [jax.ShapeDtypeStruct((rows, lanes), F32) for _, lanes, _ in SHARED_KEYS],
        scratch_shapes=buffers(columns // 2, blocks),
        compiler_params=pltpu.CompilerParams(vmem_limit_bytes=20 * 2**20),
        cost_estimate=pl.CostEstimate(flops=4 * 10**9, bytes_accessed=4 * 10**6, transcendentals=0),
        name="inside",
    )(cells, polar_cells, skip, *weights)


def edges(out_shape, cells, polar_cells, inner, outer, weights, found):
    return pl.pallas_call(
        edges_kernel,
        out_shape=jax.ShapeDtypeStruct(out_shape, F32),
        scratch_shapes=buffers(4 * HALO, out_shape[1] // 2),
        compiler_params=pltpu.CompilerParams(vmem_limit_bytes=20 * 2**20),
        name="edges",
    )(cells, polar_cells, inner, outer, *weights, *found)


def shards(
    latlon_fields,
    remap_table,
    kernel_first,
    kernel_second,
    kernel_down,
    kernel_coarse,
    kernel_up,
    kernel_merge,
    projection,
):
    _, grid_rows, columns = remap_table.shape
    count = lax.axis_size("lon")
    polar = opposite(remap_table[:, : 4 * ((POLAR + 1) // 2), :], "lon")
    parcels = pack(latlon_fields, count, columns)
    block = lax.all_to_all(parcels, "lon", split_axis=0, concat_axis=0, tiled=True)
    places, *weights = prepare(
        remap_table, kernel_first, kernel_second, kernel_down, kernel_coarse, kernel_up, kernel_merge, projection
    )
    cells, begin, finish, skip = remap_own(block, places)
    polar_cells, inner, outer = remap_polar(block, polar, begin, finish)
    outer = swap(outer, "lon", 1)
    inner = swap(inner, "lon", 0)
    found = inside(cells, polar_cells, skip, weights)
    return edges((projection.shape[0], grid_rows, columns), cells, polar_cells, inner, outer, weights, found)


def solution(mesh):
    return jax.shard_map(
        shards,
        mesh=mesh,
        in_specs=(
            P("groups", "lon", None),
            P(None, None, "lon"),
            P(),
            P(),
            P(),
            P(),
            P(),
            P(),
            P(),
        ),
        out_specs=P("groups", None, "lon"),
        check_vma=False,
    )
```

```python
import jax
import jax.numpy as jnp
from jax import lax
from jax.experimental import pallas as pl
from jax.experimental.pallas import tpu as pltpu
from jax.sharding import PartitionSpec as P

F32 = jnp.float32
BF16 = jnp.bfloat16
HALO = 4
EDGE_ROWS = 9
AHEAD = 2
PARTS = 4
POLAR = 3


def swap(block, axis, first):
    devices = lax.axis_size(axis)
    pairs = [((first + i) % devices, (first + i + 1) % devices) for i in range(0, devices, 2)]
    return lax.ppermute(block, axis, pairs + [(b, a) for a, b in pairs])


def opposite(block, axis):
    devices = lax.axis_size(axis)
    return lax.ppermute(block, axis, [(i, (i + devices // 2) % devices) for i in range(devices)])


def pack_kernel(fields_hbm, parcels, fields, load_sems, sems):
    devices, channels, _, columns = fields.shape
    span = devices // PARTS
    loads = []
    for target in range(devices):
        lanes = slice(target * columns, (target + 1) * columns)
        loads.append(pltpu.make_async_copy(fields_hbm.at[:, :, lanes], fields.at[target], load_sems.at[target]))
        loads[-1].start()
    copies = []
    for n in range(PARTS):
        for load in loads[n * span : (n + 1) * span]:
            load.wait()
        first, other = n * span, (n * span + devices // 2) % devices
        places = parcels.at[first : first + span, :channels], parcels.at[other : other + span, channels:]
        for place in places:
            copies.append(pltpu.make_async_copy(fields.at[first : first + span], place, sems.at[len(copies)]))
            copies[-1].start()
    for copy in copies:
        copy.wait()


def pack(fields, devices, columns):
    channels, rows, _ = fields.shape
    parcels = pl.pallas_call(
        pack_kernel,
        in_specs=[pl.BlockSpec(memory_space=pltpu.HBM)],
        out_specs=pl.BlockSpec(memory_space=pltpu.HBM),
        out_shape=pltpu.HBM((devices, 2 * channels, rows, columns), BF16),
        scratch_shapes=[
            pltpu.VMEM((devices, channels, rows, columns), BF16),
            pltpu.SemaphoreType.DMA((devices,)),
            pltpu.SemaphoreType.DMA((2 * PARTS,)),
        ],
        compiler_params=pltpu.CompilerParams(vmem_limit_bytes=16 * 2**20),
        name="pack",
    )(pltpu.with_memory_space_constraint(fields, pltpu.HBM))
    return parcels.reshape(devices, 2 * channels * rows, columns)


def tap(kernel_ref, row, col):
    if 0 <= row < 3 and 0 <= col < 3:
        return kernel_ref[row, col].astype(F32)
    return jnp.zeros(kernel_ref.shape[2:], F32)


def arrange(first, second, down, coarse, up, merge, projection, w1, w2, wd, wc, wu, wm, wp):
    channels = second.shape[3]
    inputs = first.shape[2]
    for half in range(2):
        for side in range(2):
            for p in range(2):
                for q in range(2):
                    t = 1 + p if half == 0 else (3, 0)[p]
                    u = 1 + q if side == 0 else (3, 0)[q]
                    at = (((half * 2 + side) * 2 + p) * 2 + q) * inputs
                    pieces = [tap(first, t - a, u - b) for a in range(2) for b in range(2)]
                    w1[at : at + inputs, :] = jnp.concatenate(pieces, axis=1).astype(BF16)
    for t in range(4):
        for code in range(4):
            at = (t * 4 + code) * channels
            source = (0, 1, -2, -1)[code]
            for p in range(2):
                pair = [tap(second, t - p, source - target + 1) for target in (-1, 0)]
                w2[at : at + channels, p * 128 : (p + 1) * 128] = jnp.concatenate(pair, axis=0).T.astype(BF16)
            source = code - 1
            for p in range(2):
                pair = [tap(merge, t - p, source - target + 1) for target in (0, 1)]
                pair = jnp.concatenate(pair, axis=0).T.astype(BF16)
                wm[at : at + channels, p * 128 : (p + 1) * 128] = pair[:channels]
                wm[16 * channels + at : 16 * channels + at + channels, p * 128 : (p + 1) * 128] = pair[channels:]
            if t < 3:
                wd[at : at + channels, :] = tap(down, t, code).astype(BF16)
    wide = coarse.shape[3]
    for a in range(3):
        for b in range(3):
            at = (a * 3 + b) * wide
            wc[at : at + wide, :] = tap(coarse, a, b).T.astype(BF16)
    row_taps = ((1, 3), (0, 2))
    col_taps = ((0, 2), (3, 1))
    for di in range(2):
        for dj in range(2):
            at = (di * 2 + dj) * wide
            for p in range(2):
                pair = jnp.concatenate([tap(up, row_taps[p][di], col_taps[q][dj]) for q in range(2)], axis=0)
                wu[at : at + wide, p * 128 : (p + 1) * 128] = pair.T.astype(BF16)
    rows = projection[...].astype(F32)
    blank = jnp.zeros_like(rows)
    lines = [jnp.concatenate([rows if m == n else blank for m in range(4)], axis=1) for n in range(4)]
    wp[...] = jnp.concatenate(lines, axis=0).astype(BF16)


def locate(rows, cols):
    grid_rows, columns = rows.shape
    half = columns // 2
    code = rows * columns + cols
    lane = lax.broadcasted_iota(jnp.int32, (grid_rows, columns), 1)
    odd = [jnp.take_along_axis(code, lax.rem(lane, half) * 2 + q, axis=1) for q in range(2)]
    left = lax.broadcasted_iota(jnp.int32, (1, columns), 1) < half
    lines = []
    for pair in range(grid_rows // 4):
        for p in range(2):
            for q in range(2):
                above, below = 4 * pair + p, 4 * pair + 2 + p
                lines.append(jnp.where(left, odd[q][above : above + 1, :], odd[q][below : below + 1, :]))
    return jnp.concatenate(lines, axis=0)


def prepare_kernel(*refs):
    args, (places, *weights), scratch, sems = refs[:8], refs[8:16], refs[16:24], refs[24]
    copies = [
        pltpu.make_async_copy(source, target, sems.at[n]) for n, (source, target) in enumerate(zip(args, scratch))
    ]
    for copy in copies:
        copy.start()
    copies[0].wait()
    table = scratch[0]
    places[...] = locate(table[0], lax.rem(table[1], table.shape[2]))
    for copy in copies[1:]:
        copy.wait()
    arrange(*scratch[1:], *weights)


def prepare(table, first, second, down, coarse, up, merge, projection):
    channels, wide = second.shape[3], coarse.shape[3]
    columns = table.shape[2]
    shapes = (
        (16 * first.shape[3], 4 * channels),
        (16 * channels, 4 * channels),
        (12 * channels, wide),
        (9 * wide, wide),
        (4 * wide, 4 * channels),
        (32 * channels, 4 * channels),
        (4 * projection.shape[0], 4 * channels),
    )
    args = (table, jnp.swapaxes(first, 2, 3), second, jnp.swapaxes(down, 2, 3), coarse, up, merge, projection)
    return pl.pallas_call(
        prepare_kernel,
        in_specs=[pl.BlockSpec(memory_space=pltpu.HBM)] * 8,
        out_shape=[jax.ShapeDtypeStruct(table.shape[1:], jnp.int32)] + [jax.ShapeDtypeStruct(s, BF16) for s in shapes],
        scratch_shapes=[pltpu.VMEM(a.shape, a.dtype) for a in args] + [pltpu.SemaphoreType.DMA((8,))],
        compiler_params=pltpu.CompilerParams(vmem_limit_bytes=16 * 2**20),
        name="prepare",
    )(*[pltpu.with_memory_space_constraint(a, pltpu.HBM) for a in args])


def collect(block, side, places, wide):
    devices, depth, columns = block.shape
    depth = depth // 2
    channels = depth // 2
    wide[...] = block[:, side * depth : (side + 1) * depth, :].astype(F32).reshape(wide.shape)
    parts = []
    for row in range(2):
        lines = [wide[pl.ds(s * depth + row, channels, stride=2), :] for s in range(devices)]
        parts.append(jnp.concatenate(lines, axis=0).astype(BF16))
    fields = jnp.concatenate(parts, axis=1)
    sources = lax.div(places, 2 * columns)
    offsets = lax.rem(places, 2 * columns).astype(F32)
    line_at = lax.broadcasted_iota(jnp.int32, (2 * columns, columns), 0).astype(F32)
    for pair in range(places.shape[0] // 4):
        chosen = []
        for n in range(4):
            here = line_at == jnp.broadcast_to(offsets[4 * pair + n : 4 * pair + n + 1, :], line_at.shape)
            chosen.append(jnp.where(here, 1.0, 0.0).astype(BF16))
        found = jnp.dot(fields, jnp.concatenate(chosen, axis=1), preferred_element_type=F32)
        lines = []
        for n in range(4):
            line = jnp.broadcast_to(sources[4 * pair + n : 4 * pair + n + 1, :], (channels, columns))
            total = jnp.zeros((channels, columns), F32)
            for s in range(devices):
                value = found[s * channels : (s + 1) * channels, n * columns : (n + 1) * columns]
                total = jnp.where(line == s, value, total)
            lines.append(total)
        yield pair, lines


def cells_of(lines, pair, cells):
    turned = jnp.concatenate(lines + lines, axis=0).T
    columns = turned.shape[0]
    half = columns // 2
    cells[pair * columns : (pair + 1) * columns, :] = turned.astype(BF16)
    begin = [turned[i * half : i * half + HALO] for i in range(2)]
    finish = [turned[(i + 1) * half - HALO : (i + 1) * half] for i in range(2)]
    return jnp.concatenate(begin, axis=0), jnp.concatenate(finish, axis=0)


def own_kernel(block, places, cells, begin, finish, skip, wide):
    for pair, lines in collect(block, 0, places[...], wide):
        for n in range(4):
            skip[(pair * 4 + n) * 8 : (pair * 4 + n + 1) * 8, :] = lines[n][:8]
        rows = slice(pair * 2 * HALO, (pair + 1) * 2 * HALO)
        begin[rows, :], finish[rows, :] = cells_of(lines, pair, cells)


def remap_own(block, places):
    devices, depth, columns = block.shape
    grid_rows = places.shape[0]
    count = grid_rows // 4
    return pl.pallas_call(
        own_kernel,
        out_shape=[
            jax.ShapeDtypeStruct((count * columns, columns), BF16),
            jax.ShapeDtypeStruct((count * 2 * HALO, columns), F32),
            jax.ShapeDtypeStruct((count * 2 * HALO, columns), F32),
            jax.ShapeDtypeStruct((grid_rows * 8, columns), F32),
        ],
        scratch_shapes=[pltpu.VMEM((devices * depth // 2, columns), F32)],
        compiler_params=pltpu.CompilerParams(vmem_limit_bytes=16 * 2**20),
        name="remap_own",
    )(block, places)


def polar_kernel(block, polar, begin, finish, cells, inner, outer, wide):
    columns = block.shape[2]
    places = locate(polar[0], lax.rem(polar[1], columns))
    begins, finishes = [begin[...]], [finish[...]]
    for pair, lines in collect(block, 1, places, wide):
        first, last = cells_of(lines, pair, cells)
        begins.append(first)
        finishes.append(last)
    even = lax.rem(lax.axis_index("lon"), 2) == 0
    begins, finishes = jnp.concatenate(begins, axis=0), jnp.concatenate(finishes, axis=0)
    inner[...] = jnp.where(even, finishes, begins)
    outer[...] = jnp.where(even, begins, finishes).astype(BF16)


def remap_polar(block, polar, begin, finish):
    devices, depth, columns = block.shape
    count = polar.shape[1] // 4
    rows = begin.shape[0] + count * 2 * HALO
    return pl.pallas_call(
        polar_kernel,
        out_shape=[
            jax.ShapeDtypeStruct((count * columns, columns), BF16),
            jax.ShapeDtypeStruct((rows, columns), F32),
            jax.ShapeDtypeStruct((rows, columns), BF16),
        ],
        scratch_shapes=[pltpu.VMEM((devices * depth // 2, columns), F32)],
        compiler_params=pltpu.CompilerParams(vmem_limit_bytes=16 * 2**20),
        name="remap_polar",
    )(block, polar, begin, finish)


def silu(values):
    h = 0.5 * values
    return (h + h * jnp.tanh(h)).astype(BF16).astype(F32)


def ring(values, step, shift):
    rows = [pltpu.roll(values[at : at + step], shift % step, 0) for at in range(0, values.shape[0], step)]
    return rows[0] if len(rows) == 1 else jnp.concatenate(rows, axis=0)


class Rows:
    def __init__(self, step, blocks):
        self.step, self.blocks = step, blocks
        self.top, self.bottom, self.pole = 0, blocks + 1, blocks + 2
        self.count = blocks + 2 + POLAR + 2

    def __call__(self, row, count=1):
        return slice(row * self.step, (row + count) * self.step)

    def of(self, i):
        return 1 + i if i < self.blocks else self.pole + 1 + i - self.blocks

    def mask(self, count, width):
        lane = lax.broadcasted_iota(jnp.int32, (count * self.step, 128), 1)
        return lax.rem(lax.div(lane, width), 2) == 0


def product(pieces, weights):
    values = pieces[0] if len(pieces) == 1 else jnp.concatenate(pieces, axis=0)
    return jnp.dot(values, weights[...], preferred_element_type=F32)


def layers(at, groups, pairs, moved, cells_of_row, y0, y1, y2, yc, yo, yu, w1, w2, wd, wc, wu):
    step, top, bottom, pole = at.step, at.top, at.bottom, at.pole
    ready = set()

    def widen(row):
        if row not in ready:
            ready.add(row)
            if row == top:
                x = pltpu.roll(cells_of_row(pole + 1), 32, 1)
            elif row == pole:
                x = pltpu.roll(cells_of_row(1), 32, 1)
            elif row == bottom or row == at.count - 1:
                x = jnp.zeros((step, 128), F32)
            else:
                x = cells_of_row(row)
            side = jnp.where(at.mask(1, 16), moved("x0", row, 1, x, -1), moved("x0", row, 1, x, 1))
            y0[at(row), :] = jnp.where(at.mask(1, 64), x, side)

    for y, polar_rows in ((y1, POLAR), (y2, POLAR - 1), (yc, POLAR - 1), (yo, POLAR - 2), (yu, POLAR - 2)):
        for row in (bottom, pole + 1 + polar_rows):
            y[at(row), :] = jnp.zeros((step, y.shape[1]), BF16)

    def layer(name, polar_rows, inputs, weights, store, edge, paired=False):
        def task(ranges):
            ranges = [(row, polar_rows if row == pole + 1 else count) for row, count in ranges]

            def begin():
                pieces = [jnp.concatenate(inputs(row, count), axis=1) for row, count in ranges]
                return product(pieces, weights)

            def finish(found):
                found = silu(found)
                start = 0
                for row, count in ranges:
                    if paired:
                        lanes = found.shape[1] // 2
                        rows = []
                        for n in range(count):
                            line = slice(start + n // 2 * step, start + (n // 2 + 1) * step)
                            rows.append(found[line, n % 2 * lanes : (n % 2 + 1) * lanes])
                        values = rows[0] if count == 1 else jnp.concatenate(rows, axis=0)
                        start += (count + 1) // 2 * step
                    else:
                        values = found[start : start + count * step]
                        start += count * step
                    store(name, row, count, values)
                    if row == pole + 1:
                        edge(top, pole + 1)
                    if row == 1:
                        edge(pole, 1)

            return begin, finish, ranges

        return [task(ranges) for ranges in (pairs if paired else groups)]

    def fine(y, shift):
        def store(name, row, count, values):
            shifted = moved(name, row, count, values, shift).astype(BF16)
            values = values.astype(BF16)
            for p in range(2):
                lanes = slice(p * 128, (p + 1) * 128)
                y[at(row, count), p * 256 : p * 256 + 128] = values[:, lanes]
                y[at(row, count), p * 256 + 128 : p * 256 + 256] = shifted[:, lanes]

        def edge(target, source):
            y[at(target), 256:512] = y[at(source), 0:256]

        return store, edge

    def first_inputs(row, count):
        for n in range(row - 1, row + count + 1):
            widen(n)
        vertical = jnp.where(at.mask(count, 32), y0[at(row + 1, count), :], y0[at(row - 1, count), :])
        return [y0[at(row, count), :].astype(BF16), vertical.astype(BF16)]

    def second_inputs(row, count):
        return [y1[at(row - 1, count), 256:512], y1[at(row, count), :], y1[at(row + 1, count), 0:256]]

    def down_inputs(row, count):
        return [y2[at(row - 1, count), 256:512], y2[at(row, count), :]]

    def coarse_inputs(row, count):
        return [yc[at(row + a, count), :] for a in (-1, 0, 1)]

    def up_inputs(row, count):
        return [yo[at(row, count), :], yo[at(row + 1, count), :]]

    def store_coarse_in(name, row, count, values):
        yc[at(row, count), 0:128] = moved(name, row, count, values, 1).astype(BF16)
        yc[at(row, count), 128:256] = values.astype(BF16)
        yc[at(row, count), 256:384] = moved(name, row, count, values, -1).astype(BF16)

    def edge_coarse_in(target, source):
        yc[at(target), :] = yc[at(source), :]

    def store_coarse_out(name, row, count, values):
        yo[at(row, count), 0:128] = moved(name, row, count, values, 1).astype(BF16)
        yo[at(row, count), 128:256] = values.astype(BF16)

    return [
        layer("y1", POLAR, first_inputs, w1, *fine(y1, 1)),
        layer("y2", POLAR - 1, second_inputs, w2, *fine(y2, -1)),
        layer("yc", POLAR - 1, down_inputs, wd, store_coarse_in, edge_coarse_in),
        layer("yo", POLAR - 2, coarse_inputs, wc, store_coarse_out, lambda target, source: None),
        layer("yu", POLAR - 2, up_inputs, wu, *fine(yu, -1)),
    ]


def run(at, stages, ahead):
    tasks, owner = [], {}
    for stage in stages:
        rows = {}
        for begin, finish, ranges in stage:
            reads = set()
            for row, count in ranges:
                reads.update(range(row - 1, row + count + 2))
            reads.update({at.pole + 1} if at.top in reads else (), {1} if at.pole in reads else ())
            tasks.append((begin, finish, {owner[row] for row in reads if row in owner}))
            for row, count in ranges:
                rows.update({n: len(tasks) - 1 for n in range(row, row + count)})
        owner = rows
    found, issued = {}, 0
    for turn in range(len(tasks)):
        while issued < len(tasks) and issued <= turn + ahead and all(n < turn for n in tasks[issued][2]):
            found[issued] = tasks[issued][0]()
            issued += 1
        tasks[turn][1](found.pop(turn))


def merge(at, row, count, y2, yu, wm):
    pieces = []
    for y in (y2, yu):
        pieces += [y[at(row - 1, count), 256:512], y[at(row, count), :], y[at(row + 1, count), 0:256]]
    return product([jnp.concatenate(pieces, axis=1)], wm)


def project(found, wp):
    merged = silu(found).astype(BF16)
    return lax.dot_general(wp[...], merged, (((1,), (1,)), ((), ())), preferred_element_type=F32)


SHARED = (("y1", 256, (1,)), ("y2", 256, (-1,)), ("yc", 128, (1, -1)), ("yo", 128, (1,)), ("yu", 256, (-1,)))
SHARED_KEYS = [(name, lanes, shift) for name, lanes, shifts in SHARED for shift in shifts]


def inside_kernel(cells, polar_cells, skip, w1, w2, wd, wc, wu, wm, wp, update, *refs):
    shared, scratch = refs[: len(SHARED_KEYS)], refs[len(SHARED_KEYS) :]
    half = update.shape[1] // 2
    blocks = update.shape[0] // 16
    at = Rows(half, blocks)
    group = 4

    groups = [[(1 + i, group)] for i in range(0, blocks, group)]
    pairs = [[(1 + i, 2 * group)] for i in range(0, blocks, 2 * group)]
    for first in (groups[0], pairs[0]):
        first.insert(0, (at.pole + 1, POLAR))

    def moved(name, row, count, values, shift):
        for (key, _, way), ref in zip(SHARED_KEYS, shared):
            if key == name and way == shift:
                column = half - HALO - 1 if shift == 1 else HALO
                for i in range(count):
                    ref[row + i : row + i + 1, :] = values[i * half + column : i * half + column + 1, :]
        return ring(values, half, shift)

    def cells_of_row(row):
        own, n = (cells, row - 1) if row <= blocks else (polar_cells, row - at.pole - 1)
        return own[n * half : (n + 1) * half, :].astype(F32)

    stages = layers(at, groups, pairs, moved, cells_of_row, *scratch[1:], w1, w2, wd, wc, wu)

    y2, yu = scratch[3], scratch[6]
    lane = lax.broadcasted_iota(jnp.int32, (8, 2 * half), 1)
    even = lax.rem(lane, 2) == 0
    edge = (lane < 2 * HALO) | (lane >= 2 * half - 2 * HALO)

    def weave(values, i, p):
        spread = lax.div(lane, 2) + i * half
        evens = jnp.take_along_axis(values[p * 16 : p * 16 + 8], spread, axis=1)
        odds = jnp.take_along_axis(values[p * 16 + 8 : p * 16 + 16], spread, axis=1)
        return jnp.where(even, evens, odds)

    def last(row, count):
        def finish(found):
            found = project(found, wp)
            for n in range(count // 2):
                pair = (row - 1) // 2 + n
                own = found[:, n * 2 * half : (n + 1) * 2 * half]
                base = skip[pair * 32 : (pair + 1) * 32, :]
                for i in range(2):
                    for p in range(2):
                        line = (4 * pair + 2 * i + p) * 8
                        inner = jnp.where(edge, 0.0, weave(own, i, p))
                        update[line : line + 8, :] = inner + weave(base, i, p)

        return lambda: merge(at, row, count, y2, yu, wm), finish, [(row, count)]

    run(at, stages + [[last(*ranges[-1]) for ranges in groups]], AHEAD)


def edges_kernel(cells, polar_cells, inner, outer, w1, w2, wd, wc, wu, wm, wp, update, *refs):
    shared, out, scratch = refs[: len(SHARED_KEYS)], refs[len(SHARED_KEYS)], refs[len(SHARED_KEYS) + 1 :]
    even = lax.rem(lax.axis_index("lon"), 2) == 0
    half = out.shape[2] // 2
    blocks = out.shape[1] // 2
    step = 4 * HALO
    at = Rows(step, blocks)
    place = lax.broadcasted_iota(jnp.int32, (step, 128), 0)
    x0 = scratch[0]
    near, far = inner[...], outer[...].astype(F32)
    left, right = jnp.where(even, far, near), jnp.where(even, near, far)
    beside = {}
    for i in range(blocks + POLAR):
        row = at.of(i)
        own, n = (cells, i) if i < blocks else (polar_cells, i - blocks)
        begin = own[n * half : n * half + 16, :].astype(F32)
        finish = own[(n + 1) * half - 16 : (n + 1) * half, :].astype(F32)
        base = row * step
        x0[base : base + HALO, :] = left[i * HALO : (i + 1) * HALO]
        x0[base + HALO : base + 2 * HALO, :] = begin[:HALO]
        x0[base + 2 * HALO : base + 3 * HALO, :] = finish[16 - HALO :]
        x0[base + 3 * HALO : base + 4 * HALO, :] = right[i * HALO : (i + 1) * HALO]
        beside[row] = {-1: begin[HALO : HALO + 1], 1: finish[15 - HALO : 16 - HALO]}
    beside[at.top] = {way: pltpu.roll(line, 32, 1) for way, line in beside[at.pole + 1].items()}
    beside[at.pole] = {way: pltpu.roll(line, 32, 1) for way, line in beside[1].items()}

    def moved(name, row, count, values, shift):
        lines = []
        target = 2 * HALO if shift == 1 else 2 * HALO - 1
        for i in range(count):
            line = pltpu.roll(values[i * step : (i + 1) * step], shift % step, 0)
            if name == "x0":
                own = beside[row + i][shift] if row + i in beside else None
            else:
                ref = next(r for (key, _, way), r in zip(SHARED_KEYS, shared) if (key, way) == (name, shift))
                own = ref[row + i : row + i + 1, :]
            if own is not None:
                parts = []
                for lanes in range(0, values.shape[1], 128):
                    fix = jnp.broadcast_to(own[:, lanes : lanes + 128], (step, 128))
                    parts.append(jnp.where(place == target, fix, line[:, lanes : lanes + 128]))
                line = parts[0] if len(parts) == 1 else jnp.concatenate(parts, axis=1)
            lines.append(line)
        return lines[0] if count == 1 else jnp.concatenate(lines, axis=0)

    cut = EDGE_ROWS
    groups = [[(1, cut)], [(1 + cut, blocks - cut), (at.pole + 1, POLAR)]]
    pairs = [[(1, blocks), (at.pole + 1, POLAR)]]
    parts = []

    def last(row, count):
        def finish(found):
            parts.append(project(found, wp))

        return lambda: merge(at, row, count, scratch[3], scratch[6], wm), finish, [(row, count)]

    stages = layers(at, groups, pairs, moved, lambda row: x0[at(row), :], *scratch[1:], w1, w2, wd, wc, wu)
    run(at, stages + [[last(1, blocks // 2), last(1 + blocks // 2, blocks // 2)]], 1)
    found = jnp.concatenate(parts, axis=1)

    columns = 2 * half
    lane = lax.broadcasted_iota(jnp.int32, (8, columns), 1)
    first = lane < 2 * HALO
    edge = first | (lane >= columns - 2 * HALO)
    column = jnp.where(first, HALO + lax.div(lane, 2), 3 * HALO - lax.div(columns + 1 - lane, 2))
    column = jnp.where(edge, column, 0)
    odd = lax.rem(lane, 2) == 1
    per = columns // step
    for i in range(blocks):
        spread = column + (i % per) * step
        lanes = slice(i // per * columns, (i // per + 1) * columns)
        for p in range(2):
            evens = jnp.take_along_axis(found[p * 16 : p * 16 + 8, lanes], spread, axis=1)
            odds = jnp.take_along_axis(found[p * 16 + 8 : p * 16 + 16, lanes], spread, axis=1)
            h = 2 * i + p
            line = slice(h * 8, (h + 1) * 8)
            out[:, h, :] = jnp.where(edge, jnp.where(odd, odds, evens), 0.0) + update[line, :]


def buffers(step, blocks):
    rows = Rows(step, blocks).count * step
    shapes = ((128, F32), (128, F32), (512, BF16), (512, BF16), (384, BF16), (256, BF16), (512, BF16))
    return [pltpu.VMEM((rows, lanes), dtype) for lanes, dtype in shapes]


def inside(cells, polar_cells, skip, weights):
    columns = skip.shape[1]
    blocks = skip.shape[0] // 16
    rows = Rows(columns // 2, blocks).count
    return pl.pallas_call(
        inside_kernel,
        out_shape=[jax.ShapeDtypeStruct((blocks * 16, columns), F32)]
        + [jax.ShapeDtypeStruct((rows, lanes), F32) for _, lanes, _ in SHARED_KEYS],
        scratch_shapes=buffers(columns // 2, blocks),
        compiler_params=pltpu.CompilerParams(vmem_limit_bytes=20 * 2**20),
        cost_estimate=pl.CostEstimate(flops=4 * 10**9, bytes_accessed=4 * 10**6, transcendentals=0),
        name="inside",
    )(cells, polar_cells, skip, *weights)


def edges(out_shape, cells, polar_cells, inner, outer, weights, found):
    return pl.pallas_call(
        edges_kernel,
        out_shape=jax.ShapeDtypeStruct(out_shape, F32),
        scratch_shapes=buffers(4 * HALO, out_shape[1] // 2),
        compiler_params=pltpu.CompilerParams(vmem_limit_bytes=20 * 2**20),
        name="edges",
    )(cells, polar_cells, inner, outer, *weights, *found)


def shards(
    latlon_fields,
    remap_table,
    kernel_first,
    kernel_second,
    kernel_down,
    kernel_coarse,
    kernel_up,
    kernel_merge,
    projection,
):
    _, grid_rows, columns = remap_table.shape
    count = lax.axis_size("lon")
    polar = opposite(remap_table[:, : 4 * ((POLAR + 1) // 2), :], "lon")
    parcels = pack(latlon_fields, count, columns)
    block = lax.all_to_all(parcels, "lon", split_axis=0, concat_axis=0, tiled=True)
    places, *weights = prepare(
        remap_table, kernel_first, kernel_second, kernel_down, kernel_coarse, kernel_up, kernel_merge, projection
    )
    cells, begin, finish, skip = remap_own(block, places)
    polar_cells, inner, outer = remap_polar(block, polar, begin, finish)
    outer = swap(outer, "lon", 1)
    inner = swap(inner, "lon", 0)
    found = inside(cells, polar_cells, skip, weights)
    return edges((projection.shape[0], grid_rows, columns), cells, polar_cells, inner, outer, weights, found)


def solution(mesh):
    return jax.shard_map(
        shards,
        mesh=mesh,
        in_specs=(
            P("groups", "lon", None),
            P(None, None, "lon"),
            P(),
            P(),
            P(),
            P(),
            P(),
            P(),
            P(),
        ),
        out_specs=P("groups", None, "lon"),
        check_vma=False,
    )
```
